32 devices in a mesh: dp: 2 (over core), hid: 4 (over y, x), wid: 4 (over z).
Axes of the slice: x: 2, y: 2, z: 4, core: 2. Of those that a mesh axis runs over, the one named last changes fastest.
Arguments:
- inputs: float32 [12544, 768], P(('dp', 'hid', 'wid')), may hold values from -6 to 6
- grid_sizes: int32 [64], P('dp'), may hold values from 7 to 12
- cotangent: float32 [12544, 768], P(('dp', 'hid', 'wid')), may hold values from -6 to 6
- window_convkernel: float32 [9, 768], replicated, may hold values from -2 to 2
- window_convbias: float32 [768], replicated, may hold values from -2 to 2
- window_gainone: float32 [768], replicated, may hold values from 0.5 to 1.5
- window_shiftone: float32 [768], replicated, may hold values from -2 to 2
- window_inweights: bfloat16 [3, 768, 768], P(None, ('hid', 'wid')), may hold values from -0.21875 to 0.21875
- window_inbias: float32 [2, 768], P(None, 'hid'), may hold values from -3 to 3
- window_outweights: bfloat16 [768, 768], P(('hid', 'wid')), may hold values from -0.4375 to 0.4375
- window_outbias: float32 [768], replicated, may hold values from -2 to 2
- window_gaintwo: float32 [768], replicated, may hold values from 0.5 to 1.5
- window_shifttwo: float32 [768], replicated, may hold values from -2 to 2
- window_upweights: bfloat16 [3072, 768], P(('hid', 'wid')), may hold values from -0.21875 to 0.21875
- window_upbias: float32 [3072], P('hid'), may hold values from -3 to 3
- window_downweights: bfloat16 [3072, 768], P(('hid', 'wid')), may hold values from -0.15625 to 0.15625
- window_downbias: float32 [768], replicated, may hold values from -2 to 2
- channel_convkernel: float32 [9, 768], replicated, may hold values from -2 to 2
- channel_convbias: float32 [768], replicated, may hold values from -2 to 2
- channel_gainone: float32 [768], replicated, may hold values from 0.5 to 1.5
- channel_shiftone: float32 [768], replicated, may hold values from -2 to 2
- channel_inweights: bfloat16 [3, 768, 768], P(None, ('hid', 'wid')), may hold values from -0.21875 to 0.21875
- channel_inbias: float32 [3, 768], P(None, 'hid'), may hold values from -3 to 3
- channel_outweights: bfloat16 [768, 768], P(('hid', 'wid')), may hold values from -0.4375 to 0.4375
- channel_outbias: float32 [768], replicated, may hold values from -2 to 2
- channel_gaintwo: float32 [768], replicated, may hold values from 0.5 to 1.5
- channel_shifttwo: float32 [768], replicated, may hold values from -2 to 2
- channel_upweights: bfloat16 [3072, 768], P(('hid', 'wid')), may hold values from -0.21875 to 0.21875
- channel_upbias: float32 [3072], P('hid'), may hold values from -3 to 3
- channel_downweights: bfloat16 [3072, 768], P(('hid', 'wid')), may hold values from -0.15625 to 0.15625
- channel_downbias: float32 [768], replicated, may hold values from -2 to 2
Outputs:
- outputs: float32 [12544, 768], P(('dp', 'hid', 'wid'))
- input_grad: float32 [12544, 768], P(('dp', 'hid', 'wid'))
- window_convkernel_grad: float32 [9, 768], replicated
- window_convbias_grad: float32 [768], replicated
- window_gainone_grad: float32 [768], replicated
- window_shiftone_grad: float32 [768], replicated
- window_inweights_grad: float32 [3, 768, 768], P(None, ('hid', 'wid'))
- window_inbias_grad: float32 [2, 768], P(None, 'hid')
- window_outweights_grad: float32 [768, 768], P(('hid', 'wid'))
- window_outbias_grad: float32 [768], replicated
- window_gaintwo_grad: float32 [768], replicated
- window_shifttwo_grad: float32 [768], replicated
- window_upweights_grad: float32 [3072, 768], P(('hid', 'wid'))
- window_upbias_grad: float32 [3072], P('hid')
- window_downweights_grad: float32 [3072, 768], P(('hid', 'wid'))
- window_downbias_grad: float32 [768], replicated
- channel_convkernel_grad: float32 [9, 768], replicated
- channel_convbias_grad: float32 [768], replicated
- channel_gainone_grad: float32 [768], replicated
- channel_shiftone_grad: float32 [768], replicated
- channel_inweights_grad: float32 [3, 768, 768], P(None, ('hid', 'wid'))
- channel_inbias_grad: float32 [3, 768], P(None, 'hid')
- channel_outweights_grad: float32 [768, 768], P(('hid', 'wid'))
- channel_outbias_grad: float32 [768], replicated
- channel_gaintwo_grad: float32 [768], replicated
- channel_shifttwo_grad: float32 [768], replicated
- channel_upweights_grad: float32 [3072, 768], P(('hid', 'wid'))
- channel_upbias_grad: float32 [3072], P('hid')
- channel_downweights_grad: float32 [3072, 768], P(('hid', 'wid'))
- channel_downbias_grad: float32 [768], replicated
The draws below stay inside these ranges and needn't reach their ends.
Inputs may be any that keep to these rules, and one draw needn't show every extreme that they name: `grid_sizes`: section-four grid side of images of 224 to 384 pixels; the slot is 14 x 14.
All inputs are finite; a program needn't handle non-finite values.
Results may differ from the reference program's by a relative error of at most 0.03.
Values may be sent and summed in bfloat16 or wider, within the bound.
No kernel may reach another device: no remote copies, remote signals or barrier semaphores. Data moves between devices by JAX's collectives and lax.ppermute only.
A program may use at most 192 MiB of HBM per device.

```python
import jax
import jax.numpy as jnp
from jax import lax

D = 768
HD = 32
FF = 3072
WINDOW = 7
PADDED = 14
IMAGES = 64
TOKENS = 12544


def plant(drawn, key, low, largest):
    place = [jax.random.randint(jax.random.fold_in(key, axis), (), 0, length) for axis, length in enumerate(drawn.shape)]
    main_axis = drawn.shape.index(max(drawn.shape))
    next_to = place[:main_axis] + [(place[main_axis] + 1) % drawn.shape[main_axis]] + place[main_axis + 1:]
    return drawn.at[tuple(place)].set(low).at[tuple(next_to)].set(largest)


def shard_levels(own_key, extent, cuts, smallest, largest):
    level = 1.0
    for axis_at, parts in cuts:
        draws = jax.random.uniform(jax.random.fold_in(jax.random.fold_in(own_key, 6), axis_at), (parts,), jnp.float32, smallest / len(cuts), largest / len(cuts))
        level = level * jnp.repeat(jnp.exp(draws), extent[axis_at] // parts).reshape((-1,) + (1,) * (len(extent) - 1 - axis_at))
    return level


def scatter_about(own_key, shape, scale, bound, cuts=(), kind=jnp.bfloat16):
    level = shard_levels(own_key, shape, cuts, -0.22, 0.18) if cuts else 1.0
    entries = jax.random.normal(own_key, shape, jnp.float32) * scale * level
    return jnp.minimum(jnp.maximum(entries, -bound), bound).astype(kind)


def setup_inputs(seed: int = 0) -> dict:
    seeds = jax.random.split(jax.random.key(seed), 32)
    return {
        "inputs": scatter_about(seeds[0], (TOKENS, D), 1.0, 6.0, ((0, 32),), jnp.float32),
        "grid_sizes": plant(jax.random.randint(seeds[1], (IMAGES,), 7, 13), jax.random.fold_in(seeds[1], 1), 7, 12).astype(jnp.int32),
        "cotangent": scatter_about(seeds[2], (TOKENS, D), 1.0, 6.0, ((0, 32),), jnp.float32),
        "window_convkernel": scatter_about(seeds[3], (9, D), 9 ** -0.5, 2.0, (), jnp.float32),
        "window_convbias": scatter_about(seeds[4], (D,), 0.3, 2.0, (), jnp.float32),
        "window_gainone": jnp.clip(1.0 + 0.1 * jax.random.normal(seeds[5], (D,), jnp.float32), 0.5, 1.5),
        "window_shiftone": scatter_about(seeds[6], (D,), 0.3, 2.0, (), jnp.float32),
        "window_inweights": scatter_about(seeds[7], (3, D, D), D ** -0.5, 0.21875, ((1, 16),)),
        "window_inbias": scatter_about(seeds[8], (2, D), 0.5, 3.0, ((1, 4),), jnp.float32),
        "window_outweights": scatter_about(seeds[9], (D, D), (D // 4) ** -0.5, 0.4375, ((0, 16),)),
        "window_outbias": scatter_about(seeds[10], (D,), 0.3, 2.0, (), jnp.float32),
        "window_gaintwo": jnp.clip(1.0 + 0.1 * jax.random.normal(seeds[11], (D,), jnp.float32), 0.5, 1.5),
        "window_shifttwo": scatter_about(seeds[12], (D,), 0.3, 2.0, (), jnp.float32),
        "window_upweights": scatter_about(seeds[13], (FF, D), D ** -0.5, 0.21875, ((0, 16),)),
        "window_upbias": scatter_about(seeds[14], (FF,), 0.5, 3.0, ((0, 4),), jnp.float32),
        "window_downweights": scatter_about(seeds[15], (FF, D), (FF // 2) ** -0.5, 0.15625, ((0, 16),)),
        "window_downbias": scatter_about(seeds[16], (D,), 0.3, 2.0, (), jnp.float32),
        "channel_convkernel": scatter_about(seeds[17], (9, D), 9 ** -0.5, 2.0, (), jnp.float32),
        "channel_convbias": scatter_about(seeds[18], (D,), 0.3, 2.0, (), jnp.float32),
        "channel_gainone": jnp.clip(1.0 + 0.1 * jax.random.normal(seeds[19], (D,), jnp.float32), 0.5, 1.5),
        "channel_shiftone": scatter_about(seeds[20], (D,), 0.3, 2.0, (), jnp.float32),
        "channel_inweights": scatter_about(seeds[21], (3, D, D), D ** -0.5, 0.21875, ((1, 16),)),
        "channel_inbias": scatter_about(seeds[22], (3, D), 0.5, 3.0, ((1, 4),), jnp.float32),
        "channel_outweights": scatter_about(seeds[23], (D, D), (D // 4) ** -0.5, 0.4375, ((0, 16),)),
        "channel_outbias": scatter_about(seeds[24], (D,), 0.3, 2.0, (), jnp.float32),
        "channel_gaintwo": jnp.clip(1.0 + 0.1 * jax.random.normal(seeds[25], (D,), jnp.float32), 0.5, 1.5),
        "channel_shifttwo": scatter_about(seeds[26], (D,), 0.3, 2.0, (), jnp.float32),
        "channel_upweights": scatter_about(seeds[27], (FF, D), D ** -0.5, 0.21875, ((0, 16),)),
        "channel_upbias": scatter_about(seeds[28], (FF,), 0.5, 3.0, ((0, 4),), jnp.float32),
        "channel_downweights": scatter_about(seeds[29], (FF, D), (FF // 2) ** -0.5, 0.15625, ((0, 16),)),
        "channel_downbias": scatter_about(seeds[30], (D,), 0.3, 2.0, (), jnp.float32),
    }


HIGH = lax.Precision.HIGHEST
EPSILON = 1e-05

@jax.custom_vjp
def low(v):
    return lax.optimization_barrier(v.astype(jnp.bfloat16)).astype(jnp.float32)

@jax.custom_vjp
def low_back(v):
    return v

def low_keep(v):
    return (low(v), None)

def low_pass(kept, grad):
    return (grad,)

def back_keep(v):
    return (v, None)

def back_low(kept, grad):
    return (low(grad),)
low.defvjp(low_keep, low_pass)
low_back.defvjp(back_keep, back_low)

def matmul(left, right):
    return jnp.dot(left, right, precision=HIGH)

def matmul_transposed(left, right):
    return lax.dot_general(left, right, (((1,), (1,)), ((), ())), precision=HIGH)

def layer_norm(values, gain, shift):
    center = lax.optimization_barrier(jnp.mean(values, axis=-1, keepdims=True))
    spread = lax.optimization_barrier(jnp.mean(values * values, axis=-1, keepdims=True)) - center * center
    return (values - center) * lax.rsqrt(spread + EPSILON) * gain + shift

def depthwise(values, kernel, bias):
    images = values.shape[0] // (PADDED * PADDED)
    grid = values.reshape(images, PADDED, PADDED, values.shape[1])
    padded = jnp.pad(grid, ((0, 0), (1, 1), (1, 1), (0, 0)))
    total = jnp.zeros_like(grid)
    for offset in range(9):
        across = offset // 3
        along = offset % 3
        total = total + padded[:, across:across + PADDED, along:along + PADDED, :] * kernel[offset]
    return total.reshape(values.shape) + bias

def to_windows(values):
    images = values.shape[0] // (PADDED * PADDED)
    side = PADDED // WINDOW
    grid = values.reshape(images, side, WINDOW, side, WINDOW, values.shape[1])
    return grid.transpose(0, 1, 3, 2, 4, 5).reshape(images * side * side, WINDOW * WINDOW, values.shape[1])

def from_windows(values):
    side = PADDED // WINDOW
    images = values.shape[0] // (side * side)
    grid = values.reshape(images, side, side, WINDOW, WINDOW, values.shape[2])
    return grid.transpose(0, 1, 3, 2, 4, 5).reshape(images * PADDED * PADDED, values.shape[2])

def split_heads(values):
    return values.reshape(values.shape[0], values.shape[1], values.shape[2] // HD, HD)

def window_attention(query_rows, key_rows, value_rows, present):
    queries = split_heads(to_windows(query_rows))
    keyset = split_heads(to_windows(key_rows))
    valueset = split_heads(to_windows(value_rows))
    keep = to_windows(present)[:, None, None, :, 0] > 0.5
    scores = low_back(jnp.einsum('wqhd,wkhd->whqk', queries, keyset, precision=HIGH) * HD ** (-0.5))
    scores = jnp.where(keep, scores, -1000000000.0)
    weights = low(jax.nn.softmax(scores, axis=-1))
    mixed = jnp.einsum('whqk,wkhd->wqhd', weights, valueset, precision=HIGH)
    return from_windows(mixed.reshape(mixed.shape[0], mixed.shape[1], -1))

def image_heads(values):
    return values.reshape(values.shape[0] // (PADDED * PADDED), PADDED * PADDED, values.shape[1] // HD, HD)

def channel_attention(query_rows, key_rows, value_rows, present):
    queries = image_heads(query_rows)
    keyset = image_heads(key_rows * present)
    valueset = image_heads(value_rows)
    scores = low_back(jnp.einsum('nthi,nthj->nhij', keyset, valueset, precision=HIGH) * HD ** (-0.5))
    weights = low(jax.nn.softmax(scores, axis=-1))
    mixed = jnp.einsum('nhij,nthj->nthi', weights, queries, precision=HIGH)
    return mixed.reshape(query_rows.shape)

def feed_forward(values, gain, shift, upward, upbias, downward, downbias):
    normed = low(layer_norm(values, gain, shift))
    hidden = low(jax.nn.gelu(low_back(matmul_transposed(normed, upward) + upbias), approximate=False))
    return low_back(matmul(hidden, downward)) + downbias

def dual_block(values, present, params):
    wkernel, wcbias, wgain, wshift, winw, winb, woutw, woutb, wgain_two, wshift_two, wupw, wupb, wdownw, wdownb, ckernel, ccbias, cgain, cshift, cinw, cinb, coutw, coutb, cgain_two, cshift_two, cupw, cupb, cdownw, cdownb = params
    start = values * present
    after_conv = start + present * depthwise(start, wkernel, wcbias)
    normed = low(layer_norm(after_conv, wgain, wshift))
    query_rows = low(low_back(matmul_transposed(normed, winw[0]) + winb[0]))
    key_rows = low(low_back(matmul_transposed(normed, winw[1])))
    value_rows = low(low_back(matmul_transposed(normed, winw[2]) + winb[1]))
    mixed = low(low_back(window_attention(query_rows, key_rows, value_rows, present)))
    after_attn = after_conv + present * (low_back(matmul(mixed, woutw)) + woutb)
    after_mlp = after_attn + present * feed_forward(after_attn, wgain_two, wshift_two, wupw, wupb, wdownw, wdownb)
    after_conv_c = after_mlp + present * depthwise(after_mlp, ckernel, ccbias)
    normed = low(layer_norm(after_conv_c, cgain, cshift))
    query_rows = low(low_back(matmul_transposed(normed, cinw[0]) + cinb[0]))
    key_rows = low(low_back(matmul_transposed(normed, cinw[1]) + cinb[1]))
    value_rows = low(low_back(matmul_transposed(normed, cinw[2]) + cinb[2]))
    mixed = low(low_back(channel_attention(query_rows, key_rows, value_rows, present)))
    after_attn_c = after_conv_c + present * (low_back(matmul(mixed, coutw)) + coutb)
    return after_attn_c + present * feed_forward(after_attn_c, cgain_two, cshift_two, cupw, cupb, cdownw, cdownb)

def reference(inputs, grid_sizes, cotangent, window_convkernel, window_convbias, window_gainone, window_shiftone, window_inweights, window_inbias, window_outweights, window_outbias, window_gaintwo, window_shifttwo, window_upweights, window_upbias, window_downweights, window_downbias, channel_convkernel, channel_convbias, channel_gainone, channel_shiftone, channel_inweights, channel_inbias, channel_outweights, channel_outbias, channel_gaintwo, channel_shifttwo, channel_upweights, channel_upbias, channel_downweights, channel_downbias):
    params = tuple((item.astype(jnp.float32) for item in (window_convkernel, window_convbias, window_gainone, window_shiftone, window_inweights, window_inbias, window_outweights, window_outbias, window_gaintwo, window_shifttwo, window_upweights, window_upbias, window_downweights, window_downbias, channel_convkernel, channel_convbias, channel_gainone, channel_shiftone, channel_inweights, channel_inbias, channel_outweights, channel_outbias, channel_gaintwo, channel_shifttwo, channel_upweights, channel_upbias, channel_downweights, channel_downbias)))
    images = grid_sizes.shape[0]
    group = max((divisor for divisor in range(1, 21) if images % divisor == 0))
    rounds = images // group
    width = inputs.shape[1]
    side = jnp.arange(PADDED, dtype=jnp.int32)
    inside = (side[None, :, None] < grid_sizes[:, None, None]) & (side[None, None, :] < grid_sizes[:, None, None])
    present = inside.astype(jnp.float32).reshape(rounds, group * PADDED * PADDED, 1)
    values = inputs.astype(jnp.float32).reshape(rounds, group * PADDED * PADDED, width)
    incoming = cotangent.astype(jnp.float32).reshape(rounds, group * PADDED * PADDED, width)

    def one_group(totals, piece):
        piece_values, piece_present, piece_grad = piece
        result, pullback = jax.vjp(lambda state, weights: dual_block(state, piece_present, weights), piece_values, params)
        grad_values, grad_params = pullback(piece_grad)
        return (jax.tree.map(jnp.add, totals, grad_params), (result, grad_values))
    zeros = jax.tree.map(jnp.zeros_like, params)
    totals, (outputs, input_grad) = lax.scan(one_group, zeros, (values, present, incoming))
    g00, g01, g02, g03, g04, g05, g06, g07, g08, g09, g10, g11, g12, g13, g14, g15, g16, g17, g18, g19, g20, g21, g22, g23, g24, g25, g26, g27 = totals
    return (outputs.reshape(-1, width), input_grad.reshape(-1, width), g00, g01, g02, g03, g04, g05, g06, g07, g08, g09, g10, g11, g12, g13, g14, g15, g16, g17, g18, g19, g20, g21, g22, g23, g24, g25, g26, g27)
```

```python
from functools import partial

import jax
import jax.numpy as jnp
from jax import lax
from jax.sharding import PartitionSpec as P

HD = 32
WINDOW = 7
PADDED = 14


EPSILON = 1e-05


def presence(sizes):
    cells = jnp.arange(PADDED, dtype=jnp.int32)
    inside = (cells[None, :, None] < sizes[:, None, None]) & (
        cells[None, None, :] < sizes[:, None, None]
    )
    return inside.astype(jnp.float32).reshape(-1, 1)


def depthwise(values, kernel, bias):
    images = values.shape[0] // (PADDED * PADDED)
    grid_cells = values.reshape(images, PADDED, PADDED, values.shape[1])
    padded = jnp.pad(grid_cells, ((0, 0), (1, 1), (1, 1), (0, 0)))
    total = jnp.zeros_like(grid_cells)
    for offset in range(9):
        across = offset // 3
        along = offset % 3
        total = (
            total + padded[:, across : across + PADDED, along : along + PADDED, :] * kernel[offset]
        )
    return total.reshape(values.shape) + bias


def to_windows(values):
    images = values.shape[0] // (PADDED * PADDED)
    window_side = PADDED // WINDOW
    grid_cells = values.reshape(images, window_side, WINDOW, window_side, WINDOW, values.shape[1])
    return grid_cells.transpose(0, 1, 3, 2, 4, 5).reshape(
        images * window_side * window_side, WINDOW * WINDOW, values.shape[1]
    )


def from_windows(values):
    window_side = PADDED // WINDOW
    images = values.shape[0] // (window_side * window_side)
    grid_cells = values.reshape(images, window_side, window_side, WINDOW, WINDOW, values.shape[2])
    return grid_cells.transpose(0, 1, 3, 2, 4, 5).reshape(images * PADDED * PADDED, values.shape[2])


def split_heads(values):
    return values.reshape(values.shape[0], values.shape[1], values.shape[2] // HD, HD)


def image_heads(values):
    return values.reshape(
        values.shape[0] // (PADDED * PADDED), PADDED * PADDED, values.shape[1] // HD, HD
    )


def outer(left, right):
    return lax.dot_general(
        left, right, (((0,), (0,)), ((), ())), preferred_element_type=jnp.float32
    )


def times_transposed(left, right):
    return lax.dot_general(
        left, right, (((1,), (1,)), ((), ())), preferred_element_type=jnp.float32
    )


def norm_forward(values, norm_gain, bias_shift):
    center = jnp.mean(values, axis=1, keepdims=True)
    scaled = lax.rsqrt(jnp.mean(values * values, axis=1, keepdims=True) - center * center + EPSILON)
    normal = (values - center) * scaled
    return ((normal * norm_gain + bias_shift).astype(jnp.bfloat16), normal, scaled)


def norm_backward(grad_normed, normal, scaled, norm_gain):
    grad_normal = grad_normed * norm_gain
    first_mean = jnp.mean(grad_normal, axis=1, keepdims=True)
    second_mean = jnp.mean(grad_normal * normal, axis=1, keepdims=True)
    grad_in = scaled * (grad_normal - first_mean - normal * second_mean)
    return (grad_in, jnp.sum(grad_normed * normal, axis=0), jnp.sum(grad_normed, axis=0))


def gather_rows(normed):
    return normed


def reduce_rows(operand, weight):
    return jnp.dot(operand, weight, preferred_element_type=jnp.float32)


def project_heads(mixed_rows, outweights):
    return reduce_rows(mixed_rows, outweights)


def gather_grads(grads):
    return grads


def reduce_back(operand, weight):
    return jnp.dot(operand, weight, preferred_element_type=jnp.float32)


def sibling(values):
    pairs = [(index, index ^ 1) for index in range(lax.axis_size("dp"))]
    return lax.ppermute(values, "dp", pairs)


def own_half(values):
    half = values.shape[-1] // 2
    first = lax.rem(lax.axis_index("dp"), 2) == 0
    return jnp.where(first, values[..., :half], values[..., half:])


def other_half(values):
    half = values.shape[-1] // 2
    first = lax.rem(lax.axis_index("dp"), 2) == 0
    return jnp.where(first, values[..., half:], values[..., :half])


def join_halves(own, other):
    first = lax.rem(lax.axis_index("dp"), 2) == 0
    return jnp.concatenate([jnp.where(first, own, other), jnp.where(first, other, own)], axis=-1)


def gather_matrix(shard, axis):
    own = lax.all_gather(own_half(shard), ("hid", "wid"), axis=axis, tiled=True)
    return join_halves(own, sibling(own))


def scatter_matrix(grads, axis):
    rounded = grads.astype(jnp.bfloat16)
    both = own_half(rounded).astype(jnp.float32) + sibling(other_half(rounded)).astype(jnp.float32)
    piece = lax.psum_scatter(
        both.astype(jnp.bfloat16), ("hid", "wid"), scatter_dimension=axis, tiled=True
    ).astype(jnp.float32)
    total = piece
    for shift in range(2, lax.axis_size("dp"), 2):
        pairs = [(index, (index + shift) % lax.axis_size("dp")) for index in range(lax.axis_size("dp"))]
        total = total + lax.ppermute(piece, "dp", pairs)
    return join_halves(total, sibling(total))


def own_rows(values, axis):
    length = values.shape[axis] // lax.axis_size("hid")
    return lax.dynamic_slice_in_dim(values, lax.axis_index("hid") * length, length, axis)


def window_scores(query_rows, key_rows, present):
    queries = split_heads(to_windows(query_rows))
    keyset = split_heads(to_windows(key_rows))
    scores = jnp.einsum(
        "wqhd,wkhd->whqk", queries, keyset, preferred_element_type=jnp.float32
    ) * HD ** (-0.5)
    keep_mask = to_windows(present)[:, None, None, :, 0] > 0.5
    return (jnp.where(keep_mask, scores, -1000000000.0), keep_mask)


def window_forward(query_rows, key_rows, value_rows, present):
    scores, keep_mask = window_scores(query_rows, key_rows, present)
    totals = jax.nn.logsumexp(scores, axis=-1, keepdims=True)
    weights = jnp.exp(scores - totals).astype(jnp.bfloat16)
    valueset = split_heads(to_windows(value_rows))
    mixed_rows = jnp.einsum(
        "whqk,wkhd->wqhd", weights, valueset, preferred_element_type=jnp.float32
    )
    return (
        from_windows(mixed_rows.reshape(mixed_rows.shape[0], mixed_rows.shape[1], -1)).astype(
            jnp.bfloat16
        ),
        totals,
    )


def window_backward(grad_mixed, query_rows, key_rows, value_rows, totals, present):
    scores, keep_mask = window_scores(query_rows, key_rows, present)
    probabilities = jnp.exp(scores - totals)
    weights = probabilities.astype(jnp.bfloat16)
    incoming = split_heads(to_windows(grad_mixed))
    queries = split_heads(to_windows(query_rows))
    keyset = split_heads(to_windows(key_rows))
    valueset = split_heads(to_windows(value_rows))
    grad_probs = jnp.einsum(
        "wqhd,wkhd->whqk", incoming, valueset, preferred_element_type=jnp.float32
    )
    grad_scores = probabilities * (
        grad_probs - jnp.sum(probabilities * grad_probs, axis=-1, keepdims=True)
    )
    grad_scores = jnp.where(keep_mask, grad_scores, 0.0).astype(jnp.bfloat16)
    grad_query = jnp.einsum(
        "whqk,wkhd->wqhd", grad_scores, keyset, preferred_element_type=jnp.float32
    ) * HD ** (-0.5)
    grad_keys = jnp.einsum(
        "whqk,wqhd->wkhd", grad_scores, queries, preferred_element_type=jnp.float32
    ) * HD ** (-0.5)
    grad_values = jnp.einsum(
        "whqk,wqhd->wkhd", weights, incoming, preferred_element_type=jnp.float32
    )

    def restore(grads):
        return from_windows(grads.reshape(grads.shape[0], grads.shape[1], -1))

    return (restore(grad_query), restore(grad_keys), restore(grad_values))


def channel_forward(query_rows, key_rows, value_rows, present):
    keyset = image_heads(key_rows * present.astype(jnp.bfloat16))
    valueset = image_heads(value_rows)
    scores = jnp.einsum(
        "nthi,nthj->nhij", keyset, valueset, preferred_element_type=jnp.float32
    ) * HD ** (-0.5)
    probabilities = jax.nn.softmax(scores, axis=-1)
    mixed_rows = jnp.einsum(
        "nhij,nthj->nthi",
        probabilities.astype(jnp.bfloat16),
        image_heads(query_rows),
        preferred_element_type=jnp.float32,
    )
    return (mixed_rows.reshape(query_rows.shape).astype(jnp.bfloat16), probabilities)


def channel_backward(grad_mixed, query_rows, key_rows, value_rows, probabilities, present):
    incoming = image_heads(grad_mixed)
    queries = image_heads(query_rows)
    keyset = image_heads(key_rows * present.astype(jnp.bfloat16))
    valueset = image_heads(value_rows)
    token_mask = image_heads(jnp.broadcast_to(present, (present.shape[0], HD)))
    grad_probs = jnp.einsum(
        "nthi,nthj->nhij", incoming, queries, preferred_element_type=jnp.float32
    )
    grad_query = jnp.einsum(
        "nhij,nthi->nthj",
        probabilities.astype(jnp.bfloat16),
        incoming,
        preferred_element_type=jnp.float32,
    )
    grad_scores = probabilities * (
        grad_probs - jnp.sum(probabilities * grad_probs, axis=-1, keepdims=True)
    )
    grad_scores = grad_scores.astype(jnp.bfloat16)
    grad_keys = jnp.einsum(
        "nhij,nthj->nthi", grad_scores, valueset, preferred_element_type=jnp.float32
    )
    grad_keys = grad_keys * HD ** (-0.5) * token_mask
    grad_values = jnp.einsum(
        "nhij,nthi->nthj", grad_scores, keyset, preferred_element_type=jnp.float32
    ) * HD ** (-0.5)
    row_shape = query_rows.shape
    return (
        grad_query.reshape(row_shape),
        grad_keys.reshape(row_shape),
        grad_values.reshape(row_shape),
    )


def conv_backward(grad_values, values, kernel, bias, present):
    pullback = jax.vjp(depthwise, values, kernel, bias)[1]
    grad_in, grad_kernel, grad_bias = pullback(grad_values * present)
    return (grad_values + grad_in, grad_kernel, grad_bias)


def attention_forward(
    values,
    present,
    group_present,
    norm_gain,
    bias_shift,
    inweights,
    inbias,
    outweights,
    outbias,
    windowed,
):
    normed, normal, scaled = norm_forward(values, norm_gain, bias_shift)
    gathered = gather_rows(normed)
    stacked = inweights.reshape(-1, inweights.shape[2])
    projected = times_transposed(gathered, stacked)
    head_width = inweights.shape[1]
    query_rows = (projected[:, :head_width] + inbias[0]).astype(jnp.bfloat16)
    key_part = projected[:, head_width : 2 * head_width]
    if not windowed:
        key_part = key_part + inbias[1]
    key_rows = key_part.astype(jnp.bfloat16)
    value_rows = (projected[:, 2 * head_width :] + inbias[inbias.shape[0] - 1]).astype(jnp.bfloat16)
    if windowed:
        mixed_rows, saved_stat = window_forward(query_rows, key_rows, value_rows, group_present)
    else:
        mixed_rows, saved_stat = channel_forward(query_rows, key_rows, value_rows, group_present)
    branch = project_heads(mixed_rows, outweights) + outbias
    saved = (
        gathered,
        normal,
        scaled,
        stacked,
        query_rows,
        key_rows,
        value_rows,
        saved_stat,
        mixed_rows,
    )
    return (values + present * branch, saved)


def attention_backward(grad_values, saved, present, group_present, norm_gain, outweights, windowed):
    gathered, normal, scaled, stacked, query_rows, key_rows, value_rows, saved_stat, mixed_rows = (
        saved
    )
    grad_branch = grad_values * present
    full_grads = gather_grads(grad_branch.astype(jnp.bfloat16))
    grad_outweights = outer(mixed_rows, full_grads)
    grad_mixed = times_transposed(full_grads, outweights).astype(jnp.bfloat16)
    if windowed:
        grad_query, grad_keys, grad_value_rows = window_backward(
            grad_mixed, query_rows, key_rows, value_rows, saved_stat, group_present
        )
    else:
        grad_query, grad_keys, grad_value_rows = channel_backward(
            grad_mixed, query_rows, key_rows, value_rows, saved_stat, group_present
        )
    rounded = jnp.concatenate([grad_query, grad_keys, grad_value_rows], axis=1).astype(jnp.bfloat16)
    column_sums = jnp.sum(rounded, axis=0, dtype=jnp.float32).reshape(3, -1)
    if windowed:
        grad_inbias = jnp.stack([column_sums[0], column_sums[2]])
    else:
        grad_inbias = column_sums
    grad_stacked = outer(rounded, gathered)
    grad_inweights = grad_stacked.reshape(3, -1, grad_stacked.shape[1])
    grad_in, grad_gain, grad_shift = norm_backward(
        reduce_back(rounded, stacked), normal, scaled, norm_gain
    )
    little_grads = (grad_gain, grad_shift, jnp.sum(grad_branch, axis=0))
    return (grad_values + grad_in, little_grads, grad_inbias, grad_inweights, grad_outweights)


def gelu_back(hidden, grad_acted):
    pullback = jax.vjp(partial(jax.nn.gelu, approximate=False), hidden)[1]
    return pullback(grad_acted)[0].astype(jnp.bfloat16)


def mlp_forward(values, norm_gain, bias_shift, upward, upbias, downward, downbias, present):
    normed, normal, scaled = norm_forward(values, norm_gain, bias_shift)
    gathered = gather_rows(normed)
    hidden = times_transposed(gathered, upward) + upbias
    acted = jax.nn.gelu(hidden, approximate=False).astype(jnp.bfloat16)
    branch = reduce_rows(acted, downward) + downbias
    return (values + present * branch, (gathered, hidden, acted, normal, scaled))


def mlp_backward(grad_values, saved, norm_gain, upward, downward, present):
    gathered, hidden, acted, normal, scaled = saved
    grad_branch = grad_values * present
    full_grads = gather_grads(grad_branch.astype(jnp.bfloat16))
    grad_down = outer(acted, full_grads)
    grad_hidden = gelu_back(hidden, times_transposed(full_grads, downward))
    grad_upbias = jnp.sum(grad_hidden, axis=0, dtype=jnp.float32)
    grad_up = outer(grad_hidden, gathered)
    grad_in, grad_gain, grad_shift = norm_backward(
        reduce_back(grad_hidden, upward), normal, scaled, norm_gain
    )
    little_grads = (grad_gain, grad_shift, jnp.sum(grad_branch, axis=0))
    return (grad_values + grad_in, little_grads, grad_upbias, grad_up, grad_down)


def body(
    inputs,
    grid_sizes,
    cotangent,
    window_convkernel,
    window_convbias,
    window_gainone,
    window_shiftone,
    window_inweights,
    window_inbias,
    window_outweights,
    window_outbias,
    window_gaintwo,
    window_shifttwo,
    window_upweights,
    window_upbias,
    window_downweights,
    window_downbias,
    channel_convkernel,
    channel_convbias,
    channel_gainone,
    channel_shiftone,
    channel_inweights,
    channel_inbias,
    channel_outweights,
    channel_outbias,
    channel_gaintwo,
    channel_shifttwo,
    channel_upweights,
    channel_upbias,
    channel_downweights,
    channel_downbias,
):
    image_count = inputs.shape[0] // (PADDED * PADDED)
    place = (lax.axis_index("hid") * lax.axis_size("wid") + lax.axis_index("wid")) * image_count
    present = presence(lax.dynamic_slice_in_dim(grid_sizes, place, image_count, 0))
    group_present = present
    local = (
        gather_matrix(window_inweights, 1),
        gather_matrix(window_outweights, 0),
        gather_matrix(window_upweights, 0),
        gather_matrix(window_downweights, 0),
        gather_matrix(channel_inweights, 1),
        gather_matrix(channel_outweights, 0),
        gather_matrix(channel_upweights, 0),
        gather_matrix(channel_downweights, 0),
    )
    window_inbias = lax.all_gather(window_inbias, "hid", axis=1, tiled=True)
    window_upbias = lax.all_gather(window_upbias, "hid", axis=0, tiled=True)
    channel_inbias = lax.all_gather(channel_inbias, "hid", axis=1, tiled=True)
    channel_upbias = lax.all_gather(channel_upbias, "hid", axis=0, tiled=True)
    start = inputs * present
    after_conv = start + present * depthwise(start, window_convkernel, window_convbias)
    after_attn, saved_one = attention_forward(
        after_conv,
        present,
        group_present,
        window_gainone,
        window_shiftone,
        local[0],
        window_inbias,
        local[1],
        window_outbias,
        True,
    )
    after_mlp, saved_two = mlp_forward(
        after_attn,
        window_gaintwo,
        window_shifttwo,
        local[2],
        window_upbias,
        local[3],
        window_downbias,
        present,
    )
    after_conv_c = after_mlp + present * depthwise(after_mlp, channel_convkernel, channel_convbias)
    after_attn_c, saved_three = attention_forward(
        after_conv_c,
        present,
        group_present,
        channel_gainone,
        channel_shiftone,
        local[4],
        channel_inbias,
        local[5],
        channel_outbias,
        False,
    )
    outputs, saved_four = mlp_forward(
        after_attn_c,
        channel_gaintwo,
        channel_shifttwo,
        local[6],
        channel_upbias,
        local[7],
        channel_downbias,
        present,
    )
    flowing, little_four, upbias_four, up_four, down_four = mlp_backward(
        cotangent, saved_four, channel_gaintwo, local[6], local[7], present
    )
    flowing, little_three, inbias_three, in_three, out_three = attention_backward(
        flowing, saved_three, present, group_present, channel_gainone, local[5], False
    )
    flowing, kernel_three, convbias_three = conv_backward(
        flowing, after_mlp, channel_convkernel, channel_convbias, present
    )
    flowing, little_two, upbias_two, up_two, down_two = mlp_backward(
        flowing, saved_two, window_gaintwo, local[2], local[3], present
    )
    flowing, little_one, inbias_one, in_one, out_one = attention_backward(
        flowing, saved_one, present, group_present, window_gainone, local[1], True
    )
    flowing, kernel_one, convbias_one = conv_backward(
        flowing, start, window_convkernel, window_convbias, present
    )
    input_grad = flowing * present
    tokens = lax.psum(
        (
            kernel_one,
            convbias_one,
            little_one[0],
            little_one[1],
            little_one[2],
            little_two[0],
            little_two[1],
            little_two[2],
            kernel_three,
            convbias_three,
            little_three[0],
            little_three[1],
            little_three[2],
            little_four[0],
            little_four[1],
            little_four[2],
        ),
        ("dp", "hid", "wid"),
    )
    heads = lax.psum(
        (inbias_one, upbias_two, inbias_three, upbias_four), ("dp", "hid", "wid")
    )
    heads = (
        own_rows(heads[0], 1),
        own_rows(heads[1], 0),
        own_rows(heads[2], 1),
        own_rows(heads[3], 0),
    )
    weights = (
        scatter_matrix(in_one, 1),
        scatter_matrix(out_one, 0),
        scatter_matrix(up_two, 0),
        scatter_matrix(down_two, 0),
        scatter_matrix(in_three, 1),
        scatter_matrix(out_three, 0),
        scatter_matrix(up_four, 0),
        scatter_matrix(down_four, 0),
    )
    return (
        outputs,
        input_grad,
        tokens[0],
        tokens[1],
        tokens[2],
        tokens[3],
        weights[0],
        heads[0],
        weights[1],
        tokens[4],
        tokens[5],
        tokens[6],
        weights[2],
        heads[1],
        weights[3],
        tokens[7],
        tokens[8],
        tokens[9],
        tokens[10],
        tokens[11],
        weights[4],
        heads[2],
        weights[5],
        tokens[12],
        tokens[13],
        tokens[14],
        weights[6],
        heads[3],
        weights[7],
        tokens[15],
    )


def solution(mesh):
    placed = (
        P(("dp", "hid", "wid"), None),
        P("dp"),
        P(("dp", "hid", "wid"), None),
        P(),
        P(),
        P(),
        P(),
        P(None, ("hid", "wid"), None),
        P(None, "hid"),
        P(("hid", "wid"), None),
        P(),
        P(),
        P(),
        P(("hid", "wid"), None),
        P("hid"),
        P(("hid", "wid"), None),
        P(),
        P(),
        P(),
        P(),
        P(),
        P(None, ("hid", "wid"), None),
        P(None, "hid"),
        P(("hid", "wid"), None),
        P(),
        P(),
        P(),
        P(("hid", "wid"), None),
        P("hid"),
        P(("hid", "wid"), None),
        P(),
    )
    return jax.shard_map(
        body,
        mesh=mesh,
        in_specs=placed,
        out_specs=(
            P(("dp", "hid", "wid"), None),
            P(("dp", "hid", "wid"), None),
            P(),
            P(),
            P(),
            P(),
            P(None, ("hid", "wid"), None),
            P(None, "hid"),
            P(("hid", "wid"), None),
            P(),
            P(),
            P(),
            P(("hid", "wid"), None),
            P("hid"),
            P(("hid", "wid"), None),
            P(),
            P(),
            P(),
            P(),
            P(),
            P(None, ("hid", "wid"), None),
            P(None, "hid"),
            P(("hid", "wid"), None),
            P(),
            P(),
            P(),
            P(("hid", "wid"), None),
            P("hid"),
            P(("hid", "wid"), None),
            P(),
        ),
        check_vma=False,
    )
```

```python
from functools import partial

import jax
import jax.numpy as jnp
from jax import lax
from jax.sharding import PartitionSpec as P

HD = 32
WINDOW = 7
PADDED = 14
GRID = 12
CELLS = GRID * GRID
EPSILON = 1e-05
F32 = jnp.float32
BF16 = jnp.bfloat16
SCALE = HD ** (-0.5)


def exchange(values, axis, bit):
    pairs = [(index, index ^ bit) for index in range(lax.axis_size(axis))]
    return lax.ppermute(values, axis, pairs)


def sibling(values):
    return exchange(values, "dp", 1)


def cross(values, first):
    hids = lax.axis_size("hid")
    pairs = []
    for core in range(lax.axis_size("dp")):
        bit = 1 if (core % 2 == 0) == first else 2
        pairs += [(core * hids + index, core * hids + (index ^ bit)) for index in range(hids)]
    return lax.ppermute(values, ("dp", "hid"), pairs)


def second_core():
    return lax.rem(lax.axis_index("dp"), 2) == 1


def gather_half(piece):
    near = piece[None]
    near = jnp.concatenate([near, exchange(near, "wid", 1)], axis=0)
    near = jnp.concatenate([near, exchange(near, "wid", 2)], axis=0)
    near = jnp.concatenate([near, cross(near, True)], axis=0)
    return near, cross(near, False)


def scatter_half(near, far):
    near = near.astype(F32) + cross(far, False).astype(F32)
    near = near[:4] + cross(near[4:].astype(BF16), True).astype(F32)
    near = near[:2] + exchange(near[2:].astype(BF16), "wid", 2).astype(F32)
    total = near[0] + exchange(near[1].astype(BF16), "wid", 1).astype(F32)
    bit = 2
    while bit < lax.axis_size("dp"):
        total = total + exchange(total, "dp", bit)
        bit *= 2
    return total


def sum_everywhere(values):
    for axis in ("dp", "hid", "wid"):
        bit = 1
        while bit < lax.axis_size(axis):
            values = values + exchange(values, axis, bit)
            bit *= 2
    return values


def by_core(own, other, axis):
    second = second_core()
    return jnp.concatenate(
        [jnp.where(second, other, own), jnp.where(second, own, other)], axis=axis
    )


def half_of(values, axis, mine):
    half = values.shape[axis] // 2
    first = lax.slice_in_dim(values, 0, half, axis=axis)
    last = lax.slice_in_dim(values, half, 2 * half, axis=axis)
    second = second_core()
    return jnp.where(second, last, first) if mine else jnp.where(second, first, last)


def flip(values, axis, by):
    for bit in (1, 2):
        length = values.shape[axis]
        parts = [lax.slice_in_dim(values, i, i + 1, axis=axis) for i in range(length)]
        swapped = jnp.concatenate([parts[i ^ bit] for i in range(length)], axis=axis)
        values = jnp.where((by & bit) != 0, swapped, values)
    return values


def hid_turn(core_is_second):
    return core_is_second


def relative_hid(values, axis, second):
    values = flip(values, axis, lax.axis_index("hid"))
    parts = [lax.slice_in_dim(values, i, i + 1, axis=axis) for i in range(4)]
    swapped = jnp.concatenate([parts[0], parts[2], parts[1], parts[3]], axis=axis)
    return jnp.where(second, swapped, values)


def absolute_hid(values, axis, second):
    parts = [lax.slice_in_dim(values, i, i + 1, axis=axis) for i in range(4)]
    swapped = jnp.concatenate([parts[0], parts[2], parts[1], parts[3]], axis=axis)
    return flip(jnp.where(second, swapped, values), axis, lax.axis_index("hid"))


def gather_bias(bias):
    other = exchange(bias, "hid", 1)
    pair = jnp.stack([bias, other], axis=-2)
    both = jnp.concatenate([pair, exchange(pair, "hid", 2)], axis=-2)
    return flip(both, both.ndim - 2, lax.axis_index("hid"))


def hidden_order(bias):
    table = bias.reshape(4, 4, 2, -1)
    table = flip(table, 1, lax.axis_index("wid"))
    second = second_core()
    own = jnp.where(second, table[:, :, 1], table[:, :, 0])
    other = jnp.where(second, table[:, :, 0], table[:, :, 1])
    own = relative_hid(own, 0, second)
    other = relative_hid(other, 0, jnp.logical_not(second))
    return jnp.concatenate([own.reshape(-1), other.reshape(-1)])


def hidden_back(grads):
    table = grads.reshape(2, 4, 4, -1)
    second = second_core()
    own = absolute_hid(table[0], 0, second)
    other = absolute_hid(table[1], 0, jnp.logical_not(second))
    both = jnp.stack([jnp.where(second, other, own), jnp.where(second, own, other)], axis=2)
    return flip(both, 1, lax.axis_index("wid")).reshape(4, -1)


def gather_hidden(weights):
    near, far = gather_half(half_of(weights, 0, True))
    width = weights.shape[1]
    other_near, other_far = sibling(near), sibling(far)
    return jnp.concatenate([part.reshape(-1, width) for part in (near, far, other_near, other_far)])


def scatter_hidden(grads):
    rows = grads.shape[0] // 16
    pieces = grads.reshape(2, 8, rows, grads.shape[1])
    total = scatter_half(pieces[0], pieces[1])
    return by_core(total, sibling(total), 0)


def gather_attention(inweights, outweights):
    piece = half_of(jnp.concatenate([inweights, outweights[None]], axis=0), 2, True)
    near, far = gather_half(piece)
    second = second_core()

    def arrange(near, far, second):
        table = jnp.concatenate([near, far]).reshape((4, 4) + piece.shape)
        table = flip(table, 1, lax.axis_index("wid"))
        parts = [table[i : i + 1] for i in range(4)]
        swapped = jnp.concatenate([parts[0], parts[2], parts[1], parts[3]])
        table = jnp.where(second, swapped, table)
        return table.transpose(2, 0, 1, 3, 4).reshape(4, -1, piece.shape[2])

    own = arrange(near, far, second)
    other = arrange(sibling(near), sibling(far), jnp.logical_not(second))
    return by_core(own, other, 2)


def scatter_attention(grads):
    second = second_core()
    table = grads.reshape(4, 4, 4, -1, grads.shape[2]).transpose(1, 2, 0, 3, 4)
    parts = [table[i : i + 1] for i in range(4)]
    swapped = jnp.concatenate([parts[0], parts[2], parts[1], parts[3]])
    table = flip(jnp.where(second, swapped, table), 1, lax.axis_index("wid"))
    table = table.reshape((2, 8) + table.shape[2:])
    total = scatter_half(table[0], table[1])
    return by_core(total, sibling(total), 2)


def compact(values):
    slots = values.reshape(-1, PADDED, PADDED, values.shape[1])
    return slots[:, :GRID, :GRID].reshape(-1, values.shape[1])


def expand(values):
    slots = values.reshape(-1, GRID, GRID, values.shape[1])
    rest = PADDED - GRID
    return jnp.pad(slots, ((0, 0), (0, rest), (0, rest), (0, 0))).reshape(-1, values.shape[1])


def presence(sizes):
    cells = jnp.arange(GRID, dtype=jnp.int32)
    inside = (cells[None, :, None] < sizes[:, None, None]) & (
        cells[None, None, :] < sizes[:, None, None]
    )
    return inside.astype(F32).reshape(-1, 1)


def depthwise(values, kernel, bias):
    images = values.shape[0] // CELLS
    grid_cells = values.reshape(images, GRID, GRID, values.shape[1])
    padded = jnp.pad(grid_cells, ((0, 0), (1, 1), (1, 1), (0, 0)))
    total = jnp.zeros_like(grid_cells)
    for offset in range(9):
        across = offset // 3
        along = offset % 3
        total = total + padded[:, across : across + GRID, along : along + GRID, :] * kernel[offset]
    return total.reshape(values.shape) + bias


def conv_backward(grad_values, values, kernel, bias, present):
    pullback = jax.vjp(depthwise, values, kernel, bias)[1]
    grad_in, grad_kernel, grad_bias = pullback(grad_values * present)
    return (grad_values + grad_in, grad_kernel, grad_bias)


def image_heads(values):
    return values.reshape(values.shape[0] // CELLS, CELLS, values.shape[1] // HD, HD)


def outer(left, right):
    return lax.dot_general(left, right, (((0,), (0,)), ((), ())), preferred_element_type=F32)


def times(left, right):
    return jnp.dot(left, right, preferred_element_type=F32)


def times_transposed(left, right):
    return lax.dot_general(left, right, (((1,), (1,)), ((), ())), preferred_element_type=F32)


def norm_forward(values, norm_gain, bias_shift):
    center = jnp.mean(values, axis=1, keepdims=True)
    scaled = lax.rsqrt(jnp.mean(values * values, axis=1, keepdims=True) - center * center + EPSILON)
    normal = (values - center) * scaled
    return ((normal * norm_gain + bias_shift).astype(BF16), normal, scaled)


def norm_backward(grad_normed, normal, scaled, norm_gain):
    grad_normal = grad_normed * norm_gain
    first_mean = jnp.mean(grad_normal, axis=1, keepdims=True)
    second_mean = jnp.mean(grad_normal * normal, axis=1, keepdims=True)
    grad_in = scaled * (grad_normal - first_mean - normal * second_mean)
    return (grad_in, jnp.sum(grad_normed * normal, axis=0), jnp.sum(grad_normed, axis=0))


def window_scores(query_rows, key_rows, keep_mask):
    scores = jnp.einsum(
        "nqhd,nkhd->nhqk", image_heads(query_rows), image_heads(key_rows), preferred_element_type=F32
    )
    return jnp.where(keep_mask, scores * SCALE, -1000000000.0)


def window_mask(present):
    cell = jnp.arange(CELLS, dtype=jnp.int32)
    window = (cell // GRID // WINDOW) * 2 + cell % GRID // WINDOW
    same = window[:, None] == window[None, :]
    return same[None, None] & (present.reshape(-1, 1, 1, CELLS) > 0.5)


def window_forward(query_rows, key_rows, value_rows, present):
    scores = window_scores(query_rows, key_rows, window_mask(present))
    totals = jax.nn.logsumexp(scores, axis=-1, keepdims=True)
    weights = jnp.exp(scores - totals).astype(BF16)
    mixed = jnp.einsum("nhqk,nkhd->nqhd", weights, image_heads(value_rows), preferred_element_type=F32)
    return mixed.reshape(query_rows.shape).astype(BF16), totals


def window_backward(grad_mixed, query_rows, key_rows, value_rows, totals, present):
    keep_mask = window_mask(present)
    scores = window_scores(query_rows, key_rows, keep_mask)
    probabilities = jnp.exp(scores - totals)
    weights = probabilities.astype(BF16)
    incoming = image_heads(grad_mixed)
    grad_probs = jnp.einsum("nqhd,nkhd->nhqk", incoming, image_heads(value_rows), preferred_element_type=F32)
    grad_scores = probabilities * (
        grad_probs - jnp.sum(probabilities * grad_probs, axis=-1, keepdims=True)
    )
    grad_scores = jnp.where(keep_mask, grad_scores, 0.0).astype(BF16)
    grad_query = jnp.einsum("nhqk,nkhd->nqhd", grad_scores, image_heads(key_rows), preferred_element_type=F32)
    grad_keys = jnp.einsum("nhqk,nqhd->nkhd", grad_scores, image_heads(query_rows), preferred_element_type=F32)
    grad_values = jnp.einsum("nhqk,nqhd->nkhd", weights, incoming, preferred_element_type=F32)
    shape = query_rows.shape
    return (
        (grad_query * SCALE).reshape(shape),
        (grad_keys * SCALE).reshape(shape),
        grad_values.reshape(shape),
    )


def channel_forward(query_rows, key_rows, value_rows, present):
    keyset = image_heads(key_rows * present.astype(BF16))
    scores = jnp.einsum("nthi,nthj->nhij", keyset, image_heads(value_rows), preferred_element_type=F32)
    probabilities = jax.nn.softmax(scores * SCALE, axis=-1)
    mixed = jnp.einsum(
        "nhij,nthj->nthi", probabilities.astype(BF16), image_heads(query_rows), preferred_element_type=F32
    )
    return (mixed.reshape(query_rows.shape).astype(BF16), probabilities)


def channel_backward(grad_mixed, query_rows, key_rows, value_rows, probabilities, present):
    incoming = image_heads(grad_mixed)
    queries = image_heads(query_rows)
    keyset = image_heads(key_rows * present.astype(BF16))
    valueset = image_heads(value_rows)
    grad_probs = jnp.einsum("nthi,nthj->nhij", incoming, queries, preferred_element_type=F32)
    grad_query = jnp.einsum("nhij,nthi->nthj", probabilities.astype(BF16), incoming, preferred_element_type=F32)
    grad_scores = probabilities * (
        grad_probs - jnp.sum(probabilities * grad_probs, axis=-1, keepdims=True)
    )
    grad_scores = grad_scores.astype(BF16)
    grad_keys = jnp.einsum("nhij,nthj->nthi", grad_scores, valueset, preferred_element_type=F32)
    grad_values = jnp.einsum("nhij,nthi->nthj", grad_scores, keyset, preferred_element_type=F32)
    shape = query_rows.shape
    return (
        grad_query.reshape(shape),
        grad_keys.reshape(shape) * SCALE * present,
        grad_values.reshape(shape) * SCALE,
    )


def attention_forward(values, present, gain, shift, weights, biases, outbias, windowed):
    normed, normal, scaled = norm_forward(values, gain, shift)
    query_rows = (times_transposed(normed, weights[0]) + biases[0]).astype(BF16)
    key_part = times_transposed(normed, weights[1])
    if not windowed:
        key_part = key_part + biases[1]
    key_rows = key_part.astype(BF16)
    value_rows = (times_transposed(normed, weights[2]) + biases[-1]).astype(BF16)
    attend = window_forward if windowed else channel_forward
    mixed, stat = attend(query_rows, key_rows, value_rows, present)
    branch = times(mixed, weights[3]) + outbias
    return values + present * branch, (normed, normal, scaled, query_rows, key_rows, value_rows, stat, mixed)


def attention_backward(grad_values, saved, present, gain, weights, windowed):
    normed, normal, scaled, query_rows, key_rows, value_rows, stat, mixed = saved
    grad_branch = grad_values * present
    low_branch = grad_branch.astype(BF16)
    grad_mixed = times_transposed(low_branch, weights[3]).astype(BF16)
    attend = window_backward if windowed else channel_backward
    grads = attend(grad_mixed, query_rows, key_rows, value_rows, stat, present)
    rounded = [item.astype(BF16) for item in grads]
    sums = [jnp.sum(item, axis=0, dtype=F32) for item in rounded]
    stacked = jnp.concatenate(rounded, axis=1)
    grad_normed = times(stacked, weights[:3].reshape(-1, weights.shape[2]))
    left = jnp.concatenate([stacked, mixed], axis=1)
    other_left = sibling(left)
    normed_half = jnp.concatenate([half_of(normed, 1, True), sibling(half_of(normed, 1, False))])
    branch_half = jnp.concatenate([half_of(low_branch, 1, True), sibling(half_of(low_branch, 1, False))])
    left = jnp.concatenate([left, other_left])
    cut = stacked.shape[1]
    grad_weights = jnp.concatenate([outer(left[:, :cut], normed_half), outer(left[:, cut:], branch_half)])
    grad_weights = grad_weights.astype(BF16).reshape(4, -1, grad_weights.shape[1])
    grad_in, grad_gain, grad_shift = norm_backward(grad_normed.astype(BF16).astype(F32), normal, scaled, gain)
    little = [grad_gain, grad_shift, jnp.sum(grad_branch, axis=0)]
    biases = [sums[0], sums[2]] if windowed else sums
    return grad_values + grad_in, little, biases, grad_weights


def mlp_forward(values, present, gain, shift, upward, upbias, downward, downbias):
    normed, normal, scaled = norm_forward(values, gain, shift)
    hidden = times_transposed(normed, upward) + upbias
    acted = jax.nn.gelu(hidden, approximate=False).astype(BF16)
    branch = times(acted, downward) + downbias
    return values + present * branch, (normed, normal, scaled, hidden, acted)


def gelu_back(hidden, grad_acted):
    pullback = jax.vjp(partial(jax.nn.gelu, approximate=False), hidden)[1]
    return pullback(grad_acted)[0].astype(BF16)


def mlp_backward(grad_values, saved, present, gain, upward, downward):
    normed, normal, scaled, hidden, acted = saved
    grad_branch = grad_values * present
    low_branch = grad_branch.astype(BF16)
    half = acted.shape[1] // 2
    branches = jnp.concatenate([low_branch, sibling(low_branch)])
    grad_down = outer(jnp.concatenate([acted[:, :half], sibling(acted[:, half:])]), branches)
    grad_hidden = gelu_back(hidden, times_transposed(low_branch, downward))
    grad_upbias = jnp.sum(grad_hidden, axis=0, dtype=F32)
    both_hidden = jnp.concatenate([grad_hidden[:, :half], sibling(grad_hidden[:, half:])])
    grad_up = outer(both_hidden, jnp.concatenate([normed, sibling(normed)]))
    grad_normed = times(grad_hidden, upward).astype(BF16).astype(F32)
    grad_in, grad_gain, grad_shift = norm_backward(grad_normed, normal, scaled, gain)
    little = [grad_gain, grad_shift, jnp.sum(grad_branch, axis=0)]
    return grad_values + grad_in, little, grad_upbias, grad_up.astype(BF16), grad_down.astype(BF16)


def head_order(bias):
    return flip(bias, 1, lax.axis_index("hid")).reshape(bias.shape[0], -1)


def body(
    inputs, grid_sizes, cotangent,
    wkernel, wcbias, wgain, wshift, winw, winb, woutw, woutb,
    wgain_two, wshift_two, wupw, wupb, wdownw, wdownb,
    ckernel, ccbias, cgain, cshift, cinw, cinb, coutw, coutb,
    cgain_two, cshift_two, cupw, cupb, cdownw, cdownb,
):
    image_count = inputs.shape[0] // (PADDED * PADDED)
    place = (lax.axis_index("hid") * lax.axis_size("wid") + lax.axis_index("wid")) * image_count
    present = presence(lax.dynamic_slice_in_dim(grid_sizes, place, image_count, 0))
    attention_one = gather_attention(winw, woutw)
    up_two = gather_hidden(wupw)
    down_two = gather_hidden(wdownw)
    attention_three = gather_attention(cinw, coutw)
    up_four = gather_hidden(cupw)
    down_four = gather_hidden(cdownw)

    table = jnp.concatenate([winb, wupb.reshape(4, -1), cinb, cupb.reshape(4, -1)])
    table = gather_bias(table)
    winb = head_order(table[0:2])
    wupb = hidden_order(table[2:6].transpose(1, 0, 2).reshape(4, -1))
    cinb = head_order(table[6:9])
    cupb = hidden_order(table[9:13].transpose(1, 0, 2).reshape(4, -1))

    start = compact(inputs) * present
    after_conv = start + present * depthwise(start, wkernel, wcbias)
    after_attn, saved_one = attention_forward(
        after_conv, present, wgain, wshift, attention_one, winb, woutb, True
    )
    after_mlp, saved_two = mlp_forward(
        after_attn, present, wgain_two, wshift_two, up_two, wupb, down_two, wdownb
    )
    after_conv_c = after_mlp + present * depthwise(after_mlp, ckernel, ccbias)
    after_attn_c, saved_three = attention_forward(
        after_conv_c, present, cgain, cshift, attention_three, cinb, coutb, False
    )
    outputs, saved_four = mlp_forward(
        after_attn_c, present, cgain_two, cshift_two, up_four, cupb, down_four, cdownb
    )

    flowing, little_four, upb_four, gup_four, gdown_four = mlp_backward(
        compact(cotangent), saved_four, present, cgain_two, up_four, down_four
    )
    gdown_four = scatter_hidden(gdown_four)
    gup_four = scatter_hidden(gup_four)
    flowing, little_three, inb_three, gatt_three = attention_backward(
        flowing, saved_three, present, cgain, attention_three, False
    )
    gatt_three = scatter_attention(gatt_three)
    flowing, kernel_three, cbias_three = conv_backward(flowing, after_mlp, ckernel, ccbias, present)
    flowing, little_two, upb_two, gup_two, gdown_two = mlp_backward(
        flowing, saved_two, present, wgain_two, up_two, down_two
    )
    gdown_two = scatter_hidden(gdown_two)
    gup_two = scatter_hidden(gup_two)
    flowing, little_one, inb_one, gatt_one = attention_backward(
        flowing, saved_one, present, wgain, attention_one, True
    )
    gatt_one = scatter_attention(gatt_one)
    flowing, kernel_one, cbias_one = conv_backward(flowing, start, wkernel, wcbias, present)

    def bias_rows(sums):
        rows = jnp.stack(sums).reshape(len(sums), 4, -1)
        return flip(rows, 1, lax.axis_index("hid")).reshape(len(sums), -1)

    early = sum_everywhere(
        jnp.concatenate(
            [kernel_three, jnp.stack([cbias_three] + little_two + little_three + little_four),
             bias_rows(inb_three), hidden_back(upb_two), hidden_back(upb_four)]
        )
    )
    late = sum_everywhere(
        jnp.concatenate([kernel_one, jnp.stack([cbias_one] + little_one), bias_rows(inb_one)])
    )

    def own_hid(rows, axis):
        length = rows.shape[axis] // 4
        return lax.dynamic_slice_in_dim(rows, lax.axis_index("hid") * length, length, axis)

    return (
        expand(outputs), expand(flowing * present),
        late[0:9], late[9], late[10], late[11], gatt_one[:3], own_hid(late[13:15], 1), gatt_one[3], late[12],
        early[10], early[11], gup_two, own_hid(early[22:26], 0).reshape(-1), gdown_two, early[12],
        early[0:9], early[9], early[13], early[14], gatt_three[:3], own_hid(early[19:22], 1), gatt_three[3], early[15],
        early[16], early[17], gup_four, own_hid(early[26:30], 0).reshape(-1), gdown_four, early[18],
    )


def solution(mesh):
    tokens, everywhere = P(("dp", "hid", "wid"), None), P()
    stacked, rows = P(None, ("hid", "wid"), None), P(("hid", "wid"), None)
    block = (
        everywhere, everywhere, everywhere, everywhere, stacked, P(None, "hid"), rows, everywhere,
        everywhere, everywhere, rows, P("hid"), rows, everywhere,
    )
    return jax.shard_map(
        body,
        mesh=mesh,
        in_specs=(tokens, P("dp"), tokens) + block + block,
        out_specs=(tokens, tokens) + block + block,
        check_vma=False,
    )
```

```python
from functools import partial

import jax
import jax.numpy as jnp
from jax import lax
from jax.experimental import pallas as pl
from jax.experimental.pallas import tpu as pltpu
from jax.sharding import PartitionSpec as P

HD = 32
WINDOW = 7
PADDED = 14
GRID = 12
CELLS = GRID * GRID
EPSILON = 1e-05
F32 = jnp.float32
BF16 = jnp.bfloat16
SCALE = HD ** (-0.5)


def exchange(values, axis, bit):
    pairs = [(index, index ^ bit) for index in range(lax.axis_size(axis))]
    return lax.ppermute(values, axis, pairs)


def sibling(values):
    return exchange(values, "dp", 1)


def cross(values, first):
    hids = lax.axis_size("hid")
    pairs = []
    for core in range(lax.axis_size("dp")):
        bit = 1 if (core % 2 == 0) == first else 2
        pairs += [(core * hids + index, core * hids + (index ^ bit)) for index in range(hids)]
    return lax.ppermute(values, ("dp", "hid"), pairs)


def second_core():
    return lax.rem(lax.axis_index("dp"), 2) == 1


def sum_everywhere(values):
    for axis in ("dp", "hid", "wid"):
        bit = 1
        while bit < lax.axis_size(axis):
            values = values + exchange(values, axis, bit)
            bit *= 2
    return values


def by_core(own, other, axis):
    second = second_core()
    return jnp.concatenate(
        [jnp.where(second, other, own), jnp.where(second, own, other)], axis=axis
    )


def half_of(values, axis, mine):
    half = values.shape[axis] // 2
    first = lax.slice_in_dim(values, 0, half, axis=axis)
    last = lax.slice_in_dim(values, half, 2 * half, axis=axis)
    second = second_core()
    return jnp.where(second, last, first) if mine else jnp.where(second, first, last)


def flip(values, axis, by):
    for bit in (1, 2):
        length = values.shape[axis]
        parts = [lax.slice_in_dim(values, i, i + 1, axis=axis) for i in range(length)]
        swapped = jnp.concatenate([parts[i ^ bit] for i in range(length)], axis=axis)
        values = jnp.where((by & bit) != 0, swapped, values)
    return values


def relative_hid(values, axis, second):
    values = flip(values, axis, lax.axis_index("hid"))
    parts = [lax.slice_in_dim(values, i, i + 1, axis=axis) for i in range(4)]
    swapped = jnp.concatenate([parts[0], parts[2], parts[1], parts[3]], axis=axis)
    return jnp.where(second, swapped, values)


def absolute_hid(values, axis, second):
    parts = [lax.slice_in_dim(values, i, i + 1, axis=axis) for i in range(4)]
    swapped = jnp.concatenate([parts[0], parts[2], parts[1], parts[3]], axis=axis)
    return flip(jnp.where(second, swapped, values), axis, lax.axis_index("hid"))


def gather_bias(bias):
    other = exchange(bias, "hid", 1)
    pair = jnp.stack([bias, other], axis=-2)
    both = jnp.concatenate([pair, exchange(pair, "hid", 2)], axis=-2)
    return flip(both, both.ndim - 2, lax.axis_index("hid"))


def hidden_order(bias):
    table = bias.reshape(4, 4, 2, -1)
    table = flip(table, 1, lax.axis_index("wid"))
    second = second_core()
    own = jnp.where(second, table[:, :, 1], table[:, :, 0])
    other = jnp.where(second, table[:, :, 0], table[:, :, 1])
    own = relative_hid(own, 0, second)
    other = relative_hid(other, 0, jnp.logical_not(second))
    return jnp.concatenate([own.reshape(-1), other.reshape(-1)])


def hidden_back(grads):
    table = grads.reshape(2, 4, 4, -1)
    second = second_core()
    own = absolute_hid(table[0], 0, second)
    other = absolute_hid(table[1], 0, jnp.logical_not(second))
    both = jnp.stack([jnp.where(second, other, own), jnp.where(second, own, other)], axis=2)
    return flip(both, 1, lax.axis_index("wid")).reshape(4, -1)


VMEM_LIMIT = 56 * 1024 * 1024
GROUP = 256
HEADS = GROUP // HD


def call(kernel, outs, operands, spaces=(), scratch=(), flops=0, limit=VMEM_LIMIT):
    vmem = pl.BlockSpec(memory_space=pltpu.VMEM)
    specs = [vmem] * len(operands)
    for index, space in spaces:
        specs[index] = pl.BlockSpec(memory_space=space)
    moved = sum(item.size * item.dtype.itemsize for item in list(operands) + list(outs))
    return pl.pallas_call(
        kernel,
        out_shape=list(outs),
        in_specs=specs,
        out_specs=[vmem] * len(outs),
        scratch_shapes=list(scratch),
        compiler_params=pltpu.CompilerParams(vmem_limit_bytes=limit),
        cost_estimate=pl.CostEstimate(flops=flops, bytes_accessed=moved, transcendentals=0),
    )(*operands)


def struct(shape, dtype):
    return jax.ShapeDtypeStruct(shape, dtype)


def mm(left, right):
    return jnp.dot(left, right, preferred_element_type=F32)


def mm_nt(left, right):
    return lax.dot_general(left, right, (((1,), (1,)), ((), ())), preferred_element_type=F32)


def mm_tn(left, right):
    return lax.dot_general(left, right, (((0,), (0,)), ((), ())), preferred_element_type=F32)


def normalize(values):
    center = jnp.mean(values, axis=1, keepdims=True)
    spread = jnp.mean(values * values, axis=1, keepdims=True) - center * center
    scaled = lax.rsqrt(spread + EPSILON)
    return (values - center) * scaled, scaled


def cells_of(rows):
    cell = lax.broadcasted_iota(jnp.int32, (rows, 1), 0)
    column = lax.rem(cell, GRID)
    line = lax.rem(lax.div(cell, GRID), GRID)
    return line, column


def shift_columns(values):
    rows = values.shape[0]
    _, column = cells_of(rows)
    before = jnp.where(column != 0, pltpu.roll(values, 1, 0), 0.0)
    after = jnp.where(column != GRID - 1, pltpu.roll(values, rows - 1, 0), 0.0)
    return before, after


def shift_lines(values, ahead):
    rows = values.shape[0]
    line, _ = cells_of(rows)
    if ahead:
        return jnp.where(line != GRID - 1, pltpu.roll(values, rows - GRID, 0), 0.0)
    return jnp.where(line != 0, pltpu.roll(values, GRID, 0), 0.0)


def convolve(values, taps):
    before, after = shift_columns(values)
    lines = [
        before * taps[3 * a] + values * taps[3 * a + 1] + after * taps[3 * a + 2] for a in range(3)
    ]
    return shift_lines(lines[0], False) + lines[1] + shift_lines(lines[2], True)


LANES = 256


def pack_cells(slots_ref, cells_ref):
    for image in range(cells_ref.shape[0] // CELLS):
        for line in range(GRID):
            cells_ref[pl.ds(image * CELLS + line * GRID, GRID), :] = slots_ref[
                pl.ds((image * PADDED + line) * PADDED, GRID), :
            ]


def unpack_cells(cells_ref, slots_ref):
    slots_ref[...] = jnp.zeros_like(slots_ref)
    for image in range(cells_ref.shape[0] // CELLS):
        for line in range(GRID):
            slots_ref[pl.ds((image * PADDED + line) * PADDED, GRID), :] = cells_ref[
                pl.ds(image * CELLS + line * GRID, GRID), :
            ]


def conv_kernel(values_ref, present_ref, kernel_ref, bias_ref, out_ref):
    present = present_ref[...]
    for lane in range(0, values_ref.shape[1], LANES):
        cut = pl.ds(lane, LANES)
        values = values_ref[:, cut]
        taps = [kernel_ref[pl.ds(i, 1), cut] for i in range(9)]
        out_ref[:, cut] = values + present * (convolve(values, taps) + bias_ref[:, cut])


def first_conv_kernel(slots_ref, present_ref, kernel_ref, bias_ref, start_ref, out_ref):
    pack_cells(slots_ref, start_ref)
    present = present_ref[...]
    for lane in range(0, start_ref.shape[1], LANES):
        cut = pl.ds(lane, LANES)
        values = start_ref[:, cut] * present
        start_ref[:, cut] = values
        taps = [kernel_ref[pl.ds(i, 1), cut] for i in range(9)]
        out_ref[:, cut] = values + present * (convolve(values, taps) + bias_ref[:, cut])


def conv_back_kernel(grads_ref, values_ref, present_ref, kernel_ref, out_ref, sums_ref, *rest):
    present = present_ref[...]
    target = rest[0] if rest else out_ref
    for lane in range(0, grads_ref.shape[1], LANES):
        cut = pl.ds(lane, LANES)
        grads = grads_ref[:, cut]
        masked = grads * present
        taps = [kernel_ref[pl.ds(8 - i, 1), cut] for i in range(9)]
        flowing = grads + convolve(masked, taps)
        target[:, cut] = flowing * present if rest else flowing
        values = values_ref[:, cut]
        before, after = shift_columns(values)
        behind = shift_lines(masked, False)
        ahead = shift_lines(masked, True)
        for a, moved in enumerate((ahead, masked, behind)):
            for e, source in enumerate((before, values, after)):
                sums_ref[pl.ds(3 * a + e, 1), cut] = jnp.sum(moved * source, axis=0, keepdims=True)
        sums_ref[pl.ds(9, 1), cut] = jnp.sum(masked, axis=0, keepdims=True)
    if rest:
        unpack_cells(target, out_ref)


def conv(values, present, kernel, bias):
    return call(conv_kernel, [struct(values.shape, F32)], [values, present, kernel, bias[None]])[0]


def first_conv(slots, present, kernel, bias):
    cells = struct((present.shape[0], slots.shape[1]), F32)
    return call(first_conv_kernel, [cells, cells], [slots, present, kernel, bias[None]])


def conv_back(grads, values, present, kernel, last):
    rows, width = grads.shape
    images = rows // CELLS
    out = struct((images * PADDED * PADDED if last else rows, width), F32)
    scratch = [pltpu.VMEM((rows, width), F32)] if last else []
    return call(
        conv_back_kernel, [out, struct((10, width), F32)], [grads, values, present, kernel], scratch=scratch
    )


UNITS = 768
TILE = 256


def mlp_kernel(
    values_ref, present_ref, gain_ref, shift_ref, upbias_ref, downbias_ref,
    u0, u1, u2, u3, d0, d1, d2, d3,
    *rest,
):
    packed = len(rest) == 6
    out_ref, acted_ref, send_ref, deriv_ref, total_ref = rest[0], rest[1], rest[2], rest[3], rest[4]
    values = values_ref[...]
    normal, _ = normalize(values)
    half = 2 * UNITS
    send_ref[:, half:] = (normal * gain_ref[...] + shift_ref[...]).astype(BF16)
    for index, (up, down) in enumerate(zip((u0, u1, u2, u3), (d0, d1, d2, d3))):
        target = acted_ref if index < 2 else send_ref
        base = (index % 2) * UNITS

        def step(part, _, up=up, target=target, base=base, index=index):
            first = pl.multiple_of(part * TILE, TILE)
            here = pl.ds(pl.multiple_of(index * UNITS + part * TILE, TILE), TILE)
            hidden = mm_nt(send_ref[:, half:], up[pl.ds(first, TILE), :]) + upbias_ref[:, here]
            below = 0.5 + 0.5 * lax.erf(hidden * (0.5**0.5))
            there = pl.ds(pl.multiple_of(base + part * TILE, TILE), TILE)
            target[:, there] = (hidden * below).astype(BF16)
            bell = jnp.exp(hidden * hidden * -0.5) * 0.3989422804014327
            deriv_ref[:, here] = below + hidden * bell
            return 0

        lax.fori_loop(0, UNITS // TILE, step, 0)
        term = mm(target[:, base : base + UNITS], down[...])
        total_ref[...] = term if index == 0 else total_ref[...] + term
    result = values + present_ref[...] * (total_ref[...] + downbias_ref[...])
    if packed:
        rest[5][...] = result
        unpack_cells(rest[5], out_ref)
    else:
        out_ref[...] = result


def mlp(values, present, gain, shift, upbias, downbias, ups, downs, last):
    rows, width = values.shape
    images = rows // CELLS
    half = 2 * UNITS
    outs = [
        struct((images * PADDED * PADDED if last else rows, width), F32),
        struct((rows, half), BF16),
        struct((rows, half + width), BF16),
        struct((rows, 2 * half), F32),
    ]
    scratch = [pltpu.VMEM((rows, width), F32)] * (2 if last else 1)
    operands = [values, present, gain[None], shift[None], upbias[None], downbias[None], *ups, *downs]
    return call(mlp_kernel, outs, operands, scratch=scratch, flops=4 * rows * width * 2 * half)


def norm_back(dn, values, gain, little_ref):
    normal, scaled = normalize(values)
    little_ref[0:1, :] = jnp.sum(dn * normal, axis=0, keepdims=True)
    little_ref[1:2, :] = jnp.sum(dn, axis=0, keepdims=True)
    grad_normal = dn * gain
    first = jnp.mean(grad_normal, axis=1, keepdims=True)
    second = jnp.mean(grad_normal * normal, axis=1, keepdims=True)
    return scaled * (grad_normal - first - normal * second)


def mlp_back_kernel(
    grads_ref, values_ref, present_ref, gain_ref, deriv_ref,
    u0, u1, u2, u3, d0, d1, d2, d3,
    out_ref, hidden_ref, send_ref, little_ref, bias_ref, total_ref, *rest,
):
    half = 2 * UNITS
    if rest:
        pack_cells(grads_ref, rest[0])
        grads_ref = rest[0]
    branch = grads_ref[...] * present_ref[...]
    little_ref[2:3, :] = jnp.sum(branch, axis=0, keepdims=True)
    send_ref[:, half:] = branch.astype(BF16)
    for index, (up, down) in enumerate(zip((u0, u1, u2, u3), (d0, d1, d2, d3))):
        target = hidden_ref if index < 2 else send_ref
        base = (index % 2) * UNITS

        def step(part, _, down=down, target=target, base=base, index=index):
            first = pl.multiple_of(part * TILE, TILE)
            here = pl.ds(pl.multiple_of(index * UNITS + part * TILE, TILE), TILE)
            acted = mm_nt(send_ref[:, half:], down[pl.ds(first, TILE), :])
            hidden = (acted * deriv_ref[:, here]).astype(BF16)
            there = pl.ds(pl.multiple_of(base + part * TILE, TILE), TILE)
            target[:, there] = hidden
            bias_ref[:, here] = jnp.sum(hidden.astype(F32), axis=0, keepdims=True)
            return 0

        lax.fori_loop(0, UNITS // TILE, step, 0)
        term = mm(target[:, base : base + UNITS], up[...])
        total_ref[...] = term if index == 0 else total_ref[...] + term
    grad_in = norm_back(total_ref[...], values_ref[...], gain_ref[...], little_ref)
    out_ref[...] = grads_ref[...] + grad_in


def mlp_back(grads, values, present, gain, deriv, ups, downs):
    rows, width = values.shape
    half = 2 * UNITS
    outs = [
        struct((rows, width), F32),
        struct((rows, half), BF16),
        struct((rows, half + width), BF16),
        struct((3, width), F32),
        struct((1, 2 * half), F32),
    ]
    scratch = [pltpu.VMEM((rows, width), F32)] * (2 if grads.shape[0] != rows else 1)
    operands = [grads, values, present, gain[None], deriv, *ups, *downs]
    return call(mlp_back_kernel, outs, operands, scratch=scratch, flops=4 * rows * width * 2 * half)


def pair_grads_kernel(wide_ref, wide_send_ref, thin_ref, thin_send_ref, near_ref, far_ref):
    half = 2 * UNITS
    for index, out_ref in enumerate((near_ref, far_ref)):
        cut = pl.ds(index * UNITS, UNITS)
        total = mm_tn(wide_ref[:, cut], thin_ref[:, half:])
        total = total + mm_tn(wide_send_ref[:, cut], thin_send_ref[:, half:])
        out_ref[...] = total.astype(BF16)


def pair_grads(wide, wide_send, thin, thin_send):
    width = thin.shape[1] - 2 * UNITS
    out = struct((UNITS, width), BF16)
    flops = 8 * wide.shape[0] * UNITS * width
    return call(pair_grads_kernel, [out, out], [wide, wide_send, thin, thin_send], flops=flops)


MATS = 4


def load_weights(place_ref, parts, weights_ref, sems):
    core, wid = place_ref[0], place_ref[1]
    copies = []
    for index, part in enumerate(parts):
        side = index // 2
        turn = core if side == 0 else 1 - core
        columns = pl.ds(pl.multiple_of(turn * 384, 384), 384)
        for i in range(2):
            line = 2 * (index % 2) + i
            order = line if line in (0, 3) else jnp.where(turn == 1, 3 - line, line)
            for j in range(4):
                first = pl.multiple_of(order * 192 + jnp.bitwise_xor(wid, j) * 48, 16)
                copies.append(
                    pltpu.make_async_copy(
                        part.at[i * 4 + j],
                        weights_ref.at[:, pl.ds(first, 48), columns],
                        sems.at[len(copies)],
                    )
                )
    for copy in copies:
        copy.start()
    return copies


def spread_heads(block):
    lane_head = lax.broadcasted_iota(jnp.int32, (1, GROUP), 1) // HD
    zero = jnp.zeros_like(block)
    return jnp.concatenate([jnp.where(lane_head == h, block, zero) for h in range(HEADS)], axis=0)


def gather_heads(wide):
    lane_head = lax.broadcasted_iota(jnp.int32, (1, GROUP), 1) // HD
    rows = wide.shape[0] // HEADS
    total = jnp.where(lane_head == 0, wide[:rows], 0.0)
    for h in range(1, HEADS):
        total = jnp.where(lane_head == h, wide[h * rows : (h + 1) * rows], total)
    return total


def window_probabilities(queries, keys, mask):
    scores = mm_nt(queries, keys) * SCALE
    scores = scores.reshape(HEADS, CELLS, CELLS)
    scores = jnp.where(mask[None] > 0.5, scores, -1000000000.0)
    raised = jnp.exp(scores - jnp.max(scores, axis=-1, keepdims=True))
    return raised * (1.0 / jnp.sum(raised, axis=-1, keepdims=True))


def channel_probabilities(keys, values):
    scores = mm_tn(keys, values) * SCALE
    line = lax.broadcasted_iota(jnp.int32, (GROUP, GROUP), 0) // HD
    column = lax.broadcasted_iota(jnp.int32, (GROUP, GROUP), 1) // HD
    scores = jnp.where(line == column, scores, -jnp.inf)
    raised = jnp.exp(scores - jnp.max(scores, axis=-1, keepdims=True))
    return raised * (1.0 / jnp.sum(raised, axis=-1, keepdims=True))


def unit_cuts(unit, width):
    groups = width // GROUP
    image = unit // groups
    rows = pl.ds(pl.multiple_of(image * CELLS, 16), CELLS)
    lane = pl.multiple_of(lax.rem(unit, groups) * GROUP, GROUP)
    return rows, lane


def attention_kernel(
    windowed, place_ref, values_ref, present_ref, mask_ref, gain_ref, shift_ref, bias_ref, outbias_ref,
    p0, p1, p2, p3, out_ref, normed_ref, qkv_ref, mixed_ref, weights_ref, sems,
):
    copies = load_weights(place_ref, (p0, p1, p2, p3), weights_ref, sems)
    rows_all, width = values_ref.shape
    normal, _ = normalize(values_ref[...])
    normed_ref[...] = (normal * gain_ref[...] + shift_ref[...]).astype(BF16)
    for copy in copies:
        copy.wait()
    for m in range(3):
        projected = mm_nt(normed_ref[...], weights_ref[m]) + bias_ref[m : m + 1, :]
        qkv_ref[:, m * width : (m + 1) * width] = projected.astype(BF16)

    def step(unit, _):
        rows, lane = unit_cuts(unit, width)
        queries = qkv_ref[rows, pl.ds(lane, GROUP)]
        keys = qkv_ref[rows, pl.ds(lane + width, GROUP)]
        values = qkv_ref[rows, pl.ds(lane + 2 * width, GROUP)]
        if windowed:
            probs = window_probabilities(spread_heads(queries), keys, mask_ref[rows, :])
            weights = probs.reshape(HEADS * CELLS, CELLS).astype(BF16)
            mixed = gather_heads(mm(weights, values))
        else:
            kept = keys * present_ref[rows, :].astype(BF16)
            weights = channel_probabilities(kept, values).astype(BF16)
            mixed = mm_nt(queries, weights)
        mixed_ref[rows, pl.ds(lane, GROUP)] = mixed.astype(BF16)
        return 0

    lax.fori_loop(0, rows_all // CELLS * (width // GROUP), step, 0)
    branch = mm(mixed_ref[...], weights_ref[3]) + outbias_ref[...]
    out_ref[...] = values_ref[...] + present_ref[...] * branch


def attention(windowed, place, values, present, mask, gain, shift, bias, outbias, parts):
    rows, width = values.shape
    outs = [
        struct((rows, width), F32),
        struct((rows, width), BF16),
        struct((rows, 3 * width), BF16),
        struct((rows, width), BF16),
    ]
    operands = [place, values, present, mask, gain[None], shift[None], bias, outbias[None], *parts]
    spaces = [(0, pltpu.SMEM)] + [(8 + i, pl.ANY) for i in range(4)]
    scratch = [pltpu.VMEM((MATS, width, width), BF16), pltpu.SemaphoreType.DMA((32,))]
    return call(
        partial(attention_kernel, windowed), outs, operands, spaces=spaces, scratch=scratch,
        flops=8 * rows * width * width,
    )


def attention_back_kernel(
    windowed, place_ref, grads_ref, values_ref, present_ref, mask_ref, gain_ref, normed_ref, qkv_ref, mixed_ref,
    p0, p1, p2, p3, out_ref, left_ref, mine_ref, theirs_ref, little_ref, bias_ref,
    weights_ref, low_ref, mix_ref, sems,
):
    copies = load_weights(place_ref, (p0, p1, p2, p3), weights_ref, sems)
    rows_all, width = values_ref.shape
    half = width // 2
    core = place_ref[0]
    own = pl.ds(pl.multiple_of(core * half, half), half)
    other = pl.ds(pl.multiple_of((1 - core) * half, half), half)
    branch = grads_ref[...] * present_ref[...]
    little_ref[2:3, :] = jnp.sum(branch, axis=0, keepdims=True)
    low_ref[...] = branch.astype(BF16)
    mine_ref[:, :half] = normed_ref[:, own]
    mine_ref[:, half:] = low_ref[:, own]
    theirs_ref[:, :half] = normed_ref[:, other]
    theirs_ref[:, half:] = low_ref[:, other]
    left_ref[:, 3 * width :] = mixed_ref[...]
    for copy in copies:
        copy.wait()
    mix_ref[...] = mm_nt(low_ref[...], weights_ref[3]).astype(BF16)

    def step(unit, _):
        rows, lane = unit_cuts(unit, width)
        queries = qkv_ref[rows, pl.ds(lane, GROUP)]
        keys = qkv_ref[rows, pl.ds(lane + width, GROUP)]
        values = qkv_ref[rows, pl.ds(lane + 2 * width, GROUP)]
        incoming = mix_ref[rows, pl.ds(lane, GROUP)]
        if windowed:
            mask = mask_ref[rows, :]
            wide_queries = spread_heads(queries)
            wide_incoming = spread_heads(incoming)
            probs = window_probabilities(wide_queries, keys, mask)
            weights = probs.reshape(HEADS * CELLS, CELLS).astype(BF16)
            grad_probs = mm_nt(wide_incoming, values).reshape(HEADS, CELLS, CELLS)
            inner = jnp.sum(probs * grad_probs, axis=-1, keepdims=True)
            grad_scores = jnp.where(mask[None] > 0.5, probs * (grad_probs - inner), 0.0)
            grad_scores = grad_scores.reshape(HEADS * CELLS, CELLS).astype(BF16)
            grad_query = gather_heads(mm(grad_scores, keys)) * SCALE
            grad_keys = mm_tn(grad_scores, wide_queries) * SCALE
            grad_values = mm_tn(weights, wide_incoming)
        else:
            present = present_ref[rows, :]
            kept = keys * present.astype(BF16)
            probs = channel_probabilities(kept, values)
            grad_probs = mm_tn(incoming, queries)
            inner = jnp.sum(probs * grad_probs, axis=-1, keepdims=True)
            grad_scores = (probs * (grad_probs - inner)).astype(BF16)
            grad_query = mm(incoming, probs.astype(BF16))
            grad_keys = mm_nt(values, grad_scores) * SCALE * present
            grad_values = mm(kept, grad_scores) * SCALE
        for m, item in enumerate((grad_query, grad_keys, grad_values)):
            left_ref[rows, pl.ds(lane + m * width, GROUP)] = item.astype(BF16)
        return 0

    lax.fori_loop(0, rows_all // CELLS * (width // GROUP), step, 0)
    total = None
    for m in range(3):
        rounded = left_ref[:, m * width : (m + 1) * width]
        bias_ref[m : m + 1, :] = jnp.sum(rounded.astype(F32), axis=0, keepdims=True)
        term = mm(rounded, weights_ref[m])
        total = term if total is None else total + term
    out_ref[...] = grads_ref[...] + norm_back(total, values_ref[...], gain_ref[...], little_ref)


def attention_back(windowed, place, grads, values, present, mask, gain, normed, qkv, mixed, parts):
    rows, width = values.shape
    outs = [
        struct((rows, width), F32),
        struct((rows, 4 * width), BF16),
        struct((rows, width), BF16),
        struct((rows, width), BF16),
        struct((3, width), F32),
        struct((3, width), F32),
    ]
    operands = [place, grads, values, present, mask, gain[None], normed, qkv, mixed, *parts]
    spaces = [(0, pltpu.SMEM)] + [(9 + i, pl.ANY) for i in range(4)]
    scratch = [
        pltpu.VMEM((MATS, width, width), BF16),
        pltpu.VMEM((rows, width), BF16),
        pltpu.VMEM((rows, width), BF16),
        pltpu.SemaphoreType.DMA((32,)),
    ]
    return call(
        partial(attention_back_kernel, windowed), outs, operands, spaces=spaces, scratch=scratch,
        flops=10 * rows * width * width,
    )


def head_grads_kernel(place_ref, left_ref, left_send_ref, right_ref, right_send_ref, near_ref, far_ref, table_ref):
    core, wid = place_ref[0], place_ref[1]
    width = left_ref.shape[1] // MATS
    half = width // 2
    for m in range(MATS):
        cut = slice(m * width, (m + 1) * width)
        side = slice(0, half) if m < 3 else slice(half, width)
        table_ref[...] = mm_tn(left_ref[:, cut], right_ref[:, side])
        table_ref[...] = table_ref[...] + mm_tn(left_send_ref[:, cut], right_send_ref[:, side])
        for line in range(4):
            order = line if line in (0, 3) else jnp.where(core == 1, 3 - line, line)
            out_ref = near_ref if line < 2 else far_ref
            for j in range(4):
                first = pl.multiple_of(order * 192 + jnp.bitwise_xor(wid, j) * 48, 16)
                out_ref[(line % 2) * 4 + j, m] = table_ref[pl.ds(first, 48), :].astype(BF16)


def head_grads(place, left, left_send, right, right_send):
    width = right.shape[1]
    out = struct((8, MATS, width // 16, width // 2), BF16)
    return call(
        head_grads_kernel, [out, out], [place, left, left_send, right, right_send],
        spaces=[(0, pltpu.SMEM)], scratch=[pltpu.VMEM((width, width // 2), F32)],
        flops=8 * left.shape[0] * width * width,
    )


class Line:
    def __init__(self, mark):
        self.mark = mark

    def gate(self, tree):
        tree, self.mark = lax.optimization_barrier((tree, self.mark))
        return tree

    def run(self, function, *operands):
        return self.gate(function(*self.gate(operands)))


class Gather:
    def __init__(self, line, piece):
        self.line, self.near, self.step, self.flight = line, piece[None], 0, ()

    def advance(self):
        gate = self.line.gate
        if self.step in (1, 2, 3):
            arrived = gate(self.flight[0])
            self.near = jnp.concatenate([self.near, arrived], axis=0)
        elif self.step == 4:
            self.far, self.other_near = gate(self.flight)
        elif self.step == 5:
            self.other_far = gate(self.flight[0])
        if self.step < 4:
            self.near = gate(self.near)
        if self.step == 0:
            self.flight = (exchange(self.near, "wid", 1),)
        elif self.step == 1:
            self.flight = (exchange(self.near, "wid", 2),)
        elif self.step == 2:
            self.flight = (cross(self.near, True),)
        elif self.step == 3:
            self.flight = (cross(self.near, False), sibling(self.near))
        elif self.step == 4:
            self.far = gate(self.far)
            self.flight = (sibling(self.far),)
        self.step += 1

    def parts(self):
        return [self.near, self.far, self.other_near, self.other_far]

    def rows(self):
        return [part.reshape(-1, part.shape[-1]) for part in self.parts()]


class Scatter:
    def __init__(self, line, near, far, axis):
        self.line, self.kept, self.sent, self.axis, self.step = line, near, far, axis, 0

    def advance(self):
        gate = self.line.gate
        if self.step in (1, 2, 3):
            arrived = gate(self.flight)
            half = arrived.shape[0] // 2
            self.sent = (self.kept[half:].astype(F32) + arrived[half:].astype(F32)).astype(BF16)
            self.kept = self.kept[:half].astype(F32) + arrived[:half].astype(F32)
        elif self.step == 4:
            total = self.kept[0] + gate(self.flight)[0].astype(F32)
            bit = 2
            while bit < lax.axis_size("dp"):
                total = total + exchange(total, "dp", bit)
                bit *= 2
            self.kept = total
        elif self.step == 5:
            self.total = by_core(self.kept, gate(self.flight), self.axis)
        if self.step < 4:
            self.sent = gate(self.sent)
        if self.step == 0:
            self.flight = cross(self.sent, False)
        elif self.step == 1:
            self.flight = cross(self.sent, True)
        elif self.step == 2:
            self.flight = exchange(self.sent, "wid", 2)
        elif self.step == 3:
            self.flight = exchange(self.sent, "wid", 1)
        elif self.step == 4:
            self.flight = sibling(gate(self.kept))
        self.step += 1


def presence(sizes):
    cells = jnp.arange(GRID, dtype=jnp.int32)
    inside = (cells[None, :, None] < sizes[:, None, None]) & (
        cells[None, None, :] < sizes[:, None, None]
    )
    return inside.astype(F32).reshape(-1, 1)


def window_mask(present):
    cell = jnp.arange(CELLS, dtype=jnp.int32)
    window = (cell // GRID // WINDOW) * 2 + cell % GRID // WINDOW
    same = window[:, None] == window[None, :]
    return (same[None] & (present.reshape(-1, 1, CELLS) > 0.5)).astype(F32).reshape(-1, CELLS)


def head_order(bias):
    return flip(bias, 1, lax.axis_index("hid")).reshape(bias.shape[0], -1)


def attention_piece(inweights, outweights):
    return half_of(jnp.concatenate([inweights, outweights[None]], axis=0), 2, True)


def body(
    inputs, grid_sizes, cotangent,
    wkernel, wcbias, wgain, wshift, winw, winb, woutw, woutb,
    wgain_two, wshift_two, wupw, wupb, wdownw, wdownb,
    ckernel, ccbias, cgain, cshift, cinw, cinb, coutw, coutb,
    cgain_two, cshift_two, cupw, cupb, cdownw, cdownb,
):
    image_count = inputs.shape[0] // (PADDED * PADDED)
    wid = lax.axis_index("wid")
    own_place = (lax.axis_index("hid") * lax.axis_size("wid") + wid) * image_count
    present = presence(lax.dynamic_slice_in_dim(grid_sizes, own_place, image_count, 0))
    mask = window_mask(present)
    place = jnp.stack([lax.rem(lax.axis_index("dp"), 2), wid]).astype(jnp.int32)
    line = Line(winb[0, 0])

    groups = [
        Gather(line, piece)
        for piece in (
            attention_piece(winw, woutw), half_of(wupw, 0, True), half_of(wdownw, 0, True),
            attention_piece(cinw, coutw), half_of(cupw, 0, True), half_of(cdownw, 0, True),
        )
    ]
    done = 0

    def gather_step():
        nonlocal done
        for index, group in enumerate(groups):
            if index <= done and done - index < 6:
                group.advance()
        done += 1

    table = jnp.concatenate([winb, wupb.reshape(4, -1), cinb, cupb.reshape(4, -1)])
    table = gather_bias(table)
    winb = head_order(table[0:2])
    winb = jnp.stack([winb[0], jnp.zeros_like(winb[0]), winb[1]])
    wupb = hidden_order(table[2:6].transpose(1, 0, 2).reshape(4, -1))
    cinb = head_order(table[6:9])
    cupb = hidden_order(table[9:13].transpose(1, 0, 2).reshape(4, -1))

    gather_step()
    start, after_conv = line.run(first_conv, inputs, present, wkernel, wcbias)
    for _ in range(5):
        gather_step()
    att_one = groups[0].parts()
    after_attn, normed_one, qkv_one, mixed_one = line.run(
        partial(attention, True), place, after_conv, present, mask, wgain, wshift, winb, woutb, att_one
    )
    gather_step()
    gather_step()
    ups_two, downs_two = groups[1].rows(), groups[2].rows()
    after_mlp, acted_two, fpack_two, deriv_two = line.run(
        partial(mlp, last=False),
        after_attn, present, wgain_two, wshift_two, wupb, wdownb, ups_two, downs_two,
    )
    fpack_two_other = sibling(fpack_two)
    gather_step()
    after_conv_c = line.run(conv, after_mlp, present, ckernel, ccbias)
    att_three = groups[3].parts()
    after_attn_c, normed_three, qkv_three, mixed_three = line.run(
        partial(attention, False), place, after_conv_c, present, mask, cgain, cshift, cinb, coutb, att_three
    )
    gather_step()
    fpack_two_other = line.gate(fpack_two_other)
    gather_step()
    ups_four, downs_four = groups[4].rows(), groups[5].rows()
    outputs, acted_four, fpack_four, deriv_four = line.run(
        partial(mlp, last=True),
        after_attn_c, present, cgain_two, cshift_two, cupb, cdownb, ups_four, downs_four,
    )

    fpack_four_other = sibling(fpack_four)
    flowing, gh_four, bpack_four, little_four, upb_four = line.run(
        mlp_back, cotangent, after_attn_c, present, cgain_two, deriv_four, ups_four, downs_four
    )
    bpack_four_other = sibling(bpack_four)
    fpack_four_other, bpack_four_other = line.gate((fpack_four_other, bpack_four_other))

    def mlp_scatter(wide, wide_send, thin, thin_send):
        near, far = line.run(pair_grads, wide, wide_send, thin, thin_send)
        group = Scatter(line, near.reshape(8, -1, near.shape[1]), far.reshape(8, -1, far.shape[1]), 0)
        group.advance()
        return group

    d_four = mlp_scatter(acted_four, fpack_four_other, bpack_four, bpack_four_other)
    u_four = mlp_scatter(gh_four, bpack_four_other, fpack_four, fpack_four_other)
    flowing, left_three, mine_three, theirs_three, little_three, inb_three = line.run(
        partial(attention_back, False),
        place, flowing, after_conv_c, present, mask, cgain, normed_three, qkv_three, mixed_three, att_three,
    )
    sent_three = sibling(left_three), sibling(theirs_three)
    d_four.advance()
    u_four.advance()
    sent_three = line.gate(sent_three)
    a_three = Scatter(line, *line.run(head_grads, place, left_three, sent_three[0], mine_three, sent_three[1]), 2)
    a_three.advance()
    d_four.advance()
    flowing, sums_three = line.run(
        partial(conv_back, last=False), flowing, after_mlp, present, ckernel
    )
    u_four.advance()
    flowing, gh_two, bpack_two, little_two, upb_two = line.run(
        mlp_back, flowing, after_attn, present, wgain_two, deriv_two, ups_two, downs_two
    )
    bpack_two_other = sibling(bpack_two)
    d_four.advance()
    a_three.advance()
    bpack_two_other = line.gate(bpack_two_other)
    d_two = mlp_scatter(acted_two, fpack_two_other, bpack_two, bpack_two_other)
    u_two = mlp_scatter(gh_two, bpack_two_other, fpack_two, fpack_two_other)
    u_four.advance()
    a_three.advance()
    d_four.advance()
    flowing, left_one, mine_one, theirs_one, little_one, inb_one = line.run(
        partial(attention_back, True),
        place, flowing, after_conv, present, mask, wgain, normed_one, qkv_one, mixed_one, att_one,
    )
    sent_one = sibling(left_one), sibling(theirs_one)
    d_two.advance()
    u_two.advance()
    sent_one = line.gate(sent_one)
    a_one = Scatter(line, *line.run(head_grads, place, left_one, sent_one[0], mine_one, sent_one[1]), 2)
    a_one.advance()
    u_four.advance()
    a_three.advance()
    d_four.advance()
    input_grad, sums_one = line.run(partial(conv_back, last=True), flowing, start, present, wkernel)
    d_two.advance()
    u_two.advance()
    u_four.advance()
    a_three.advance()

    def bias_rows(rows):
        rows = rows.reshape(rows.shape[0], 4, -1)
        return flip(rows, 1, lax.axis_index("hid")).reshape(rows.shape[0], -1)

    early = jnp.concatenate(
        [sums_three, little_two, little_three, little_four,
         bias_rows(inb_three), hidden_back(upb_two), hidden_back(upb_four)]
    )
    late = jnp.concatenate([sums_one, little_one, bias_rows(inb_one)])
    small = sum_everywhere(jnp.concatenate([early, late]))
    early, late = small[:30], small[30:]
    a_one.advance()
    d_two.advance()
    u_two.advance()
    a_three.advance()
    a_one.advance()
    d_two.advance()
    u_two.advance()
    a_one.advance()
    d_two.advance()
    u_two.advance()
    a_one.advance()
    a_one.advance()

    def own_hid(rows, axis):
        length = rows.shape[axis] // 4
        return lax.dynamic_slice_in_dim(rows, lax.axis_index("hid") * length, length, axis)

    for group in (d_two, u_two, a_one, d_four, u_four, a_three):
        while group.step < 6:
            group.advance()
    gatt_one, gatt_three = a_one.total, a_three.total
    return (
        outputs, input_grad,
        late[0:9], late[9], late[10], late[11], gatt_one[:3], own_hid(late[13:16:2], 1), gatt_one[3], late[12],
        early[10], early[11], u_two.total, own_hid(early[22:26], 0).reshape(-1), d_two.total, early[12],
        early[0:9], early[9], early[13], early[14], gatt_three[:3], own_hid(early[19:22], 1), gatt_three[3], early[15],
        early[16], early[17], u_four.total, own_hid(early[26:30], 0).reshape(-1), d_four.total, early[18],
    )


def solution(mesh):
    tokens, everywhere = P(("dp", "hid", "wid"), None), P()
    stacked, rows = P(None, ("hid", "wid"), None), P(("hid", "wid"), None)
    block = (
        everywhere, everywhere, everywhere, everywhere, stacked, P(None, "hid"), rows, everywhere,
        everywhere, everywhere, rows, P("hid"), rows, everywhere,
    )
    return jax.shard_map(
        body,
        mesh=mesh,
        in_specs=(tokens, P("dp"), tokens) + block + block,
        out_specs=(tokens, tokens) + block + block,
        check_vma=False,
    )
```

```python
from functools import partial

import jax
import jax.numpy as jnp
from jax import lax
from jax.experimental import pallas as pl
from jax.experimental.pallas import tpu as pltpu
from jax.sharding import PartitionSpec as P

HD = 32
WINDOW = 7
PADDED = 14
GRID = 12
CELLS = GRID * GRID
EPSILON = 1e-05
F32 = jnp.float32
BF16 = jnp.bfloat16
SCALE = HD ** (-0.5)


def exchange(values, axis, bit):
    pairs = [(index, index ^ bit) for index in range(lax.axis_size(axis))]
    return lax.ppermute(values, axis, pairs)


def sibling(values):
    return exchange(values, "dp", 1)


def cross(values, first):
    hids = lax.axis_size("hid")
    pairs = []
    for core in range(lax.axis_size("dp")):
        bit = 1 if (core % 2 == 0) == first else 2
        pairs += [(core * hids + index, core * hids + (index ^ bit)) for index in range(hids)]
    return lax.ppermute(values, ("dp", "hid"), pairs)


def second_core():
    return lax.rem(lax.axis_index("dp"), 2) == 1


def by_core(own, other, axis):
    second = second_core()
    return jnp.concatenate(
        [jnp.where(second, other, own), jnp.where(second, own, other)], axis=axis
    )


VMEM_LIMIT = 56 * 1024 * 1024
GROUP = 256
HEADS = GROUP // HD


def call(kernel, outs, operands, spaces=(), scratch=(), flops=0, limit=VMEM_LIMIT):
    vmem = pl.BlockSpec(memory_space=pltpu.VMEM)
    specs = [vmem] * len(operands)
    for index, space in spaces:
        specs[index] = pl.BlockSpec(memory_space=space)
    moved = sum(item.size * item.dtype.itemsize for item in list(operands) + list(outs))
    return pl.pallas_call(
        kernel,
        out_shape=list(outs),
        in_specs=specs,
        out_specs=[vmem] * len(outs),
        scratch_shapes=list(scratch),
        compiler_params=pltpu.CompilerParams(vmem_limit_bytes=limit),
        cost_estimate=pl.CostEstimate(flops=1, bytes_accessed=1, transcendentals=0),
    )(*operands)


def struct(shape, dtype):
    return jax.ShapeDtypeStruct(shape, dtype)


def mm(left, right):
    return jnp.dot(left, right, preferred_element_type=F32)


def mm_nt(left, right):
    return lax.dot_general(left, right, (((1,), (1,)), ((), ())), preferred_element_type=F32)


def mm_tn(left, right):
    return lax.dot_general(left, right, (((0,), (0,)), ((), ())), preferred_element_type=F32)


def normalize(values):
    center = jnp.mean(values, axis=1, keepdims=True)
    spread = jnp.mean(values * values, axis=1, keepdims=True) - center * center
    scaled = lax.rsqrt(spread + EPSILON)
    return (values - center) * scaled, scaled


def cells_of(rows):
    cell = lax.broadcasted_iota(jnp.int32, (rows, 1), 0)
    column = lax.rem(cell, GRID)
    line = lax.rem(lax.div(cell, GRID), GRID)
    return line, column


def shift_columns(values):
    rows = values.shape[0]
    _, column = cells_of(rows)
    before = jnp.where(column != 0, pltpu.roll(values, 1, 0), 0.0)
    after = jnp.where(column != GRID - 1, pltpu.roll(values, rows - 1, 0), 0.0)
    return before, after


def shift_lines(values, ahead):
    rows = values.shape[0]
    line, _ = cells_of(rows)
    if ahead:
        return jnp.where(line != GRID - 1, pltpu.roll(values, rows - GRID, 0), 0.0)
    return jnp.where(line != 0, pltpu.roll(values, GRID, 0), 0.0)


def convolve(values, taps):
    before, after = shift_columns(values)
    lines = [
        before * taps[3 * a] + values * taps[3 * a + 1] + after * taps[3 * a + 2] for a in range(3)
    ]
    return shift_lines(lines[0], False) + lines[1] + shift_lines(lines[2], True)


def presence(place_ref, rows, image=None):
    line, column = cells_of(rows)
    if image is not None:
        side = place_ref[3 + image]
    else:
        cell = lax.broadcasted_iota(jnp.int32, (rows, 1), 0)
        side = jnp.zeros((rows, 1), jnp.int32) + place_ref[3]
        for index in range(1, rows // CELLS):
            side = jnp.where(cell >= index * CELLS, place_ref[3 + index], side)
    return jnp.where((line < side) & (column < side), 1.0, 0.0).astype(F32)


def window_mask(place_ref, image):
    side = place_ref[3 + image]
    query = lax.broadcasted_iota(jnp.int32, (CELLS, 1), 0)
    key = lax.broadcasted_iota(jnp.int32, (1, CELLS), 1)
    line, column = lax.div(key, GRID), lax.rem(key, GRID)
    kept = (line < side) & (column < side)

    def window(cell):
        below = lax.div(cell, GRID) >= WINDOW
        right = lax.rem(cell, GRID) >= WINDOW
        return jnp.where(below, 2, 0) + jnp.where(right, 1, 0)

    own = jnp.where(kept, window(key), -1)
    return window(query) == own


LANES = 256


def pack_cells(slots_ref, cells_ref):
    for image in range(cells_ref.shape[0] // CELLS):
        for line in range(GRID):
            cells_ref[pl.ds(image * CELLS + line * GRID, GRID), :] = slots_ref[
                pl.ds((image * PADDED + line) * PADDED, GRID), :
            ]


def unpack_cells(cells_ref, slots_ref):
    slots_ref[...] = jnp.zeros_like(slots_ref)
    for image in range(cells_ref.shape[0] // CELLS):
        for line in range(GRID):
            slots_ref[pl.ds((image * PADDED + line) * PADDED, GRID), :] = cells_ref[
                pl.ds(image * CELLS + line * GRID, GRID), :
            ]


def conv_lanes(values, present, table_ref, base, cut):
    taps = [table_ref[pl.ds(base + i, 1), cut] for i in range(9)]
    return values + present * (convolve(values, taps) + table_ref[pl.ds(base + 9, 1), cut])


def conv_kernel(base, place_ref, values_ref, table_ref, out_ref):
    present = presence(place_ref, values_ref.shape[0])
    for lane in range(0, values_ref.shape[1], LANES):
        cut = pl.ds(lane, LANES)
        out_ref[:, cut] = conv_lanes(values_ref[:, cut], present, table_ref, base, cut)


def first_conv_kernel(base, place_ref, slots_ref, table_ref, start_ref, out_ref):
    pack_cells(slots_ref, start_ref)
    present = presence(place_ref, start_ref.shape[0])
    for lane in range(0, start_ref.shape[1], LANES):
        cut = pl.ds(lane, LANES)
        values = start_ref[:, cut] * present
        start_ref[:, cut] = values
        out_ref[:, cut] = conv_lanes(values, present, table_ref, base, cut)


def conv_back_kernel(base, place_ref, grads_ref, values_ref, table_ref, out_ref, sums_ref, *rest):
    present = presence(place_ref, grads_ref.shape[0])
    target = rest[0] if rest else out_ref
    for lane in range(0, grads_ref.shape[1], LANES):
        cut = pl.ds(lane, LANES)
        grads = grads_ref[:, cut]
        masked = grads * present
        taps = [table_ref[pl.ds(base + 8 - i, 1), cut] for i in range(9)]
        flowing = grads + convolve(masked, taps)
        target[:, cut] = flowing * present if rest else flowing
        values = values_ref[:, cut]
        before, after = shift_columns(values)
        behind = shift_lines(masked, False)
        ahead = shift_lines(masked, True)
        for a, moved in enumerate((ahead, masked, behind)):
            for e, source in enumerate((before, values, after)):
                sums_ref[pl.ds(3 * a + e, 1), cut] = jnp.sum(moved * source, axis=0, keepdims=True)
        sums_ref[pl.ds(9, 1), cut] = jnp.sum(masked, axis=0, keepdims=True)
    if rest:
        unpack_cells(target, out_ref)


SMALL = [(0, pltpu.SMEM)]


def conv(base, place, values, table):
    return call(partial(conv_kernel, base), [struct(values.shape, F32)], [place, values, table], SMALL)[0]


def first_conv(base, place, slots, table):
    cells = struct((slots.shape[0] // (PADDED * PADDED) * CELLS, slots.shape[1]), F32)
    return call(partial(first_conv_kernel, base), [cells, cells], [place, slots, table], SMALL)


def conv_back(base, last, place, grads, values, table):
    rows, width = grads.shape
    images = rows // CELLS
    out = struct((images * PADDED * PADDED if last else rows, width), F32)
    scratch = [pltpu.VMEM((rows, width), F32)] if last else []
    return call(
        partial(conv_back_kernel, base), [out, struct((10, width), F32)], [place, grads, values, table],
        SMALL, scratch=scratch,
    )


def low_kernel(place_ref, slots_ref, cells_ref, low_ref):
    pack_cells(slots_ref, cells_ref)
    low_ref[...] = (cells_ref[...] * presence(place_ref, cells_ref.shape[0])).astype(BF16)


def low_cells(place, slots):
    shape = (slots.shape[0] // (PADDED * PADDED) * CELLS, slots.shape[1])
    return call(low_kernel, [struct(shape, F32), struct(shape, BF16)], [place, slots], SMALL)


UNITS = 768
TILE = 256


def mlp_kernel(
    base_row, place_ref, values_ref, table_ref, upbias_ref,
    u0, u1, u2, u3, d0, d1, d2, d3,
    *rest,
):
    packed = len(rest) == 6
    gain, shift, downbias = (table_ref[pl.ds(base_row + i, 1), :] for i in (13, 14, 15))
    ubias = 0 if base_row == 0 else 1
    out_ref, acted_ref, send_ref, deriv_ref, total_ref = rest[0], rest[1], rest[2], rest[3], rest[4]
    values = values_ref[...]
    normal, _ = normalize(values)
    half = 2 * UNITS
    send_ref[:, half:] = (normal * gain + shift).astype(BF16)
    for index, (up, down) in enumerate(zip((u0, u1, u2, u3), (d0, d1, d2, d3))):
        target = acted_ref if index < 2 else send_ref
        base = (index % 2) * UNITS

        def step(part, _, up=up, target=target, base=base, index=index):
            first = pl.multiple_of(part * TILE, TILE)
            here = pl.ds(pl.multiple_of(index * UNITS + part * TILE, TILE), TILE)
            hidden = mm_nt(send_ref[:, half:], up[pl.ds(first, TILE), :]) + upbias_ref[ubias : ubias + 1, here]
            below = 0.5 + 0.5 * lax.erf(hidden * (0.5**0.5))
            there = pl.ds(pl.multiple_of(base + part * TILE, TILE), TILE)
            target[:, there] = (hidden * below).astype(BF16)
            bell = jnp.exp(hidden * hidden * -0.5) * 0.3989422804014327
            deriv_ref[:, here] = below + hidden * bell
            return 0

        lax.fori_loop(0, UNITS // TILE, step, 0)
        term = mm(target[:, base : base + UNITS], down[...])
        total_ref[...] = term if index == 0 else total_ref[...] + term
    result = values + presence(place_ref, values.shape[0]) * (total_ref[...] + downbias)
    if packed:
        rest[5][...] = result
        unpack_cells(rest[5], out_ref)
    else:
        out_ref[...] = result


def mlp(base, last, place, values, table, upbias, ups, downs):
    rows, width = values.shape
    images = rows // CELLS
    half = 2 * UNITS
    outs = [
        struct((images * PADDED * PADDED if last else rows, width), F32),
        struct((rows, half), BF16),
        struct((rows, half + width), BF16),
        struct((rows, 2 * half), F32),
    ]
    scratch = [pltpu.VMEM((rows, width), F32)] * (2 if last else 1)
    operands = [place, values, table, upbias, *ups, *downs]
    flops = 4 * rows * width * 2 * half
    return call(partial(mlp_kernel, base), outs, operands, SMALL, scratch=scratch, flops=flops)


def norm_back(dn, values, gain, little_ref):
    normal, scaled = normalize(values)
    little_ref[0:1, :] = jnp.sum(dn * normal, axis=0, keepdims=True)
    little_ref[1:2, :] = jnp.sum(dn, axis=0, keepdims=True)
    grad_normal = dn * gain
    first = jnp.mean(grad_normal, axis=1, keepdims=True)
    second = jnp.mean(grad_normal * normal, axis=1, keepdims=True)
    return scaled * (grad_normal - first - normal * second)


def mlp_back_kernel(
    base_row, place_ref, grads_ref, values_ref, table_ref, deriv_ref,
    u0, u1, u2, u3, d0, d1, d2, d3,
    out_ref, hidden_ref, send_ref, little_ref, bias_ref, total_ref,
):
    half = 2 * UNITS
    branch = grads_ref[...] * presence(place_ref, grads_ref.shape[0])
    little_ref[2:3, :] = jnp.sum(branch, axis=0, keepdims=True)
    send_ref[:, half:] = branch.astype(BF16)
    for index, (up, down) in enumerate(zip((u0, u1, u2, u3), (d0, d1, d2, d3))):
        target = hidden_ref if index < 2 else send_ref
        base = (index % 2) * UNITS

        def step(part, _, down=down, target=target, base=base, index=index):
            first = pl.multiple_of(part * TILE, TILE)
            here = pl.ds(pl.multiple_of(index * UNITS + part * TILE, TILE), TILE)
            acted = mm_nt(send_ref[:, half:], down[pl.ds(first, TILE), :])
            hidden = (acted * deriv_ref[:, here]).astype(BF16)
            there = pl.ds(pl.multiple_of(base + part * TILE, TILE), TILE)
            target[:, there] = hidden
            bias_ref[:, here] = jnp.sum(hidden.astype(F32), axis=0, keepdims=True)
            return 0

        lax.fori_loop(0, UNITS // TILE, step, 0)
        term = mm(target[:, base : base + UNITS], up[...])
        total_ref[...] = term if index == 0 else total_ref[...] + term
    gain = table_ref[pl.ds(base_row + 13, 1), :]
    out_ref[...] = grads_ref[...] + norm_back(total_ref[...], values_ref[...], gain, little_ref)


def mlp_back(base, place, grads, values, table, deriv, ups, downs):
    rows, width = values.shape
    half = 2 * UNITS
    outs = [
        struct((rows, width), F32),
        struct((rows, half), BF16),
        struct((rows, half + width), BF16),
        struct((3, width), F32),
        struct((1, 2 * half), F32),
    ]
    scratch = [pltpu.VMEM((rows, width), F32)]
    operands = [place, grads, values, table, deriv, *ups, *downs]
    flops = 4 * rows * width * 2 * half
    return call(partial(mlp_back_kernel, base), outs, operands, SMALL, scratch=scratch, flops=flops)


def pair_grads_kernel(wide_ref, wide_send_ref, thin_ref, thin_send_ref, near_ref, far_ref):
    half = thin_ref.shape[1] - near_ref.shape[1]
    half_send = thin_send_ref.shape[1] - near_ref.shape[1]
    for index, out_ref in enumerate((near_ref, far_ref)):
        cut = pl.ds(index * UNITS, UNITS)
        total = mm_tn(wide_ref[:, cut], thin_ref[:, half:])
        total = total + mm_tn(wide_send_ref[:, cut], thin_send_ref[:, half_send:])
        out_ref[...] = total.astype(BF16)


def pair_grads(wide, wide_send, thin, thin_send):
    width = min(thin.shape[1], UNITS)
    out = struct((UNITS, width), BF16)
    flops = 8 * wide.shape[0] * UNITS * width
    return call(pair_grads_kernel, [out, out], [wide, wide_send, thin, thin_send], flops=flops)


MATS = 4
SWAP = (0, 2, 1, 3)


def load_weights(place_ref, parts, weights_ref, sems):
    core, wid = place_ref[0], place_ref[1]
    copies = []
    for index, part in enumerate(parts):
        side = index // 2
        turn = core if side == 0 else 1 - core
        columns = pl.ds(pl.multiple_of(turn * 384, 384), 384)
        for i in range(2):
            line = 2 * (index % 2) + i
            order = line if side == 0 else SWAP[line]
            for j in range(4):
                first = pl.multiple_of(order * 192 + jnp.bitwise_xor(wid, j) * 48, 16)
                copies.append(
                    pltpu.make_async_copy(
                        part.at[i * 4 + j],
                        weights_ref.at[:, pl.ds(first, 48), columns],
                        sems.at[len(copies)],
                    )
                )
    for copy in copies:
        copy.start()
    return copies


def spread_heads(block):
    lane_head = lax.broadcasted_iota(jnp.int32, (1, GROUP), 1) // HD
    zero = jnp.zeros_like(block)
    return jnp.concatenate([jnp.where(lane_head == h, block, zero) for h in range(HEADS)], axis=0)


def gather_heads(wide):
    lane_head = lax.broadcasted_iota(jnp.int32, (1, GROUP), 1) // HD
    rows = wide.shape[0] // HEADS
    total = jnp.where(lane_head == 0, wide[:rows], 0.0)
    for h in range(1, HEADS):
        total = jnp.where(lane_head == h, wide[h * rows : (h + 1) * rows], total)
    return total


def window_probabilities(queries, keys, mask):
    scores = mm_nt(queries, keys) * SCALE
    scores = scores.reshape(HEADS, CELLS, CELLS)
    scores = jnp.where(mask[None], scores, -1000000000.0)
    raised = jnp.exp(scores - jnp.max(scores, axis=-1, keepdims=True))
    return raised * (1.0 / jnp.sum(raised, axis=-1, keepdims=True))


def channel_probabilities(keys, values):
    scores = mm_tn(keys, values) * SCALE
    line = lax.broadcasted_iota(jnp.int32, (GROUP, GROUP), 0) // HD
    column = lax.broadcasted_iota(jnp.int32, (GROUP, GROUP), 1) // HD
    scores = jnp.where(line == column, scores, -jnp.inf)
    raised = jnp.exp(scores - jnp.max(scores, axis=-1, keepdims=True))
    return raised * (1.0 / jnp.sum(raised, axis=-1, keepdims=True))


def unit_cuts(unit, width):
    groups = width // GROUP
    image = lax.div(unit, groups)
    rows = pl.ds(pl.multiple_of(image * CELLS, 16), CELLS)
    lane = pl.multiple_of(lax.rem(unit, groups) * GROUP, GROUP)
    return image, rows, lane


def attention_kernel(
    windowed, place_ref, values_ref, table_ref, bias_ref,
    p0, p1, p2, p3, out_ref, normed_ref, qkv_ref, mixed_ref, weights_ref, sems,
):
    copies = load_weights(place_ref, (p0, p1, p2, p3), weights_ref, sems)
    rows_all, width = values_ref.shape
    base = 0 if windowed else 16
    gain, shift, outbias = (table_ref[pl.ds(base + i, 1), :] for i in (10, 11, 12))
    first_bias = 0 if windowed else 3
    normal, _ = normalize(values_ref[...])
    normed_ref[...] = (normal * gain + shift).astype(BF16)
    for copy in copies:
        copy.wait()
    for m in range(3):
        projected = mm_nt(normed_ref[...], weights_ref[m])
        projected = projected + bias_ref[pl.ds(first_bias + m, 1), :]
        qkv_ref[:, m * width : (m + 1) * width] = projected.astype(BF16)

    def step(unit, _):
        image, rows, lane = unit_cuts(unit, width)
        queries = qkv_ref[rows, pl.ds(lane, GROUP)]
        keys = qkv_ref[rows, pl.ds(lane + width, GROUP)]
        values = qkv_ref[rows, pl.ds(lane + 2 * width, GROUP)]
        if windowed:
            probs = window_probabilities(spread_heads(queries), keys, window_mask(place_ref, image))
            weights = probs.reshape(HEADS * CELLS, CELLS).astype(BF16)
            mixed = gather_heads(mm(weights, values))
        else:
            kept = keys * presence(place_ref, CELLS, image).astype(BF16)
            weights = channel_probabilities(kept, values).astype(BF16)
            mixed = mm_nt(queries, weights)
        mixed_ref[rows, pl.ds(lane, GROUP)] = mixed.astype(BF16)
        return 0

    lax.fori_loop(0, rows_all // CELLS * (width // GROUP), step, 0)
    branch = mm(mixed_ref[...], weights_ref[3]) + outbias
    out_ref[...] = values_ref[...] + presence(place_ref, rows_all) * branch


def attention(windowed, place, values, table, bias, parts):
    rows, width = values.shape
    outs = [
        struct((rows, width), F32),
        struct((rows, width), BF16),
        struct((rows, 3 * width), BF16),
        struct((rows, width), BF16),
    ]
    operands = [place, values, table, bias, *parts]
    spaces = SMALL + [(4 + i, pl.ANY) for i in range(4)]
    scratch = [pltpu.VMEM((MATS, width, width), BF16), pltpu.SemaphoreType.DMA((32,))]
    return call(
        partial(attention_kernel, windowed), outs, operands, spaces=spaces, scratch=scratch,
        flops=8 * rows * width * width,
    )


def attention_back_kernel(
    windowed, place_ref, grads_ref, values_ref, table_ref, normed_ref, qkv_ref, mixed_ref,
    p0, p1, p2, p3, out_ref, left_ref, mine_ref, theirs_ref, little_ref, bias_ref,
    weights_ref, low_ref, mix_ref, sems,
):
    copies = load_weights(place_ref, (p0, p1, p2, p3), weights_ref, sems)
    rows_all, width = values_ref.shape
    half = width // 2
    core = place_ref[0]
    own = pl.ds(pl.multiple_of(core * half, half), half)
    other = pl.ds(pl.multiple_of((1 - core) * half, half), half)
    branch = grads_ref[...] * presence(place_ref, rows_all)
    little_ref[2:3, :] = jnp.sum(branch, axis=0, keepdims=True)
    low_ref[...] = branch.astype(BF16)
    mine_ref[:, :half] = normed_ref[:, own]
    mine_ref[:, half:] = low_ref[:, own]
    theirs_ref[:, :half] = normed_ref[:, other]
    theirs_ref[:, half:] = low_ref[:, other]
    left_ref[:, 3 * width :] = mixed_ref[...]
    for copy in copies:
        copy.wait()
    mix_ref[...] = mm_nt(low_ref[...], weights_ref[3]).astype(BF16)

    def step(unit, _):
        image, rows, lane = unit_cuts(unit, width)
        queries = qkv_ref[rows, pl.ds(lane, GROUP)]
        keys = qkv_ref[rows, pl.ds(lane + width, GROUP)]
        values = qkv_ref[rows, pl.ds(lane + 2 * width, GROUP)]
        incoming = mix_ref[rows, pl.ds(lane, GROUP)]
        if windowed:
            mask = window_mask(place_ref, image)
            wide_queries = spread_heads(queries)
            wide_incoming = spread_heads(incoming)
            probs = window_probabilities(wide_queries, keys, mask)
            weights = probs.reshape(HEADS * CELLS, CELLS).astype(BF16)
            grad_probs = mm_nt(wide_incoming, values).reshape(HEADS, CELLS, CELLS)
            inner = jnp.sum(probs * grad_probs, axis=-1, keepdims=True)
            grad_scores = jnp.where(mask[None], probs * (grad_probs - inner), 0.0)
            grad_scores = grad_scores.reshape(HEADS * CELLS, CELLS).astype(BF16)
            grad_query = gather_heads(mm(grad_scores, keys)) * SCALE
            grad_keys = mm_tn(grad_scores, wide_queries) * SCALE
            grad_values = mm_tn(weights, wide_incoming)
        else:
            present = presence(place_ref, CELLS, image)
            kept = keys * present.astype(BF16)
            probs = channel_probabilities(kept, values)
            grad_probs = mm_tn(incoming, queries)
            inner = jnp.sum(probs * grad_probs, axis=-1, keepdims=True)
            grad_scores = (probs * (grad_probs - inner)).astype(BF16)
            grad_query = mm(incoming, probs.astype(BF16))
            grad_keys = mm_nt(values, grad_scores) * SCALE * present
            grad_values = mm(kept, grad_scores) * SCALE
        for m, item in enumerate((grad_query, grad_keys, grad_values)):
            left_ref[rows, pl.ds(lane + m * width, GROUP)] = item.astype(BF16)
        return 0

    lax.fori_loop(0, rows_all // CELLS * (width // GROUP), step, 0)
    total = None
    for m in range(3):
        rounded = left_ref[:, m * width : (m + 1) * width]
        bias_ref[m : m + 1, :] = jnp.sum(rounded.astype(F32), axis=0, keepdims=True)
        term = mm(rounded, weights_ref[m])
        total = term if total is None else total + term
    gain = table_ref[pl.ds((0 if windowed else 16) + 10, 1), :]
    out_ref[...] = grads_ref[...] + norm_back(total, values_ref[...], gain, little_ref)


def attention_back(windowed, place, grads, values, table, normed, qkv, mixed, parts):
    rows, width = values.shape
    outs = [
        struct((rows, width), F32),
        struct((rows, 4 * width), BF16),
        struct((rows, width), BF16),
        struct((rows, width), BF16),
        struct((3, width), F32),
        struct((3, width), F32),
    ]
    operands = [place, grads, values, table, normed, qkv, mixed, *parts]
    spaces = SMALL + [(7 + i, pl.ANY) for i in range(4)]
    scratch = [
        pltpu.VMEM((MATS, width, width), BF16),
        pltpu.VMEM((rows, width), BF16),
        pltpu.VMEM((rows, width), BF16),
        pltpu.SemaphoreType.DMA((32,)),
    ]
    return call(
        partial(attention_back_kernel, windowed), outs, operands, spaces=spaces, scratch=scratch,
        flops=10 * rows * width * width,
    )


def head_grads_kernel(place_ref, left_ref, left_send_ref, right_ref, right_send_ref, near_ref, far_ref, table_ref, other_ref):
    wid = place_ref[1]
    width = left_ref.shape[1] // MATS
    half = width // 2
    for m in range(MATS):
        cut = slice(m * width, (m + 1) * width)
        side = slice(0, half) if m < 3 else slice(half, width)
        table_ref[...] = mm_tn(left_ref[:, cut], right_ref[:, side])
        other_ref[...] = mm_tn(left_send_ref[:, cut], right_send_ref[:, side])
        for line in range(4):
            out_ref = near_ref if line < 2 else far_ref
            for j in range(4):
                inner = jnp.bitwise_xor(wid, j) * 48
                mine = table_ref[pl.ds(pl.multiple_of(line * 192 + inner, 16), 48), :]
                other = other_ref[pl.ds(pl.multiple_of(SWAP[line] * 192 + inner, 16), 48), :]
                out_ref[(line % 2) * 4 + j, m] = (mine + other).astype(BF16)


def head_grads(place, left, left_send, right, right_send):
    width = right.shape[1]
    out = struct((8, MATS, width // 16, width // 2), BF16)
    return call(
        head_grads_kernel, [out, out], [place, left, left_send, right, right_send],
        SMALL, scratch=[pltpu.VMEM((width, width // 2), F32)] * 2,
        flops=8 * left.shape[0] * width * width,
    )


def pieces_kernel(place_ref, *refs):
    core = place_ref[0]
    for base in (0, 4):
        inw, outw, up, down = refs[base : base + 4]
        outs = refs[8 + base // 4 * 3 : 11 + base // 4 * 3]
        half = inw.shape[2] // 2
        columns = pl.ds(pl.multiple_of(core * half, half), half)
        for m in range(3):
            outs[0][0, m] = inw[m, :, columns]
        outs[0][0, 3] = outw[:, columns]
        rows = up.shape[0] // 2
        own = pl.ds(pl.multiple_of(core * rows, rows), rows)
        outs[1][0] = up[own, :]
        outs[2][0] = down[own, :]


def pieces(place, *weights):
    outs = []
    for base in (0, 4):
        inw, _, up, _ = weights[base : base + 4]
        outs.append(struct((1, MATS, inw.shape[1], inw.shape[2] // 2), BF16))
        outs += [struct((1, up.shape[0] // 2, up.shape[1]), BF16)] * 2
    return call(pieces_kernel, outs, [place, *weights], SMALL)


def table_kernel(*refs):
    inputs, (table_ref, bias_ref) = refs[:20], refs[20:]
    for base in (0, 1):
        kernel, cbias, gain, shift, inb, outb, gain_two, shift_two, upb, downb = inputs[base * 10 : base * 10 + 10]
        table_ref[pl.ds(base * 16, 9), :] = kernel[...]
        for index, item in enumerate((cbias, gain, shift, outb, gain_two, shift_two, downb)):
            table_ref[pl.ds(base * 16 + 9 + index, 1), :] = item[...].reshape(1, -1)
        first = 0 if base == 0 else 6
        count = inb.shape[0]
        bias_ref[pl.ds(first, count), :] = inb[...]
        wide = upb[...].reshape(1, -1)
        step = wide.shape[1] // 4
        for index in range(4):
            bias_ref[pl.ds(first + count + index, 1), :] = wide[:, index * step : (index + 1) * step]
    bias_ref[pl.ds(13, 3), :] = jnp.zeros((3, bias_ref.shape[1]), F32)


def tables(*small):
    width = small[0].shape[1]
    return call(table_kernel, [struct((32, width), F32), struct((16, small[4].shape[1]), F32)], list(small))


def order_kernel(place_ref, g0, g1, g2, head_ref, hidden_ref):
    core, wid = place_ref[0], place_ref[1]
    hids = [g0, g1, g2.at[0], g2.at[1]]
    step = g0.shape[1]
    half = step // 2
    head_ref[...] = jnp.zeros_like(head_ref)
    hidden_ref[...] = jnp.zeros_like(hidden_ref)
    for row, source in ((0, 0), (2, 1), (3, 6), (4, 7), (5, 8)):
        for i in range(4):
            head_ref[row : row + 1, i * step : (i + 1) * step] = hids[i][source : source + 1, :]
    for index, first in ((0, 2), (1, 9)):
        for side in range(2):
            for i in range(4):
                hid = hids[i if side == 0 else SWAP[i]]
                for j in range(4):
                    line = hid[pl.ds(first + jnp.bitwise_xor(wid, j), 1), :]
                    value = jnp.where(core == side, line[:, :half], line[:, half:])
                    lane = side * 16 * half + (i * 4 + j) * half
                    hidden_ref[index : index + 1, lane : lane + half] = value


def order_biases(place, g0, g1, g2):
    step = g0.shape[1]
    outs = [struct((8, 4 * step), F32), struct((8, 16 * step), F32)]
    return call(order_kernel, outs, [place, g0, g1, g2], SMALL)


BIASES = 16


def small_kernel(counts, kinds, place_ref, *refs):
    out_ref = refs[-1]
    core, wid, hid = place_ref[0], place_ref[1], place_ref[2]
    out_ref[...] = jnp.zeros_like(out_ref)
    row = 0
    for count, ref in zip(counts, refs):
        out_ref[pl.ds(row, count), :] = ref[...]
        row += count
    base = out_ref.shape[0] - BIASES
    rest = refs[len(counts) : -1]
    heads, hiddens = rest[0], rest[1:]
    step = heads.shape[1] // 4
    half = step // 2
    gap = jnp.zeros((1, 256 - step), F32)
    blank = jnp.zeros((1, half), F32)
    for i in range(4):
        owned = jnp.bitwise_xor(hid, jnp.where(core == 0, i, SWAP[i]))
        for j in range(4):
            parts = []
            for ref in hiddens:
                lane = (i * 4 + j) * half
                mine = ref[0:1, lane : lane + half]
                lane = 16 * half + (SWAP[i] * 4 + j) * half
                other = ref[0:1, lane : lane + half]
                parts += [jnp.where(core == 0, mine, other), jnp.where(core == 0, other, mine), gap]
            for _ in range(2 - len(hiddens)):
                parts += [blank, blank, gap]
            line = pl.ds(base + owned * 4 + jnp.bitwise_xor(wid, j), 1)
            out_ref[line, 0:512] = jnp.concatenate(parts, axis=1)
        for place_of, kind in enumerate(kinds):
            line = pl.ds(base + owned * 4 + place_of, 1)
            value = heads[kind : kind + 1, i * step : (i + 1) * step]
            out_ref[line, 512:768] = jnp.concatenate([value, gap], axis=1)


def small_table(kinds, place, rows, heads, hiddens):
    counts = [item.shape[0] for item in rows]
    total = (sum(counts) + 7) // 8 * 8 + BIASES
    return call(
        partial(small_kernel, counts, kinds), [struct((total, rows[0].shape[1]), F32)],
        [place, *rows, heads, *hiddens], SMALL,
    )[0]


def outputs_kernel(place_ref, early_ref, late_ref, *outs):
    hid = place_ref[2]
    early_base = early_ref.shape[0] - BIASES
    late_base = late_ref.shape[0] - BIASES
    plan = (
        (outs[:10], late_ref, 0, late_ref, 10, late_base, early_ref, 10, 0),
        (outs[10:], early_ref, 0, early_ref, 13, early_base, early_ref, 16, 1),
    )
    for refs, sums, first, one, at_one, heads_base, two, at_two, column in plan:
        kernel, cbias, gain, shift, inb, outb, gain_two, shift_two, upb, downb = refs
        heads = late_ref if column == 0 else early_ref
        kernel[...] = sums[pl.ds(first, 9), :]
        for ref, source, row in (
            (cbias, sums, 9), (gain, one, at_one), (shift, one, at_one + 1), (outb, one, at_one + 2),
            (gain_two, two, at_two), (shift_two, two, at_two + 1), (downb, two, at_two + 2),
        ):
            ref[...] = source[pl.ds(row, 1), :].reshape(-1)
        step = inb.shape[1]
        for index in range(inb.shape[0]):
            inb[pl.ds(index, 1), :] = heads[pl.ds(heads_base + hid * 4 + index, 1), :][:, 512 : 512 + step]
        for index in range(4):
            line = early_ref[pl.ds(early_base + hid * 4 + index, 1), :]
            upb[pl.ds(index * step, step)] = line[:, column * 256 : column * 256 + step].reshape(-1)


def small_outputs(place, early, late):
    width = early.shape[1]
    step = width // 4
    outs = []
    for count in (2, 3):
        flat = struct((width,), F32)
        outs += [struct((9, width), F32), flat, flat, flat, struct((count, step), F32), flat, flat, flat, flat, flat]
    return call(outputs_kernel, outs, [place, early, late], SMALL)


class Line:
    def __init__(self, mark):
        self.mark = mark

    def gate(self, tree):
        tree, self.mark = lax.optimization_barrier((tree, self.mark))
        return tree

    def run(self, function, *operands):
        return self.gate(function(*self.gate(operands)))


class Gather:
    def __init__(self, line, piece):
        self.line, self.near, self.step, self.flight = line, piece, 0, ()

    def advance(self):
        gate = self.line.gate
        if self.step in (1, 2, 3):
            arrived = gate(self.flight[0])
            self.near = jnp.concatenate([self.near, arrived], axis=0)
        elif self.step == 4:
            self.far, self.other_near = gate(self.flight)
        elif self.step == 5:
            self.other_far = gate(self.flight[0])
        if self.step < 4:
            self.near = gate(self.near)
        if self.step == 0:
            self.flight = (exchange(self.near, "wid", 1),)
        elif self.step == 1:
            self.flight = (exchange(self.near, "wid", 2),)
        elif self.step == 2:
            self.flight = (cross(self.near, True),)
        elif self.step == 3:
            self.flight = (cross(self.near, False), sibling(self.near))
        elif self.step == 4:
            self.far = gate(self.far)
            self.flight = (sibling(self.far),)
        self.step += 1

    def parts(self):
        return [self.near, self.far, self.other_near, self.other_far]

    def rows(self):
        return [part.reshape(-1, part.shape[-1]) for part in self.parts()]


class Scatter:
    def __init__(self, line, near, far, axis):
        self.line, self.kept, self.sent, self.axis, self.step = line, near, far, axis, 0

    def advance(self):
        gate = self.line.gate
        if self.step in (1, 2, 3):
            arrived = gate(self.flight)
            half = arrived.shape[0] // 2
            self.sent = (self.kept[half:].astype(F32) + arrived[half:].astype(F32)).astype(BF16)
            self.kept = self.kept[:half].astype(F32) + arrived[:half].astype(F32)
        elif self.step == 4:
            total = self.kept[0] + gate(self.flight)[0].astype(F32)
            bit = 2
            while bit < lax.axis_size("dp"):
                total = total + exchange(total, "dp", bit)
                bit *= 2
            self.kept = total
        elif self.step == 5:
            self.total = by_core(self.kept, gate(self.flight), self.axis)
        if self.step < 4:
            self.sent = gate(self.sent)
        if self.step == 0:
            self.flight = cross(self.sent, False)
        elif self.step == 1:
            self.flight = cross(self.sent, True)
        elif self.step == 2:
            self.flight = exchange(self.sent, "wid", 2)
        elif self.step == 3:
            self.flight = exchange(self.sent, "wid", 1)
        elif self.step == 4:
            self.flight = sibling(gate(self.kept))
        self.step += 1


class Small:
    def __init__(self, line, table):
        self.line, self.table, self.flight = line, table, None
        self.steps = []
        for axis in ("dp", "hid", "wid"):
            bit = 1
            while bit < lax.axis_size(axis):
                self.steps.append((axis, bit))
                bit *= 2

    def advance(self):
        if self.flight is not None:
            self.table = self.table + self.line.gate(self.flight)
            self.flight = None
        if self.steps:
            axis, bit = self.steps.pop(0)
            self.table = self.line.gate(self.table)
            self.flight = exchange(self.table, axis, bit)
            return True
        return False


def body(
    inputs, grid_sizes, cotangent,
    wkernel, wcbias, wgain, wshift, winw, winb, woutw, woutb,
    wgain_two, wshift_two, wupw, wupb, wdownw, wdownb,
    ckernel, ccbias, cgain, cshift, cinw, cinb, coutw, coutb,
    cgain_two, cshift_two, cupw, cupb, cdownw, cdownb,
):
    image_count = inputs.shape[0] // (PADDED * PADDED)
    hid, wid = lax.axis_index("hid"), lax.axis_index("wid")
    own_sizes = lax.dynamic_slice_in_dim(
        grid_sizes, (hid * lax.axis_size("wid") + wid) * image_count, image_count, 0
    )
    at = jnp.stack([lax.rem(lax.axis_index("dp"), 2), wid, hid]).astype(jnp.int32)
    place = jnp.concatenate([at, own_sizes])
    line = Line(winb[0, 0])

    groups = [
        Gather(line, piece)
        for piece in pieces(place, winw, woutw, wupw, wdownw, cinw, coutw, cupw, cdownw)
    ]

    def go(*numbers):
        for number in numbers:
            groups[number].advance()

    go(0)
    table, bias = line.run(
        tables, wkernel, wcbias, wgain, wshift, winb, woutb, wgain_two, wshift_two, wupb, wdownb,
        ckernel, ccbias, cgain, cshift, cinb, coutb, cgain_two, cshift_two, cupb, cdownb,
    )
    go(0, 1)
    bias_one = cross(bias, True)
    start, after_conv = line.run(partial(first_conv, 0), place, inputs, table)
    cotangent, low_four = line.run(low_cells, place, cotangent)
    bias_one = line.gate(bias_one)
    bias_two = cross(jnp.stack([bias, bias_one]), False)
    low_four_other = sibling(low_four)
    go(1, 2)
    go(0, 2, 3)
    bias_two, low_four_other = line.gate((bias_two, low_four_other))
    head_bias, hidden_bias = line.run(order_biases, place, bias, bias_one, bias_two)
    go(0)
    go(1, 3, 4)
    go(0, 1, 0)
    att_one = groups[0].parts()
    after_attn, normed_one, qkv_one, mixed_one = line.run(
        partial(attention, True), place, after_conv, table, head_bias, att_one
    )
    go(2, 4, 5)
    go(1, 2, 3, 5, 2, 1, 3, 2)
    ups_two, downs_two = groups[1].rows(), groups[2].rows()
    after_mlp, acted_two, fpack_two, deriv_two = line.run(
        partial(mlp, 0, False), place, after_attn, table, hidden_bias, ups_two, downs_two
    )
    fpack_two_other = sibling(fpack_two)
    go(4, 3, 4, 5)
    after_conv_c = line.run(partial(conv, 16), place, after_mlp, table)
    go(3, 5)
    att_three = groups[3].parts()
    after_attn_c, normed_three, qkv_three, mixed_three = line.run(
        partial(attention, False), place, after_conv_c, table, head_bias, att_three
    )
    fpack_two_other = line.gate(fpack_two_other)
    go(4, 5, 4, 5)
    ups_four, downs_four = groups[4].rows(), groups[5].rows()
    outputs, acted_four, fpack_four, deriv_four = line.run(
        partial(mlp, 16, True), place, after_attn_c, table, hidden_bias, ups_four, downs_four
    )

    def scatter(near, far, axis):
        group = Scatter(line, near.reshape((8, -1) + near.shape[-1:] if axis == 0 else near.shape),
                        far.reshape((8, -1) + far.shape[-1:] if axis == 0 else far.shape), axis)
        group.advance()
        return group

    fpack_four_other = line.gate(sibling(fpack_four))
    d_four = scatter(*line.run(pair_grads, acted_four, fpack_four_other, low_four, low_four_other), 0)
    flowing, gh_four, bpack_four, little_four, upb_four = line.run(
        partial(mlp_back, 16), place, cotangent, after_attn_c, table, deriv_four, ups_four, downs_four
    )
    bpack_four_other = sibling(bpack_four)
    d_four.advance()
    bpack_four_other = line.gate(bpack_four_other)
    u_four = scatter(*line.run(pair_grads, gh_four, bpack_four_other, fpack_four, fpack_four_other), 0)
    d_four.advance()
    flowing, left_three, mine_three, theirs_three, little_three, inb_three = line.run(
        partial(attention_back, False),
        place, flowing, after_conv_c, table, normed_three, qkv_three, mixed_three, att_three,
    )
    sent_three = sibling(left_three), sibling(theirs_three)
    u_four.advance()
    sent_three = line.gate(sent_three)
    a_three = scatter(*line.run(head_grads, place, left_three, sent_three[0], mine_three, sent_three[1]), 2)
    d_four.advance()
    u_four.advance()
    flowing, sums_three = line.run(partial(conv_back, 16, False), place, flowing, after_mlp, table)
    flowing, gh_two, bpack_two, little_two, upb_two = line.run(
        partial(mlp_back, 0), place, flowing, after_attn, table, deriv_two, ups_two, downs_two
    )
    bpack_two_other = sibling(bpack_two)
    a_three.advance()
    bpack_two_other = line.gate(bpack_two_other)
    d_two = scatter(*line.run(pair_grads, acted_two, fpack_two_other, bpack_two, bpack_two_other), 0)
    u_four.advance()
    d_four.advance()
    a_three.advance()
    u_two = scatter(*line.run(pair_grads, gh_two, bpack_two_other, fpack_two, fpack_two_other), 0)
    early = line.run(
        partial(small_table, (0, 1, 2)), place,
        [sums_three, little_two, little_three, little_four], inb_three, [upb_two, upb_four],
    )
    early = Small(line, early)
    early.advance()
    u_four.advance()
    flowing, left_one, mine_one, theirs_one, little_one, inb_one = line.run(
        partial(attention_back, True),
        place, flowing, after_conv, table, normed_one, qkv_one, mixed_one, att_one,
    )
    sent_one = sibling(left_one), sibling(theirs_one)
    d_two.advance()
    a_three.advance()
    early.advance()
    sent_one = line.gate(sent_one)
    a_one = scatter(*line.run(head_grads, place, left_one, sent_one[0], mine_one, sent_one[1]), 2)
    u_two.advance()
    d_two.advance()
    early.advance()
    input_grad, sums_one = line.run(partial(conv_back, 0, True), place, flowing, start, table)
    late = Small(line, line.run(partial(small_table, (0, 2)), place, [sums_one, little_one], inb_one, []))
    early.advance()
    late.advance()
    a_three.advance()
    u_two.advance()
    late.advance()
    early.advance()
    a_one.advance()
    late.advance()
    d_two.advance()
    early.advance()
    a_one.advance()
    late.advance()
    u_two.advance()
    late.advance()
    a_one.advance()
    u_two.advance()
    while late.advance():
        pass
    while early.advance():
        pass
    small = line.run(small_outputs, place, early.table, late.table)
    for group in (d_four, u_four, a_three, d_two, u_two, a_one):
        while group.step < 6:
            group.advance()
    gatt_one, gatt_three = a_one.total, a_three.total

    def ordered(small, attention, up, down):
        return (
            *small[:4], attention[:3], small[4], attention[3], *small[5:8], up.total, small[8], down.total, small[9]
        )

    return (
        outputs, input_grad,
        *ordered(small[:10], gatt_one, u_two, d_two),
        *ordered(small[10:], gatt_three, u_four, d_four),
    )


def solution(mesh):
    tokens, everywhere = P(("dp", "hid", "wid"), None), P()
    stacked, rows = P(None, ("hid", "wid"), None), P(("hid", "wid"), None)
    block = (
        everywhere, everywhere, everywhere, everywhere, stacked, P(None, "hid"), rows, everywhere,
        everywhere, everywhere, rows, P("hid"), rows, everywhere,
    )
    return jax.shard_map(
        body,
        mesh=mesh,
        in_specs=(tokens, P("dp"), tokens) + block + block,
        out_specs=(tokens, tokens) + block + block,
        check_vma=False,
    )
```

```python
from functools import partial

import jax
import jax.numpy as jnp
from jax import lax
from jax.experimental import pallas as pl
from jax.experimental.pallas import tpu as pltpu
from jax.sharding import PartitionSpec as P

HD = 32
WINDOW = 7
PADDED = 14
GRID = 12
CELLS = GRID * GRID
EPSILON = 1e-05
F32 = jnp.float32
BF16 = jnp.bfloat16
SCALE = HD ** (-0.5)


def exchange(values, axis, bit):
    pairs = [(index, index ^ bit) for index in range(lax.axis_size(axis))]
    return lax.ppermute(values, axis, pairs)


def sibling(values):
    return exchange(values, "dp", 1)


def cross(values, first):
    hids = lax.axis_size("hid")
    pairs = []
    for core in range(lax.axis_size("dp")):
        bit = 1 if (core % 2 == 0) == first else 2
        pairs += [(core * hids + index, core * hids + (index ^ bit)) for index in range(hids)]
    return lax.ppermute(values, ("dp", "hid"), pairs)


def second_core():
    return lax.rem(lax.axis_index("dp"), 2) == 1


def by_core(own, other, axis):
    second = second_core()
    return jnp.concatenate(
        [jnp.where(second, other, own), jnp.where(second, own, other)], axis=axis
    )


VMEM_LIMIT = 16 * 1024 * 1024
GROUP = 256
WAIT = 1_000_000_000
HEADS = GROUP // HD


def call(kernel, outs, operands, spaces=(), scratch=(), flops=1):
    vmem = pl.BlockSpec(memory_space=pltpu.VMEM)
    specs = [vmem] * len(operands)
    for index, space in spaces:
        specs[index] = pl.BlockSpec(memory_space=space)
    return pl.pallas_call(
        kernel,
        out_shape=list(outs),
        in_specs=specs,
        out_specs=[vmem] * len(outs),
        scratch_shapes=list(scratch),
        compiler_params=pltpu.CompilerParams(vmem_limit_bytes=VMEM_LIMIT),
        cost_estimate=pl.CostEstimate(flops=flops, bytes_accessed=1, transcendentals=0),
    )(*operands)


def struct(shape, dtype):
    return jax.ShapeDtypeStruct(shape, dtype)


def mm(left, right):
    return jnp.dot(left, right, preferred_element_type=F32)


def mm_nt(left, right):
    return lax.dot_general(left, right, (((1,), (1,)), ((), ())), preferred_element_type=F32)


def mm_tn(left, right):
    return lax.dot_general(left, right, (((0,), (0,)), ((), ())), preferred_element_type=F32)


def normalize(values):
    center = jnp.mean(values, axis=1, keepdims=True)
    spread = jnp.mean(values * values, axis=1, keepdims=True) - center * center
    scaled = lax.rsqrt(spread + EPSILON)
    return (values - center) * scaled, scaled


def cells_of(rows):
    cell = lax.broadcasted_iota(jnp.int32, (rows, 1), 0)
    column = lax.rem(cell, GRID)
    line = lax.rem(lax.div(cell, GRID), GRID)
    return line, column


def shift_columns(values):
    rows = values.shape[0]
    _, column = cells_of(rows)
    before = jnp.where(column != 0, pltpu.roll(values, 1, 0), 0.0)
    after = jnp.where(column != GRID - 1, pltpu.roll(values, rows - 1, 0), 0.0)
    return before, after


def shift_lines(values, ahead):
    rows = values.shape[0]
    line, _ = cells_of(rows)
    if ahead:
        return jnp.where(line != GRID - 1, pltpu.roll(values, rows - GRID, 0), 0.0)
    return jnp.where(line != 0, pltpu.roll(values, GRID, 0), 0.0)


def convolve(values, taps):
    before, after = shift_columns(values)
    lines = [
        before * taps[3 * a] + values * taps[3 * a + 1] + after * taps[3 * a + 2] for a in range(3)
    ]
    return shift_lines(lines[0], False) + lines[1] + shift_lines(lines[2], True)


def presence(place_ref, rows, image=None):
    line, column = cells_of(rows)
    if image is not None:
        side = place_ref[3 + image]
    else:
        cell = lax.broadcasted_iota(jnp.int32, (rows, 1), 0)
        side = jnp.zeros((rows, 1), jnp.int32) + place_ref[3]
        for index in range(1, rows // CELLS):
            side = jnp.where(cell >= index * CELLS, place_ref[3 + index], side)
    return jnp.where((line < side) & (column < side), 1.0, 0.0).astype(F32)


def window_mask(place_ref, image):
    side = place_ref[3 + image]
    query = lax.broadcasted_iota(jnp.int32, (CELLS, 1), 0)
    key = lax.broadcasted_iota(jnp.int32, (1, CELLS), 1)
    line, column = lax.div(key, GRID), lax.rem(key, GRID)
    kept = (line < side) & (column < side)

    def window(cell):
        below = lax.div(cell, GRID) >= WINDOW
        right = lax.rem(cell, GRID) >= WINDOW
        return jnp.where(below, 2, 0) + jnp.where(right, 1, 0)

    own = jnp.where(kept, window(key), -1)
    return window(query) == own


LANES = 256


def pack_cells(slots_ref, cells_ref):
    for image in range(cells_ref.shape[0] // CELLS):
        for line in range(GRID):
            cells_ref[pl.ds(image * CELLS + line * GRID, GRID), :] = slots_ref[
                pl.ds((image * PADDED + line) * PADDED, GRID), :
            ]


def unpack_cells(cells_ref, slots_ref):
    slots_ref[...] = jnp.zeros_like(slots_ref)
    for image in range(cells_ref.shape[0] // CELLS):
        for line in range(GRID):
            slots_ref[pl.ds((image * PADDED + line) * PADDED, GRID), :] = cells_ref[
                pl.ds(image * CELLS + line * GRID, GRID), :
            ]


def conv_lanes(values, present, table_ref, base, cut):
    taps = [table_ref[pl.ds(base + i, 1), cut] for i in range(9)]
    return values + present * (convolve(values, taps) + table_ref[pl.ds(base + 9, 1), cut])


def conv_kernel(base, place_ref, values_ref, table_ref, out_ref):
    present = presence(place_ref, values_ref.shape[0])
    for lane in range(0, values_ref.shape[1], LANES):
        cut = pl.ds(lane, LANES)
        out_ref[:, cut] = conv_lanes(values_ref[:, cut], present, table_ref, base, cut)


def first_conv_kernel(base, place_ref, slots_ref, table_ref, start_ref, out_ref):
    pack_cells(slots_ref, start_ref)
    present = presence(place_ref, start_ref.shape[0])
    for lane in range(0, start_ref.shape[1], LANES):
        cut = pl.ds(lane, LANES)
        values = start_ref[:, cut] * present
        start_ref[:, cut] = values
        out_ref[:, cut] = conv_lanes(values, present, table_ref, base, cut)


def conv_back_kernel(base, place_ref, grads_ref, values_ref, table_ref, out_ref, sums_ref, *rest):
    present = presence(place_ref, grads_ref.shape[0])
    target = rest[0] if rest else out_ref
    for lane in range(0, grads_ref.shape[1], LANES):
        cut = pl.ds(lane, LANES)
        grads = grads_ref[:, cut]
        masked = grads * present
        taps = [table_ref[pl.ds(base + 8 - i, 1), cut] for i in range(9)]
        flowing = grads + convolve(masked, taps)
        target[:, cut] = flowing * present if rest else flowing
        values = values_ref[:, cut]
        before, after = shift_columns(values)
        behind = shift_lines(masked, False)
        ahead = shift_lines(masked, True)
        for a, moved in enumerate((ahead, masked, behind)):
            for e, source in enumerate((before, values, after)):
                sums_ref[pl.ds(3 * a + e, 1), cut] = jnp.sum(moved * source, axis=0, keepdims=True)
        sums_ref[pl.ds(9, 1), cut] = jnp.sum(masked, axis=0, keepdims=True)
    if rest:
        unpack_cells(target, out_ref)


SMALL = [(0, pltpu.SMEM)]


def conv(base, place, values, table):
    return call(partial(conv_kernel, base), [struct(values.shape, F32)], [place, values, table], SMALL)[0]


def first_conv(base, place, slots, table):
    cells = struct((slots.shape[0] // (PADDED * PADDED) * CELLS, slots.shape[1]), F32)
    return call(partial(first_conv_kernel, base), [cells, cells], [place, slots, table], SMALL)


def conv_back(base, last, place, grads, values, table):
    rows, width = grads.shape
    images = rows // CELLS
    out = struct((images * PADDED * PADDED if last else rows, width), F32)
    scratch = [pltpu.VMEM((rows, width), F32)] if last else []
    return call(
        partial(conv_back_kernel, base), [out, struct((10, width), F32)], [place, grads, values, table],
        SMALL, scratch=scratch,
    )


def cells(slots):
    shape = (slots.shape[0] // (PADDED * PADDED) * CELLS, slots.shape[1])
    return call(pack_cells, [struct(shape, F32)], [slots])[0]


UNITS = 768


def tile(part, which):
    return part[:, which].reshape(-1, part.shape[-1])


def mlp_kernel(base_row, place_ref, values_ref, table_ref, upbias_ref, p0, p1, p2, p3, *rest):
    last = base_row != 0
    gain, shift, downbias = (table_ref[pl.ds(base_row + i, 1), :] for i in (13, 14, 15))
    ubias = 1 if last else 0
    out_ref, acted_ref, send_ref, deriv_ref, total_ref = rest[:5]
    values = values_ref[...]
    normal, _ = normalize(values)
    half = 2 * UNITS
    send_ref[:, half:] = (normal * gain + shift).astype(BF16)
    for index, part in enumerate((p0, p1, p2, p3)):
        target = acted_ref if index < 2 else send_ref
        base = (index % 2) * UNITS
        here = slice(index * UNITS, (index + 1) * UNITS)
        there = slice(base, base + UNITS)
        hidden = mm_nt(send_ref[:, half:], tile(part, 0)) + upbias_ref[ubias : ubias + 1, here]
        below = 0.5 + 0.5 * lax.erf(hidden * (0.5**0.5))
        target[:, there] = (hidden * below).astype(BF16)
        bell = jnp.exp(hidden * hidden * -0.5) * 0.3989422804014327
        deriv_ref[:, here] = below + hidden * bell
        term = mm(target[:, there], tile(part, 1))
        total_ref[...] = term if index == 0 else total_ref[...] + term
    result = values + presence(place_ref, values.shape[0]) * (total_ref[...] + downbias)
    if last:
        rest[5][...] = result
        unpack_cells(rest[5], out_ref)
    else:
        out_ref[...] = result


def mlp(base, place, values, table, upbias, parts):
    last = base != 0
    rows, width = values.shape
    images = rows // CELLS
    half = 2 * UNITS
    outs = [
        struct((images * PADDED * PADDED if last else rows, width), F32),
        struct((rows, half), BF16),
        struct((rows, half + width), BF16),
        struct((rows, 2 * half), F32),
    ]
    scratch = [pltpu.VMEM((rows, width), F32)] * (2 if last else 1)
    operands = [place, values, table, upbias, *parts]
    return call(partial(mlp_kernel, base), outs, operands, SMALL, scratch=scratch)


def norm_back(dn, values, gain, little_ref):
    normal, scaled = normalize(values)
    little_ref[0:1, :] = jnp.sum(dn * normal, axis=0, keepdims=True)
    little_ref[1:2, :] = jnp.sum(dn, axis=0, keepdims=True)
    grad_normal = dn * gain
    first = jnp.mean(grad_normal, axis=1, keepdims=True)
    second = jnp.mean(grad_normal * normal, axis=1, keepdims=True)
    return scaled * (grad_normal - first - normal * second)


def mlp_back_kernel(
    base_row, place_ref, grads_ref, values_ref, table_ref, deriv_ref, p0, p1, p2, p3,
    out_ref, hidden_ref, send_ref, little_ref, bias_ref, total_ref,
):
    half = 2 * UNITS
    branch = grads_ref[...] * presence(place_ref, grads_ref.shape[0])
    little_ref[2:3, :] = jnp.sum(branch, axis=0, keepdims=True)
    send_ref[:, half:] = branch.astype(BF16)
    for index, part in enumerate((p0, p1, p2, p3)):
        target = hidden_ref if index < 2 else send_ref
        base = (index % 2) * UNITS
        here = slice(index * UNITS, (index + 1) * UNITS)
        there = slice(base, base + UNITS)
        acted = mm_nt(send_ref[:, half:], tile(part, 1))
        hidden = (acted * deriv_ref[:, here]).astype(BF16)
        target[:, there] = hidden
        bias_ref[:, here] = jnp.sum(hidden.astype(F32), axis=0, keepdims=True)
        term = mm(target[:, there], tile(part, 0))
        total_ref[...] = term if index == 0 else total_ref[...] + term
    gain = table_ref[pl.ds(base_row + 13, 1), :]
    out_ref[...] = grads_ref[...] + norm_back(total_ref[...], values_ref[...], gain, little_ref)


def mlp_back(base, place, grads, values, table, deriv, parts):
    rows, width = values.shape
    half = 2 * UNITS
    outs = [
        struct((rows, width), F32),
        struct((rows, half), BF16),
        struct((rows, half + width), BF16),
        struct((3, width), F32),
        struct((1, 2 * half), F32),
    ]
    scratch = [pltpu.VMEM((rows, width), F32)]
    operands = [place, grads, values, table, deriv, *parts]
    return call(partial(mlp_back_kernel, base), outs, operands, SMALL, scratch=scratch)


def pair_grads_kernel(acted_ref, normed_ref, normed_send_ref, hidden_ref, branch_ref, branch_send_ref, near_ref, far_ref):
    half = 2 * UNITS
    for index, out_ref in enumerate((near_ref, far_ref)):
        cut = slice(index * UNITS, (index + 1) * UNITS)
        for which, (wide, wide_send, thin, thin_send) in enumerate((
            (hidden_ref, branch_send_ref, normed_ref, normed_send_ref),
            (acted_ref, normed_send_ref, branch_ref, branch_send_ref),
        )):
            total = mm_tn(wide[:, cut], thin[:, half:]) + mm_tn(wide_send[:, cut], thin_send[:, half:])
            out_ref[:, which] = total.astype(BF16).reshape(8, -1, total.shape[1])


def pair_grads(acted, normed, normed_send, hidden, branch, branch_send):
    width = normed.shape[1] - 2 * UNITS
    out = struct((8, 2, UNITS // 8, width), BF16)
    return call(pair_grads_kernel, [out, out], [acted, normed, normed_send, hidden, branch, branch_send])


MATS = 4
SWAP = (0, 2, 1, 3)


def load_weights(place_ref, parts, weights_ref, sems):
    core, wid = place_ref[0], place_ref[1]
    copies = []
    for index, part in enumerate(parts):
        side = index // 2
        turn = core if side == 0 else 1 - core
        columns = pl.ds(pl.multiple_of(turn * 384, 384), 384)
        for i in range(2):
            line = 2 * (index % 2) + i
            order = line if side == 0 else SWAP[line]
            for j in range(4):
                first = pl.multiple_of(order * 192 + jnp.bitwise_xor(wid, j) * 48, 16)
                copies.append(
                    pltpu.make_async_copy(
                        part.at[i * 4 + j],
                        weights_ref.at[:, pl.ds(first, 48), columns],
                        sems.at[len(copies)],
                    )
                )
    for copy in copies:
        copy.start()
    return copies


def spread_heads(block):
    lane_head = lax.broadcasted_iota(jnp.int32, (1, GROUP), 1) // HD
    zero = jnp.zeros_like(block)
    return jnp.concatenate([jnp.where(lane_head == h, block, zero) for h in range(HEADS)], axis=0)


def gather_heads(wide):
    lane_head = lax.broadcasted_iota(jnp.int32, (1, GROUP), 1) // HD
    rows = wide.shape[0] // HEADS
    total = jnp.where(lane_head == 0, wide[:rows], 0.0)
    for h in range(1, HEADS):
        total = jnp.where(lane_head == h, wide[h * rows : (h + 1) * rows], total)
    return total


def window_probabilities(queries, keys, mask):
    scores = mm_nt(queries, keys) * SCALE
    scores = scores.reshape(HEADS, CELLS, CELLS)
    scores = jnp.where(mask[None], scores, -1000000000.0)
    raised = jnp.exp(scores - jnp.max(scores, axis=-1, keepdims=True))
    return raised * (1.0 / jnp.sum(raised, axis=-1, keepdims=True))


def channel_probabilities(keys, values):
    scores = mm_tn(keys, values) * SCALE
    line = lax.broadcasted_iota(jnp.int32, (GROUP, GROUP), 0) // HD
    column = lax.broadcasted_iota(jnp.int32, (GROUP, GROUP), 1) // HD
    scores = jnp.where(line == column, scores, -jnp.inf)
    raised = jnp.exp(scores - jnp.max(scores, axis=-1, keepdims=True))
    return raised * (1.0 / jnp.sum(raised, axis=-1, keepdims=True))


def unit_cuts(unit, width):
    groups = width // GROUP
    image = lax.div(unit, groups)
    rows = pl.ds(pl.multiple_of(image * CELLS, 16), CELLS)
    lane = pl.multiple_of(lax.rem(unit, groups) * GROUP, GROUP)
    return image, rows, lane


def attention_kernel(
    windowed, place_ref, values_ref, table_ref, bias_ref,
    p0, p1, p2, p3, out_ref, normed_ref, qkv_ref, mixed_ref, weights_ref, sems,
):
    copies = load_weights(place_ref, (p0, p1, p2, p3), weights_ref, sems)
    rows_all, width = values_ref.shape
    base = 0 if windowed else 16
    gain, shift, outbias = (table_ref[pl.ds(base + i, 1), :] for i in (10, 11, 12))
    first_bias = 0 if windowed else 3
    normal, _ = normalize(values_ref[...])
    normed_ref[...] = (normal * gain + shift).astype(BF16)
    for copy in copies:
        copy.wait()
    for m in range(3):
        projected = mm_nt(normed_ref[...], weights_ref[m])
        projected = projected + bias_ref[pl.ds(first_bias + m, 1), :]
        qkv_ref[:, m * width : (m + 1) * width] = projected.astype(BF16)

    def step(unit, _):
        image, rows, lane = unit_cuts(unit, width)
        queries = qkv_ref[rows, pl.ds(lane, GROUP)]
        keys = qkv_ref[rows, pl.ds(lane + width, GROUP)]
        values = qkv_ref[rows, pl.ds(lane + 2 * width, GROUP)]
        if windowed:
            probs = window_probabilities(spread_heads(queries), keys, window_mask(place_ref, image))
            weights = probs.reshape(HEADS * CELLS, CELLS).astype(BF16)
            mixed = gather_heads(mm(weights, values))
        else:
            kept = keys * presence(place_ref, CELLS, image).astype(BF16)
            weights = channel_probabilities(kept, values).astype(BF16)
            mixed = mm_nt(queries, weights)
        mixed_ref[rows, pl.ds(lane, GROUP)] = mixed.astype(BF16)
        return 0

    lax.fori_loop(0, rows_all // CELLS * (width // GROUP), step, 0)
    branch = mm(mixed_ref[...], weights_ref[3]) + outbias
    out_ref[...] = values_ref[...] + presence(place_ref, rows_all) * branch


def attention(windowed, place, values, table, bias, parts):
    rows, width = values.shape
    outs = [
        struct((rows, width), F32),
        struct((rows, width), BF16),
        struct((rows, 3 * width), BF16),
        struct((rows, width), BF16),
    ]
    operands = [place, values, table, bias, *parts]
    spaces = SMALL + [(4 + i, pltpu.HBM) for i in range(4)]
    scratch = [pltpu.VMEM((MATS, width, width), BF16), pltpu.SemaphoreType.DMA((32,))]
    return call(
        partial(attention_kernel, windowed), outs, operands, spaces=spaces, scratch=scratch,
    )


def attention_back_kernel(
    windowed, place_ref, grads_ref, values_ref, table_ref, normed_ref, qkv_ref, mixed_ref,
    p0, p1, p2, p3, out_ref, left_ref, rest_ref, mine_ref, little_ref, bias_ref,
    weights_ref, low_ref, mix_ref, sems,
):
    copies = load_weights(place_ref, (p0, p1, p2, p3), weights_ref, sems)
    rows_all, width = values_ref.shape
    half = width // 2
    core = place_ref[0]
    own = pl.ds(pl.multiple_of(core * half, half), half)
    other = pl.ds(pl.multiple_of((1 - core) * half, half), half)
    branch = grads_ref[...] * presence(place_ref, rows_all)
    little_ref[2:3, :] = jnp.sum(branch, axis=0, keepdims=True)
    low_ref[...] = branch.astype(BF16)
    mine_ref[:, :half] = normed_ref[:, own]
    mine_ref[:, half:] = low_ref[:, own]
    rest_ref[:, width : width + half] = normed_ref[:, other]
    rest_ref[:, width + half :] = low_ref[:, other]
    rest_ref[:, :width] = mixed_ref[...]
    for copy in copies:
        copy.wait()
    mix_ref[...] = mm_nt(low_ref[...], weights_ref[3]).astype(BF16)

    def step(unit, _):
        image, rows, lane = unit_cuts(unit, width)
        queries = qkv_ref[rows, pl.ds(lane, GROUP)]
        keys = qkv_ref[rows, pl.ds(lane + width, GROUP)]
        values = qkv_ref[rows, pl.ds(lane + 2 * width, GROUP)]
        incoming = mix_ref[rows, pl.ds(lane, GROUP)]
        if windowed:
            mask = window_mask(place_ref, image)
            wide_queries = spread_heads(queries)
            wide_incoming = spread_heads(incoming)
            probs = window_probabilities(wide_queries, keys, mask)
            weights = probs.reshape(HEADS * CELLS, CELLS).astype(BF16)
            grad_probs = mm_nt(wide_incoming, values).reshape(HEADS, CELLS, CELLS)
            inner = jnp.sum(probs * grad_probs, axis=-1, keepdims=True)
            grad_scores = jnp.where(mask[None], probs * (grad_probs - inner), 0.0)
            grad_scores = grad_scores.reshape(HEADS * CELLS, CELLS).astype(BF16)
            grad_query = gather_heads(mm(grad_scores, keys)) * SCALE
            grad_keys = mm_tn(grad_scores, wide_queries) * SCALE
            grad_values = mm_tn(weights, wide_incoming)
        else:
            present = presence(place_ref, CELLS, image)
            kept = keys * present.astype(BF16)
            probs = channel_probabilities(kept, values)
            grad_probs = mm_tn(incoming, queries)
            inner = jnp.sum(probs * grad_probs, axis=-1, keepdims=True)
            grad_scores = (probs * (grad_probs - inner)).astype(BF16)
            grad_query = mm(incoming, probs.astype(BF16))
            grad_keys = mm_nt(values, grad_scores) * SCALE * present
            grad_values = mm(kept, grad_scores) * SCALE
        for m, item in enumerate((grad_query, grad_keys, grad_values)):
            left_ref[rows, pl.ds(lane + m * width, GROUP)] = item.astype(BF16)
        return 0

    lax.fori_loop(0, rows_all // CELLS * (width // GROUP), step, 0)
    total = None
    for m in range(3):
        rounded = left_ref[:, m * width : (m + 1) * width]
        bias_ref[m : m + 1, :] = jnp.sum(rounded.astype(F32), axis=0, keepdims=True)
        term = mm(rounded, weights_ref[m])
        total = term if total is None else total + term
    gain = table_ref[pl.ds((0 if windowed else 16) + 10, 1), :]
    out_ref[...] = grads_ref[...] + norm_back(total, values_ref[...], gain, little_ref)


def attention_back(windowed, place, grads, values, table, normed, qkv, mixed, parts):
    rows, width = values.shape
    outs = [
        struct((rows, width), F32),
        struct((rows, 3 * width), BF16),
        struct((rows, 2 * width), BF16),
        struct((rows, width), BF16),
        struct((3, width), F32),
        struct((3, width), F32),
    ]
    operands = [place, grads, values, table, normed, qkv, mixed, *parts]
    spaces = SMALL + [(7 + i, pltpu.HBM) for i in range(4)]
    scratch = [
        pltpu.VMEM((MATS, width, width), BF16),
        pltpu.VMEM((rows, width), BF16),
        pltpu.VMEM((rows, width), BF16),
        pltpu.SemaphoreType.DMA((32,)),
    ]
    return call(
        partial(attention_back_kernel, windowed), outs, operands, spaces=spaces, scratch=scratch,
    )


def head_grads_kernel(
    place_ref, left_ref, rest_ref, left_send_ref, rest_send_ref, right_ref, near_ref, far_ref, table_ref, other_ref
):
    wid = place_ref[1]
    width = right_ref.shape[1]
    half = width // 2
    for m in range(MATS):
        left, left_send = (left_ref, left_send_ref) if m < 3 else (rest_ref, rest_send_ref)
        cut = slice(m % 3 * width, (m % 3 + 1) * width)
        side = slice(0, half) if m < 3 else slice(half, width)
        beside = slice(width + side.start, width + side.stop)
        table_ref[...] = mm_tn(left[:, cut], right_ref[:, side])
        other_ref[...] = mm_tn(left_send[:, cut], rest_send_ref[:, beside])
        for line in range(4):
            out_ref = near_ref if line < 2 else far_ref
            for j in range(4):
                inner = jnp.bitwise_xor(wid, j) * 48
                mine = table_ref[pl.ds(pl.multiple_of(line * 192 + inner, 16), 48), :]
                other = other_ref[pl.ds(pl.multiple_of(SWAP[line] * 192 + inner, 16), 48), :]
                out_ref[(line % 2) * 4 + j, m] = (mine + other).astype(BF16)


def head_grads(place, left, rest, left_send, rest_send, right):
    width = right.shape[1]
    out = struct((8, MATS, width // 16, width // 2), BF16)
    return call(
        head_grads_kernel, [out, out], [place, left, rest, left_send, rest_send, right],
        SMALL, scratch=[pltpu.VMEM((width, width // 2), F32)] * 2,
    )


def pieces_kernel(place_ref, *refs):
    core = place_ref[0]
    weights, outs, sems = refs[:8], refs[8:12], refs[12]
    moves = []
    for index in range(2):
        inw, outw, up, down = weights[4 * index : 4 * index + 4]
        heads, units = outs[2 * index : 2 * index + 2]
        half = inw.shape[2] // 2
        columns = pl.ds(pl.multiple_of(core * half, half), half)
        moves.append((inw.at[:, :, columns], heads.at[0, pl.ds(0, 3)]))
        moves.append((outw.at[:, columns], heads.at[0, 3]))
        rows = up.shape[0] // 2
        own = pl.ds(pl.multiple_of(core * rows, rows), rows)
        moves.append((up.at[own, :], units.at[0, 0]))
        moves.append((down.at[own, :], units.at[0, 1]))
    copies = [pltpu.make_async_copy(*move, sems.at[index]) for index, move in enumerate(moves)]
    for copy in copies:
        copy.start()
    for copy in copies:
        copy.wait()


def pieces(place, *weights):
    inw, _, up, _ = weights[:4]
    heads = struct((1, MATS, inw.shape[1], inw.shape[2] // 2), BF16)
    units = struct((1, 2, up.shape[0] // 2, up.shape[1]), BF16)
    spaces = SMALL + [(1 + index, pltpu.HBM) for index in range(8)]
    scratch = [pltpu.SemaphoreType.DMA((8,))]
    return call(pieces_kernel, [heads, units, heads, units], [place, *weights], spaces, scratch)


def table_kernel(*refs):
    inputs, (table_ref, bias_ref) = refs[:20], refs[20:]
    for base in (0, 1):
        kernel, cbias, gain, shift, inb, outb, gain_two, shift_two, upb, downb = inputs[base * 10 : base * 10 + 10]
        table_ref[pl.ds(base * 16, 9), :] = kernel[...]
        for index, item in enumerate((cbias, gain, shift, outb, gain_two, shift_two, downb)):
            table_ref[pl.ds(base * 16 + 9 + index, 1), :] = item[...].reshape(1, -1)
        first = 0 if base == 0 else 6
        count = inb.shape[0]
        bias_ref[pl.ds(first, count), :] = inb[...]
        wide = upb[...].reshape(1, -1)
        step = wide.shape[1] // 4
        for index in range(4):
            bias_ref[pl.ds(first + count + index, 1), :] = wide[:, index * step : (index + 1) * step]
    bias_ref[pl.ds(13, 3), :] = jnp.zeros((3, bias_ref.shape[1]), F32)


def tables(*small):
    width = small[0].shape[1]
    return call(table_kernel, [struct((32, width), F32), struct((16, small[4].shape[1]), F32)], list(small))


def order_kernel(place_ref, g0, g1, g2, head_ref, hidden_ref):
    core, wid = place_ref[0], place_ref[1]
    hids = [g0, g1, g2.at[0], g2.at[1]]
    step = g0.shape[1]
    half = step // 2
    head_ref[...] = jnp.zeros_like(head_ref)
    hidden_ref[...] = jnp.zeros_like(hidden_ref)
    for row, source in ((0, 0), (2, 1), (3, 6), (4, 7), (5, 8)):
        for i in range(4):
            head_ref[row : row + 1, i * step : (i + 1) * step] = hids[i][source : source + 1, :]
    for index, first in ((0, 2), (1, 9)):
        for side in range(2):
            for i in range(4):
                hid = hids[i if side == 0 else SWAP[i]]
                for j in range(4):
                    line = hid[pl.ds(first + jnp.bitwise_xor(wid, j), 1), :]
                    value = jnp.where(core == side, line[:, :half], line[:, half:])
                    lane = side * 16 * half + (i * 4 + j) * half
                    hidden_ref[index : index + 1, lane : lane + half] = value


def order_biases(place, g0, g1, g2):
    step = g0.shape[1]
    outs = [struct((8, 4 * step), F32), struct((8, 16 * step), F32)]
    return call(order_kernel, outs, [place, g0, g1, g2], SMALL)


BIASES = 16


def small_kernel(counts, place_ref, *refs):
    out_ref = refs[-1]
    core, wid, hid = place_ref[0], place_ref[1], place_ref[2]
    out_ref[...] = jnp.zeros_like(out_ref)
    row = 0
    for count, ref in zip(counts, refs):
        out_ref[pl.ds(row, count), :] = ref[...]
        row += count
    base = out_ref.shape[0] - 2 * BIASES
    window_heads, channel_heads, *hiddens = refs[len(counts) : -1]
    step = window_heads.shape[1] // 4
    half = step // 2
    gap = jnp.zeros((1, 256 - step), F32)
    for i in range(4):
        owned = jnp.bitwise_xor(hid, jnp.where(core == 0, i, SWAP[i]))
        for j in range(4):
            parts = []
            for ref in hiddens:
                lane = (i * 4 + j) * half
                mine = ref[0:1, lane : lane + half]
                lane = 16 * half + (SWAP[i] * 4 + j) * half
                other = ref[0:1, lane : lane + half]
                parts += [jnp.where(core == 0, mine, other), jnp.where(core == 0, other, mine), gap]
            line = pl.ds(base + owned * 4 + jnp.bitwise_xor(wid, j), 1)
            out_ref[line, 0:512] = jnp.concatenate(parts, axis=1)
        for first, heads, kinds in ((base, channel_heads, (0, 1, 2)), (base + BIASES, window_heads, (0, 2))):
            for position, kind in enumerate(kinds):
                value = heads[kind : kind + 1, i * step : (i + 1) * step]
                line = pl.ds(first + owned * 4 + position, 1)
                out_ref[line, 512:768] = jnp.concatenate([value, gap], axis=1)


def small_table(place, rows, window_heads, channel_heads, hiddens):
    counts = [item.shape[0] for item in rows]
    total = (sum(counts) + 7) // 8 * 8 + 2 * BIASES
    return call(
        partial(small_kernel, counts), [struct((total, rows[0].shape[1]), F32)],
        [place, *rows, window_heads, channel_heads, *hiddens], SMALL,
    )[0]


def outputs_kernel(place_ref, table_ref, *outs):
    hid = place_ref[2]
    base = table_ref.shape[0] - 2 * BIASES
    plan = ((outs[:10], 0, 10, 13, base + BIASES, 0), (outs[10:], 16, 26, 29, base, 256))
    for refs, sums, one, two, heads, lane in plan:
        kernel, cbias, gain, shift, inb, outb, gain_two, shift_two, upb, downb = refs
        kernel[...] = table_ref[pl.ds(sums, 9), :]
        rows = (sums + 9, one, one + 1, one + 2, two, two + 1, two + 2)
        for ref, row in zip((cbias, gain, shift, outb, gain_two, shift_two, downb), rows):
            ref[...] = table_ref[pl.ds(row, 1), :].reshape(-1)
        step = inb.shape[1]
        for index in range(inb.shape[0]):
            inb[pl.ds(index, 1), :] = table_ref[pl.ds(heads + hid * 4 + index, 1), :][:, 512 : 512 + step]
        for index in range(4):
            line = table_ref[pl.ds(base + hid * 4 + index, 1), :]
            upb[pl.ds(index * step, step)] = line[:, lane : lane + step].reshape(-1)


def small_outputs(place, table):
    width = table.shape[1]
    step = width // 4
    outs = []
    for count in (2, 3):
        flat = struct((width,), F32)
        outs += [struct((9, width), F32), flat, flat, flat, struct((count, step), F32), flat, flat, flat, flat, flat]
    return call(outputs_kernel, outs, [place, table], SMALL)


def join_kernel(first_ref, second_ref, out_ref):
    count = first_ref.shape[0]
    out_ref[:count] = first_ref[...]
    out_ref[count:] = second_ref[...]


def join(first, second, wait=5):
    shape = (2 * first.shape[0], *first.shape[1:])
    return call(join_kernel, [struct(shape, first.dtype)], [first, second], flops=max(wait * WAIT, 1))[0]


def fold_kernel(kept_ref, arrived_ref, still_ref, sent_ref):
    half = still_ref.shape[0]
    still_ref[...] = kept_ref[:half].astype(F32) + arrived_ref[:half].astype(F32)
    sent_ref[...] = (kept_ref[half:].astype(F32) + arrived_ref[half:].astype(F32)).astype(BF16)


def fold(kept, arrived):
    shape = (kept.shape[0] // 2, *kept.shape[1:])
    return call(fold_kernel, [struct(shape, F32), struct(shape, BF16)], [kept, arrived], flops=5 * WAIT)


def total_kernel(kept_ref, arrived_ref, out_ref):
    out_ref[...] = kept_ref[0] + arrived_ref[0].astype(F32)


def fold_last(kept, arrived):
    return call(total_kernel, [struct(kept.shape[1:], F32)], [kept, arrived], flops=5 * WAIT)[0]


def rows_kernel(place_ref, own_ref, other_ref, *outs):
    rows = own_ref.shape[1]
    core = place_ref[0]
    for index, out_ref in enumerate(outs):
        out_ref[pl.ds(pl.multiple_of(core * rows, 8), rows), :] = own_ref[index]
        out_ref[pl.ds(pl.multiple_of((1 - core) * rows, 8), rows), :] = other_ref[index]


def both_rows(place, own, other):
    out = struct((2 * own.shape[1], own.shape[2]), F32)
    return call(rows_kernel, [out, out], [place, own, other], SMALL)


def columns_kernel(place_ref, own_ref, other_ref, in_ref, out_ref):
    half = own_ref.shape[2]
    core = place_ref[0]
    for turn, ref in ((core, own_ref), (1 - core, other_ref)):
        cut = pl.ds(pl.multiple_of(turn * half, 128), half)
        for m in range(3):
            in_ref[m, :, cut] = ref[m]
        out_ref[:, cut] = ref[3]


def both_columns(place, own, other):
    rows, width = own.shape[1], own.shape[2] * 2
    return call(
        columns_kernel, [struct((3, rows, width), F32), struct((rows, width), F32)], [place, own, other], SMALL
    )


def add_kernel(first_ref, second_ref, out_ref):
    out_ref[...] = first_ref[...] + second_ref[...]


def add(first, second):
    return call(add_kernel, [struct(first.shape, F32)], [first, second])[0]


class Line:
    def __init__(self, mark):
        self.mark = mark

    def gate(self, tree):
        tree, self.mark = lax.optimization_barrier((tree, self.mark))
        return tree

    def run(self, function, *operands):
        return self.gate(function(*self.gate(operands)))


class Scatter:
    def __init__(self, line, place, near, far, heads):
        self.line, self.place, self.kept, self.sent = line, place, near, far
        self.heads, self.step = heads, 0

    def advance(self):
        gate = self.line.gate
        if self.step in (1, 2, 3):
            self.kept, self.sent = self.line.run(fold, self.kept, self.flight)
        elif self.step == 4:
            self.kept = self.line.run(fold_last, self.kept, self.flight)
            bit = 2
            while bit < lax.axis_size("dp"):
                self.kept = self.line.run(add, self.kept, exchange(self.kept, "dp", bit))
                bit *= 2
        elif self.step == 5:
            join_cores = both_columns if self.heads else both_rows
            self.total = self.line.run(join_cores, self.place, self.kept, self.flight)
        if self.step < 4:
            self.sent = gate(self.sent)
        if self.step == 0:
            self.flight = cross(self.sent, False)
        elif self.step == 1:
            self.flight = cross(self.sent, True)
        elif self.step == 2:
            self.flight = exchange(self.sent, "wid", 2)
        elif self.step == 3:
            self.flight = exchange(self.sent, "wid", 1)
        elif self.step == 4:
            self.flight = sibling(gate(self.kept))
        self.step += 1


class Small:
    def __init__(self, line, table):
        self.line, self.table, self.flight = line, table, None
        self.steps = []
        for axis in ("dp", "hid", "wid"):
            bit = 1
            while bit < lax.axis_size(axis):
                self.steps.append((axis, bit))
                bit *= 2

    def advance(self):
        if self.flight is not None:
            self.table = self.line.run(add, self.table, self.flight)
            self.flight = None
        if self.steps:
            axis, bit = self.steps.pop(0)
            self.table = self.line.gate(self.table)
            self.flight = exchange(self.table, axis, bit)
            return True
        return False


def body(
    inputs, grid_sizes, cotangent,
    wkernel, wcbias, wgain, wshift, winw, winb, woutw, woutb,
    wgain_two, wshift_two, wupw, wupb, wdownw, wdownb,
    ckernel, ccbias, cgain, cshift, cinw, cinb, coutw, coutb,
    cgain_two, cshift_two, cupw, cupb, cdownw, cdownb,
):
    image_count = inputs.shape[0] // (PADDED * PADDED)
    hid, wid = lax.axis_index("hid"), lax.axis_index("wid")
    own_sizes = lax.dynamic_slice_in_dim(
        grid_sizes, (hid * lax.axis_size("wid") + wid) * image_count, image_count, 0
    )
    at = jnp.stack([lax.rem(lax.axis_index("dp"), 2), wid, hid]).astype(jnp.int32)
    place = jnp.concatenate([at, own_sizes])
    line = Line(winb[0, 0])

    def send(move, values):
        return move(line.gate(values))

    def w1(values):
        return exchange(values, "wid", 1)

    def w2(values):
        return exchange(values, "wid", 2)

    def h1(values):
        return cross(values, True)

    def h2(values):
        return cross(values, False)

    gate = line.gate

    def both(near, arrived, wait=5):
        return line.run(partial(join, wait=wait), near, arrived)

    own0, own1, own2, own3 = pieces(place, winw, woutw, wupw, wdownw, cinw, coutw, cupw, cdownw)

    w1_0 = send(w1, own0)
    table, bias = line.run(
        tables, wkernel, wcbias, wgain, wshift, winb, woutb, wgain_two, wshift_two, wupb, wdownb,
        ckernel, ccbias, cgain, cshift, cinb, coutb, cgain_two, cshift_two, cupb, cdownb,
    )
    near0 = both(own0, w1_0)
    w2_0 = send(w2, near0)
    w1_1 = send(w1, own1)
    bias_one = send(h1, bias)
    start, after_conv = line.run(partial(first_conv, 0), place, inputs, table)
    cotangent = line.run(cells, cotangent)
    bias_one = gate(bias_one)
    bias_two = send(h2, jnp.stack([bias, bias_one]))
    near1 = both(own1, w1_1)
    bias_two = gate(bias_two)
    head_bias, hidden_bias = line.run(order_biases, place, bias, bias_one, bias_two)
    near0 = both(near0, w2_0)
    h1_0 = send(h1, near0)
    w2_1 = send(w2, near1)
    near0 = both(near0, h1_0, 0)
    h2_0 = send(h2, near0)
    near1 = both(near1, w2_1, 9)
    h1_1 = send(h1, near1)
    w1_2 = send(w1, own2)
    far0 = gate(h2_0)
    s_0 = send(sibling, near0), send(sibling, far0)
    near2 = both(own2, w1_2)
    w2_2 = send(w2, near2)
    s_0 = gate(s_0)
    att_one = [near0, far0, *s_0]
    after_attn, normed_one, qkv_one, mixed_one = line.run(
        partial(attention, True), place, after_conv, table, head_bias, att_one
    )
    near1 = both(near1, h1_1)
    h2_1 = send(h2, near1)
    near2 = both(near2, w2_2)
    h1_2 = send(h1, near2)
    w1_3 = send(w1, own3)
    near3 = both(own3, w1_3)
    w2_3 = send(w2, near3)
    near2 = both(near2, h1_2)
    h2_2 = send(h2, near2)
    near3 = both(near3, w2_3)
    h1_3 = send(h1, near3)
    far1 = gate(h2_1)
    far2 = gate(h2_2)
    s_1 = send(sibling, near1), send(sibling, far1)
    near3 = both(near3, h1_3)
    h2_3 = send(h2, near3)
    s_1 = gate(s_1)
    mlp_two = [near1, far1, *s_1]
    after_mlp, acted_two, fpack_two, deriv_two = line.run(
        partial(mlp, 0), place, after_attn, table, hidden_bias, mlp_two
    )
    s_2 = send(sibling, near2), send(sibling, far2)
    after_conv_c = line.run(partial(conv, 16), place, after_mlp, table)
    s_2 = gate(s_2)
    s_3 = send(sibling, near3)
    att_three = [near2, far2, *s_2]
    after_attn_c, normed_three, qkv_three, mixed_three = line.run(
        partial(attention, False), place, after_conv_c, table, head_bias, att_three
    )
    s_3 = gate(s_3)
    fpack_two_other = gate(send(sibling, fpack_two))
    far3 = gate(h2_3)
    s_far3 = gate(send(sibling, far3))
    mlp_four = [near3, far3, s_3, s_far3]
    outputs, acted_four, fpack_four, deriv_four = line.run(
        partial(mlp, 16), place, after_attn_c, table, hidden_bias, mlp_four
    )

    def scatter(near, far, heads):
        group = Scatter(line, place, near, far, heads)
        group.advance()
        return group

    fpack_four_other = send(sibling, fpack_four)
    flowing, gh_four, bpack_four, little_four, upb_four = line.run(
        partial(mlp_back, 16), place, cotangent, after_attn_c, table, deriv_four, mlp_four
    )
    fpack_four_other = gate(fpack_four_other)
    bpack_four_other = gate(send(sibling, bpack_four))
    m_four = scatter(
        *line.run(pair_grads, acted_four, fpack_four, fpack_four_other, gh_four, bpack_four, bpack_four_other), False
    )
    flowing, left_three, rest_three, mine_three, little_three, inb_three = line.run(
        partial(attention_back, False),
        place, flowing, after_conv_c, table, normed_three, qkv_three, mixed_three, att_three,
    )
    sent_three = gate((send(sibling, left_three), send(sibling, rest_three)))
    near_far = line.run(head_grads, place, left_three, rest_three, *sent_three, mine_three)
    m_four.advance()
    a_three = scatter(*near_far, True)
    flowing, sums_three = line.run(partial(conv_back, 16, False), place, flowing, after_mlp, table)
    flowing, gh_two, bpack_two, little_two, upb_two = line.run(
        partial(mlp_back, 0), place, flowing, after_attn, table, deriv_two, mlp_two
    )
    m_four.advance()
    bpack_two_other = gate(send(sibling, bpack_two))
    near_far = line.run(pair_grads, acted_two, fpack_two, fpack_two_other, gh_two, bpack_two, bpack_two_other)
    a_three.advance()
    m_two = scatter(*near_far, False)
    flowing, left_one, rest_one, mine_one, little_one, inb_one = line.run(
        partial(attention_back, True),
        place, flowing, after_conv, table, normed_one, qkv_one, mixed_one, att_one,
    )
    a_three.advance()
    m_four.advance()
    sent_one = gate((send(sibling, left_one), send(sibling, rest_one)))
    near_far = line.run(head_grads, place, left_one, rest_one, *sent_one, mine_one)
    m_two.advance()
    input_grad, sums_one = line.run(partial(conv_back, 0, True), place, flowing, start, table)
    small = line.run(
        small_table, place, [sums_one, little_one, little_two, sums_three, little_three, little_four],
        inb_one, inb_three, [upb_two, upb_four],
    )
    m_two.advance()
    a_one = scatter(*near_far, True)
    m_four.advance()
    a_three.advance()
    small = Small(line, small)
    small.advance()
    m_four.advance()
    small.advance()
    a_three.advance()
    a_one.advance()
    small.advance()
    a_three.advance()
    a_one.advance()
    m_two.advance()
    small.advance()
    m_two.advance()
    small.advance()
    a_one.advance()
    m_two.advance()
    a_one.advance()
    small.advance()
    a_one.advance()
    small = line.run(small_outputs, place, small.table)

    def ordered(small, attention, units):
        return (
            *small[:4], attention[0], small[4], attention[1], *small[5:8], units[0], small[8], units[1], small[9]
        )

    return (
        outputs, input_grad,
        *ordered(small[:10], a_one.total, m_two.total),
        *ordered(small[10:], a_three.total, m_four.total),
    )


def solution(mesh):
    tokens, everywhere = P(("dp", "hid", "wid"), None), P()
    stacked, rows = P(None, ("hid", "wid"), None), P(("hid", "wid"), None)
    block = (
        everywhere, everywhere, everywhere, everywhere, stacked, P(None, "hid"), rows, everywhere,
        everywhere, everywhere, rows, P("hid"), rows, everywhere,
    )
    return jax.shard_map(
        body,
        mesh=mesh,
        in_specs=(tokens, P("dp"), tokens) + block + block,
        out_specs=(tokens, tokens) + block + block,
        check_vma=False,
    )
```

```python
from functools import partial

import jax
import jax.numpy as jnp
from jax import lax
from jax.experimental import pallas as pl
from jax.experimental.pallas import tpu as pltpu
from jax.sharding import PartitionSpec as P

HD = 32
WINDOW = 7
PADDED = 14
GRID = 12
CELLS = GRID * GRID
EPSILON = 1e-05
F32 = jnp.float32
BF16 = jnp.bfloat16
SCALE = HD ** (-0.5)


def exchange(values, axis, bit):
    pairs = [(index, index ^ bit) for index in range(lax.axis_size(axis))]
    return lax.ppermute(values, axis, pairs)


def sibling(values):
    return exchange(values, "dp", 1)


def cross(values, first):
    hids = lax.axis_size("hid")
    pairs = []
    for core in range(lax.axis_size("dp")):
        bit = 1 if (core % 2 == 0) == first else 2
        pairs += [(core * hids + index, core * hids + (index ^ bit)) for index in range(hids)]
    return lax.ppermute(values, ("dp", "hid"), pairs)


def second_core():
    return lax.rem(lax.axis_index("dp"), 2) == 1


def by_core(own, other, axis):
    second = second_core()
    return jnp.concatenate(
        [jnp.where(second, other, own), jnp.where(second, own, other)], axis=axis
    )


VMEM_LIMIT = 16 * 1024 * 1024
GROUP = 256
WAIT = 1_000_000_000
FOLD = 5
HEADS = GROUP // HD


def call(kernel, outs, operands, spaces=(), scratch=(), flops=1, limit=VMEM_LIMIT):
    vmem = pl.BlockSpec(memory_space=pltpu.VMEM)
    specs = [vmem] * len(operands)
    for index, space in spaces:
        specs[index] = pl.BlockSpec(memory_space=space)
    return pl.pallas_call(
        kernel,
        out_shape=list(outs),
        in_specs=specs,
        out_specs=[vmem] * len(outs),
        scratch_shapes=list(scratch),
        compiler_params=pltpu.CompilerParams(vmem_limit_bytes=limit),
        cost_estimate=pl.CostEstimate(flops=flops, bytes_accessed=1, transcendentals=0),
    )(*operands)


def struct(shape, dtype):
    return jax.ShapeDtypeStruct(shape, dtype)


def mm(left, right):
    return jnp.dot(left, right, preferred_element_type=F32)


def mm_nt(left, right):
    return lax.dot_general(left, right, (((1,), (1,)), ((), ())), preferred_element_type=F32)


def mm_tn(left, right):
    return lax.dot_general(left, right, (((0,), (0,)), ((), ())), preferred_element_type=F32)


def normalize(values):
    center = jnp.mean(values, axis=1, keepdims=True)
    spread = jnp.mean(values * values, axis=1, keepdims=True) - center * center
    scaled = lax.rsqrt(spread + EPSILON)
    return (values - center) * scaled, scaled


def cells_of(rows):
    cell = lax.broadcasted_iota(jnp.int32, (rows, 1), 0)
    column = lax.rem(cell, GRID)
    line = lax.rem(lax.div(cell, GRID), GRID)
    return line, column


def shift_columns(values):
    rows = values.shape[0]
    _, column = cells_of(rows)
    before = jnp.where(column != 0, pltpu.roll(values, 1, 0), 0.0)
    after = jnp.where(column != GRID - 1, pltpu.roll(values, rows - 1, 0), 0.0)
    return before, after


def shift_lines(values, ahead):
    rows = values.shape[0]
    line, _ = cells_of(rows)
    if ahead:
        return jnp.where(line != GRID - 1, pltpu.roll(values, rows - GRID, 0), 0.0)
    return jnp.where(line != 0, pltpu.roll(values, GRID, 0), 0.0)


def convolve(values, taps):
    before, after = shift_columns(values)
    lines = [
        before * taps[3 * a] + values * taps[3 * a + 1] + after * taps[3 * a + 2] for a in range(3)
    ]
    return shift_lines(lines[0], False) + lines[1] + shift_lines(lines[2], True)


def presence(place_ref, rows, image=None):
    line, column = cells_of(rows)
    if image is not None:
        side = place_ref[3 + image]
    else:
        cell = lax.broadcasted_iota(jnp.int32, (rows, 1), 0)
        side = jnp.zeros((rows, 1), jnp.int32) + place_ref[3]
        for index in range(1, rows // CELLS):
            side = jnp.where(cell >= index * CELLS, place_ref[3 + index], side)
    return jnp.where((line < side) & (column < side), 1.0, 0.0).astype(F32)


def window_mask(place_ref, image):
    side = place_ref[3 + image]
    query = lax.broadcasted_iota(jnp.int32, (CELLS, 1), 0)
    key = lax.broadcasted_iota(jnp.int32, (1, CELLS), 1)
    line, column = lax.div(key, GRID), lax.rem(key, GRID)
    kept = (line < side) & (column < side)

    def window(cell):
        below = lax.div(cell, GRID) >= WINDOW
        right = lax.rem(cell, GRID) >= WINDOW
        return jnp.where(below, 2, 0) + jnp.where(right, 1, 0)

    own = jnp.where(kept, window(key), -1)
    return window(query) == own


LANES = 256


def pack_cells(slots_ref, cells_ref):
    for image in range(cells_ref.shape[0] // CELLS):
        for line in range(GRID):
            cells_ref[pl.ds(image * CELLS + line * GRID, GRID), :] = slots_ref[
                pl.ds((image * PADDED + line) * PADDED, GRID), :
            ]


def unpack_cells(cells_ref, slots_ref):
    slots_ref[...] = jnp.zeros_like(slots_ref)
    for image in range(cells_ref.shape[0] // CELLS):
        for line in range(GRID):
            slots_ref[pl.ds((image * PADDED + line) * PADDED, GRID), :] = cells_ref[
                pl.ds(image * CELLS + line * GRID, GRID), :
            ]


def conv_lanes(values, present, table_ref, base, cut):
    taps = [table_ref[pl.ds(base + i, 1), cut] for i in range(9)]
    return values + present * (convolve(values, taps) + table_ref[pl.ds(base + 9, 1), cut])


def conv_kernel(base, place_ref, values_ref, table_ref, out_ref):
    present = presence(place_ref, values_ref.shape[0])
    for lane in range(0, values_ref.shape[1], LANES):
        cut = pl.ds(lane, LANES)
        out_ref[:, cut] = conv_lanes(values_ref[:, cut], present, table_ref, base, cut)


def first_conv_kernel(base, place_ref, slots_ref, table_ref, start_ref, out_ref):
    pack_cells(slots_ref, start_ref)
    present = presence(place_ref, start_ref.shape[0])
    for lane in range(0, start_ref.shape[1], LANES):
        cut = pl.ds(lane, LANES)
        values = start_ref[:, cut] * present
        start_ref[:, cut] = values
        out_ref[:, cut] = conv_lanes(values, present, table_ref, base, cut)


def conv_back_kernel(base, place_ref, grads_ref, values_ref, table_ref, out_ref, sums_ref, *rest):
    present = presence(place_ref, grads_ref.shape[0])
    target = rest[0] if rest else out_ref
    for lane in range(0, grads_ref.shape[1], LANES):
        cut = pl.ds(lane, LANES)
        grads = grads_ref[:, cut]
        masked = grads * present
        taps = [table_ref[pl.ds(base + 8 - i, 1), cut] for i in range(9)]
        flowing = grads + convolve(masked, taps)
        target[:, cut] = flowing * present if rest else flowing
        values = values_ref[:, cut]
        before, after = shift_columns(values)
        behind = shift_lines(masked, False)
        ahead = shift_lines(masked, True)
        for a, moved in enumerate((ahead, masked, behind)):
            for e, source in enumerate((before, values, after)):
                sums_ref[pl.ds(3 * a + e, 1), cut] = jnp.sum(moved * source, axis=0, keepdims=True)
        sums_ref[pl.ds(9, 1), cut] = jnp.sum(masked, axis=0, keepdims=True)
    if rest:
        unpack_cells(target, out_ref)


SMALL = [(0, pltpu.SMEM)]


def conv(base, place, values, table):
    return call(partial(conv_kernel, base), [struct(values.shape, F32)], [place, values, table], SMALL)[0]


def first_conv(base, place, slots, table):
    cells = struct((slots.shape[0] // (PADDED * PADDED) * CELLS, slots.shape[1]), F32)
    return call(partial(first_conv_kernel, base), [cells, cells], [place, slots, table], SMALL)


def conv_back(base, last, place, grads, values, table):
    rows, width = grads.shape
    images = rows // CELLS
    out = struct((images * PADDED * PADDED if last else rows, width), F32)
    scratch = [pltpu.VMEM((rows, width), F32)] if last else []
    return call(
        partial(conv_back_kernel, base), [out, struct((10, width), F32)], [place, grads, values, table],
        SMALL, scratch=scratch,
    )


def cells(slots):
    shape = (slots.shape[0] // (PADDED * PADDED) * CELLS, slots.shape[1])
    return call(pack_cells, [struct(shape, F32)], [slots])[0]


UNITS = 768


def tile(part, which):
    return part[:, which].reshape(-1, part.shape[-1])


def mlp_kernel(base_row, place_ref, values_ref, table_ref, upbias_ref, p0, p1, p2, p3, *rest):
    last = base_row != 0
    gain, shift, downbias = (table_ref[pl.ds(base_row + i, 1), :] for i in (13, 14, 15))
    ubias = 1 if last else 0
    out_ref, acted_ref, send_ref, deriv_ref, total_ref = rest[:5]
    values = values_ref[...]
    normal, _ = normalize(values)
    half = 2 * UNITS
    send_ref[:, half:] = (normal * gain + shift).astype(BF16)
    for index, part in enumerate((p0, p1, p2, p3)):
        target = acted_ref if index < 2 else send_ref
        base = (index % 2) * UNITS
        here = slice(index * UNITS, (index + 1) * UNITS)
        there = slice(base, base + UNITS)
        hidden = mm_nt(send_ref[:, half:], tile(part, 0)) + upbias_ref[ubias : ubias + 1, here]
        below = 0.5 + 0.5 * lax.erf(hidden * (0.5**0.5))
        target[:, there] = (hidden * below).astype(BF16)
        bell = jnp.exp(hidden * hidden * -0.5) * 0.3989422804014327
        deriv_ref[:, here] = below + hidden * bell
        term = mm(target[:, there], tile(part, 1))
        total_ref[...] = term if index == 0 else total_ref[...] + term
    result = values + presence(place_ref, values.shape[0]) * (total_ref[...] + downbias)
    if last:
        rest[5][...] = result
        unpack_cells(rest[5], out_ref)
    else:
        out_ref[...] = result


def mlp(base, place, values, table, upbias, parts):
    last = base != 0
    rows, width = values.shape
    images = rows // CELLS
    half = 2 * UNITS
    outs = [
        struct((images * PADDED * PADDED if last else rows, width), F32),
        struct((rows, half), BF16),
        struct((rows, half + width), BF16),
        struct((rows, 2 * half), F32),
    ]
    scratch = [pltpu.VMEM((rows, width), F32)] * (2 if last else 1)
    operands = [place, values, table, upbias, *parts]
    return call(partial(mlp_kernel, base), outs, operands, SMALL, scratch=scratch)


def norm_back(dn, values, gain, little_ref):
    normal, scaled = normalize(values)
    little_ref[0:1, :] = jnp.sum(dn * normal, axis=0, keepdims=True)
    little_ref[1:2, :] = jnp.sum(dn, axis=0, keepdims=True)
    grad_normal = dn * gain
    first = jnp.mean(grad_normal, axis=1, keepdims=True)
    second = jnp.mean(grad_normal * normal, axis=1, keepdims=True)
    return scaled * (grad_normal - first - normal * second)


def mlp_back_kernel(
    base_row, place_ref, grads_ref, values_ref, table_ref, deriv_ref, p0, p1, p2, p3,
    out_ref, hidden_ref, send_ref, low_ref, little_ref, bias_ref, total_ref,
):
    branch = grads_ref[...] * presence(place_ref, grads_ref.shape[0])
    little_ref[2:3, :] = jnp.sum(branch, axis=0, keepdims=True)
    low_ref[...] = branch.astype(BF16)
    for index, part in enumerate((p0, p1, p2, p3)):
        target = hidden_ref if index < 2 else send_ref
        base = (index % 2) * UNITS
        here = slice(index * UNITS, (index + 1) * UNITS)
        there = slice(base, base + UNITS)
        acted = mm_nt(low_ref[...], tile(part, 1))
        hidden = (acted * deriv_ref[:, here]).astype(BF16)
        target[:, there] = hidden
        bias_ref[:, here] = jnp.sum(hidden.astype(F32), axis=0, keepdims=True)
        term = mm(target[:, there], tile(part, 0))
        total_ref[...] = term if index == 0 else total_ref[...] + term
    gain = table_ref[pl.ds(base_row + 13, 1), :]
    out_ref[...] = grads_ref[...] + norm_back(total_ref[...], values_ref[...], gain, little_ref)


def mlp_back(base, place, grads, values, table, deriv, parts):
    rows, width = values.shape
    half = 2 * UNITS
    outs = [
        struct((rows, width), F32),
        struct((rows, half), BF16),
        struct((rows, half), BF16),
        struct((rows, width), BF16),
        struct((3, width), F32),
        struct((1, 2 * half), F32),
    ]
    scratch = [pltpu.VMEM((rows, width), F32)]
    operands = [place, grads, values, table, deriv, *parts]
    return call(partial(mlp_back_kernel, base), outs, operands, SMALL, scratch=scratch)


def pair_grads_kernel(
    acted_ref, normed_ref, normed_send_ref, hidden_ref, branch_ref, hidden_send_ref, branch_send_ref, near_ref, far_ref
):
    half = 2 * UNITS
    for index, out_ref in enumerate((near_ref, far_ref)):
        cut = slice(index * UNITS, (index + 1) * UNITS)
        up = mm_tn(hidden_ref[:, cut], normed_ref[:, half:])
        up = up + mm_tn(hidden_send_ref[:, cut], normed_send_ref[:, half:])
        out_ref[:, 0] = up.astype(BF16).reshape(8, -1, up.shape[1])
        down = mm_tn(acted_ref[:, cut], branch_ref[...])
        down = down + mm_tn(normed_send_ref[:, cut], branch_send_ref[...])
        out_ref[:, 1] = down.astype(BF16).reshape(8, -1, down.shape[1])


def pair_grads(*operands):
    width = operands[4].shape[1]
    out = struct((8, 2, UNITS // 8, width), BF16)
    return call(pair_grads_kernel, [out, out], list(operands))


MATS = 4
SWAP = (0, 2, 1, 3)


def load_weights(place_ref, parts, weights_ref, sems):
    core, wid = place_ref[0], place_ref[1]
    copies = []
    for index, part in enumerate(parts):
        side = index // 2
        turn = core if side == 0 else 1 - core
        columns = pl.ds(pl.multiple_of(turn * 384, 384), 384)
        for i in range(2):
            line = 2 * (index % 2) + i
            order = line if side == 0 else SWAP[line]
            for j in range(4):
                first = pl.multiple_of(order * 192 + jnp.bitwise_xor(wid, SWAP[j]) * 48, 16)
                copies.append(
                    pltpu.make_async_copy(
                        part.at[i * 4 + j],
                        weights_ref.at[:, pl.ds(first, 48), columns],
                        sems.at[len(copies)],
                    )
                )
    for copy in copies:
        copy.start()
    return copies


def spread_heads(block):
    lane_head = lax.broadcasted_iota(jnp.int32, (1, GROUP), 1) // HD
    zero = jnp.zeros_like(block)
    return jnp.concatenate([jnp.where(lane_head == h, block, zero) for h in range(HEADS)], axis=0)


def gather_heads(wide):
    lane_head = lax.broadcasted_iota(jnp.int32, (1, GROUP), 1) // HD
    rows = wide.shape[0] // HEADS
    total = jnp.where(lane_head == 0, wide[:rows], 0.0)
    for h in range(1, HEADS):
        total = jnp.where(lane_head == h, wide[h * rows : (h + 1) * rows], total)
    return total


def window_probabilities(queries, keys, mask):
    scores = mm_nt(queries, keys) * SCALE
    scores = scores.reshape(HEADS, CELLS, CELLS)
    scores = jnp.where(mask[None], scores, -1000000000.0)
    raised = jnp.exp(scores - jnp.max(scores, axis=-1, keepdims=True))
    return raised * (1.0 / jnp.sum(raised, axis=-1, keepdims=True))


def channel_probabilities(keys, values):
    scores = mm_tn(keys, values) * SCALE
    line = lax.broadcasted_iota(jnp.int32, (GROUP, GROUP), 0) // HD
    column = lax.broadcasted_iota(jnp.int32, (GROUP, GROUP), 1) // HD
    scores = jnp.where(line == column, scores, -jnp.inf)
    raised = jnp.exp(scores - jnp.max(scores, axis=-1, keepdims=True))
    return raised * (1.0 / jnp.sum(raised, axis=-1, keepdims=True))


def unit_cuts(unit, width):
    groups = width // GROUP
    image = lax.div(unit, groups)
    rows = pl.ds(pl.multiple_of(image * CELLS, 16), CELLS)
    lane = pl.multiple_of(lax.rem(unit, groups) * GROUP, GROUP)
    return image, rows, lane


def attention_kernel(
    windowed, place_ref, values_ref, table_ref, bias_ref,
    p0, p1, p2, p3, out_ref, normed_ref, qkv_ref, mixed_ref, weights_ref, sems,
):
    copies = load_weights(place_ref, (p0, p1, p2, p3), weights_ref, sems)
    rows_all, width = values_ref.shape
    base = 0 if windowed else 16
    gain, shift, outbias = (table_ref[pl.ds(base + i, 1), :] for i in (10, 11, 12))
    first_bias = 0 if windowed else 3
    normal, _ = normalize(values_ref[...])
    normed_ref[...] = (normal * gain + shift).astype(BF16)
    for copy in copies:
        copy.wait()
    for m in range(3):
        projected = mm_nt(normed_ref[...], weights_ref[m])
        projected = projected + bias_ref[pl.ds(first_bias + m, 1), :]
        qkv_ref[:, m * width : (m + 1) * width] = projected.astype(BF16)

    def step(unit, _):
        image, rows, lane = unit_cuts(unit, width)
        queries = qkv_ref[rows, pl.ds(lane, GROUP)]
        keys = qkv_ref[rows, pl.ds(lane + width, GROUP)]
        values = qkv_ref[rows, pl.ds(lane + 2 * width, GROUP)]
        if windowed:
            probs = window_probabilities(spread_heads(queries), keys, window_mask(place_ref, image))
            weights = probs.reshape(HEADS * CELLS, CELLS).astype(BF16)
            mixed = gather_heads(mm(weights, values))
        else:
            kept = keys * presence(place_ref, CELLS, image).astype(BF16)
            weights = channel_probabilities(kept, values).astype(BF16)
            mixed = mm_nt(queries, weights)
        mixed_ref[rows, pl.ds(lane, GROUP)] = mixed.astype(BF16)
        return 0

    lax.fori_loop(0, rows_all // CELLS * (width // GROUP), step, 0)
    branch = mm(mixed_ref[...], weights_ref[3]) + outbias
    out_ref[...] = values_ref[...] + presence(place_ref, rows_all) * branch


def attention(windowed, place, values, table, bias, parts):
    rows, width = values.shape
    outs = [
        struct((rows, width), F32),
        struct((rows, width), BF16),
        struct((rows, 3 * width), BF16),
        struct((rows, width), BF16),
    ]
    operands = [place, values, table, bias, *parts]
    spaces = SMALL + [(4 + i, pltpu.HBM) for i in range(4)]
    scratch = [pltpu.VMEM((MATS, width, width), BF16), pltpu.SemaphoreType.DMA((32,))]
    return call(
        partial(attention_kernel, windowed), outs, operands, spaces=spaces, scratch=scratch,
    )


def attention_back_kernel(
    windowed, place_ref, grads_ref, values_ref, table_ref, normed_ref, qkv_ref, mixed_ref,
    p0, p1, p2, p3, out_ref, left_ref, rest_ref, mine_ref, little_ref, bias_ref,
    weights_ref, low_ref, mix_ref, sems,
):
    copies = load_weights(place_ref, (p0, p1, p2, p3), weights_ref, sems)
    rows_all, width = values_ref.shape
    half = width // 2
    core = place_ref[0]
    own = pl.ds(pl.multiple_of(core * half, half), half)
    other = pl.ds(pl.multiple_of((1 - core) * half, half), half)
    branch = grads_ref[...] * presence(place_ref, rows_all)
    little_ref[2:3, :] = jnp.sum(branch, axis=0, keepdims=True)
    low_ref[...] = branch.astype(BF16)
    mine_ref[:, :half] = normed_ref[:, own]
    mine_ref[:, half:] = low_ref[:, own]
    rest_ref[:, width : width + half] = normed_ref[:, other]
    rest_ref[:, width + half :] = low_ref[:, other]
    rest_ref[:, :width] = mixed_ref[...]
    for copy in copies:
        copy.wait()
    mix_ref[...] = mm_nt(low_ref[...], weights_ref[3]).astype(BF16)

    def step(unit, _):
        image, rows, lane = unit_cuts(unit, width)
        queries = qkv_ref[rows, pl.ds(lane, GROUP)]
        keys = qkv_ref[rows, pl.ds(lane + width, GROUP)]
        values = qkv_ref[rows, pl.ds(lane + 2 * width, GROUP)]
        incoming = mix_ref[rows, pl.ds(lane, GROUP)]
        if windowed:
            mask = window_mask(place_ref, image)
            wide_queries = spread_heads(queries)
            wide_incoming = spread_heads(incoming)
            probs = window_probabilities(wide_queries, keys, mask)
            weights = probs.reshape(HEADS * CELLS, CELLS).astype(BF16)
            grad_probs = mm_nt(wide_incoming, values).reshape(HEADS, CELLS, CELLS)
            inner = jnp.sum(probs * grad_probs, axis=-1, keepdims=True)
            grad_scores = jnp.where(mask[None], probs * (grad_probs - inner), 0.0)
            grad_scores = grad_scores.reshape(HEADS * CELLS, CELLS).astype(BF16)
            grad_query = gather_heads(mm(grad_scores, keys)) * SCALE
            grad_keys = mm_tn(grad_scores, wide_queries) * SCALE
            grad_values = mm_tn(weights, wide_incoming)
        else:
            present = presence(place_ref, CELLS, image)
            kept = keys * present.astype(BF16)
            probs = channel_probabilities(kept, values)
            grad_probs = mm_tn(incoming, queries)
            inner = jnp.sum(probs * grad_probs, axis=-1, keepdims=True)
            grad_scores = (probs * (grad_probs - inner)).astype(BF16)
            grad_query = mm(incoming, probs.astype(BF16))
            grad_keys = mm_nt(values, grad_scores) * SCALE * present
            grad_values = mm(kept, grad_scores) * SCALE
        for m, item in enumerate((grad_query, grad_keys, grad_values)):
            left_ref[rows, pl.ds(lane + m * width, GROUP)] = item.astype(BF16)
        return 0

    lax.fori_loop(0, rows_all // CELLS * (width // GROUP), step, 0)
    total = None
    for m in range(3):
        rounded = left_ref[:, m * width : (m + 1) * width]
        bias_ref[m : m + 1, :] = jnp.sum(rounded.astype(F32), axis=0, keepdims=True)
        term = mm(rounded, weights_ref[m])
        total = term if total is None else total + term
    gain = table_ref[pl.ds((0 if windowed else 16) + 10, 1), :]
    out_ref[...] = grads_ref[...] + norm_back(total, values_ref[...], gain, little_ref)


def attention_back(windowed, place, grads, values, table, normed, qkv, mixed, parts):
    rows, width = values.shape
    outs = [
        struct((rows, width), F32),
        struct((rows, 3 * width), BF16),
        struct((rows, 2 * width), BF16),
        struct((rows, width), BF16),
        struct((3, width), F32),
        struct((3, width), F32),
    ]
    operands = [place, grads, values, table, normed, qkv, mixed, *parts]
    spaces = SMALL + [(7 + i, pltpu.HBM) for i in range(4)]
    scratch = [
        pltpu.VMEM((MATS, width, width), BF16),
        pltpu.VMEM((rows, width), BF16),
        pltpu.VMEM((rows, width), BF16),
        pltpu.SemaphoreType.DMA((32,)),
    ]
    return call(
        partial(attention_back_kernel, windowed), outs, operands, spaces=spaces, scratch=scratch,
    )


def head_grads_kernel(
    place_ref, left_ref, rest_ref, left_send_ref, rest_send_ref, right_ref, near_ref, far_ref, table_ref, other_ref
):
    wid = place_ref[1]
    width = right_ref.shape[1]
    half = width // 2
    for m in range(MATS):
        left, left_send = (left_ref, left_send_ref) if m < 3 else (rest_ref, rest_send_ref)
        cut = slice(m % 3 * width, (m % 3 + 1) * width)
        side = slice(0, half) if m < 3 else slice(half, width)
        beside = slice(width + side.start, width + side.stop)
        table_ref[...] = mm_tn(left[:, cut], right_ref[:, side])
        other_ref[...] = mm_tn(left_send[:, cut], rest_send_ref[:, beside])
        for line in range(4):
            out_ref = near_ref if line < 2 else far_ref
            for j in range(4):
                inner = jnp.bitwise_xor(wid, SWAP[j]) * 48
                mine = table_ref[pl.ds(pl.multiple_of(line * 192 + inner, 16), 48), :]
                other = other_ref[pl.ds(pl.multiple_of(SWAP[line] * 192 + inner, 16), 48), :]
                out_ref[(line % 2) * 4 + j, m] = (mine + other).astype(BF16)


def head_grads(place, left, rest, left_send, rest_send, right):
    width = right.shape[1]
    out = struct((8, MATS, width // 16, width // 2), BF16)
    return call(
        head_grads_kernel, [out, out], [place, left, rest, left_send, rest_send, right],
        SMALL, scratch=[pltpu.VMEM((width, width // 2), F32)] * 2,
    )


def pieces_kernel(place_ref, *refs):
    core = place_ref[0]
    weights, outs, sems = refs[:8], refs[8:12], refs[12]
    moves = []
    for index in range(2):
        inw, outw, up, down = weights[4 * index : 4 * index + 4]
        heads, units = outs[2 * index : 2 * index + 2]
        half = inw.shape[2] // 2
        columns = pl.ds(pl.multiple_of(core * half, half), half)
        moves.append((inw.at[:, :, columns], heads.at[0, pl.ds(0, 3)]))
        moves.append((outw.at[:, columns], heads.at[0, 3]))
        rows = up.shape[0] // 2
        own = pl.ds(pl.multiple_of(core * rows, rows), rows)
        moves.append((up.at[own, :], units.at[0, 0]))
        moves.append((down.at[own, :], units.at[0, 1]))
    copies = [pltpu.make_async_copy(*move, sems.at[index]) for index, move in enumerate(moves)]
    for copy in copies:
        copy.start()
    for copy in copies:
        copy.wait()


def pieces(place, *weights):
    inw, _, up, _ = weights[:4]
    heads = struct((1, MATS, inw.shape[1], inw.shape[2] // 2), BF16)
    units = struct((1, 2, up.shape[0] // 2, up.shape[1]), BF16)
    spaces = SMALL + [(1 + index, pltpu.HBM) for index in range(8)]
    scratch = [pltpu.SemaphoreType.DMA((8,))]
    return call(
        pieces_kernel, [heads, units, heads, units], [place, *weights], spaces, scratch, limit=58 * 1024 * 1024
    )


def table_kernel(*refs):
    inputs, (table_ref, bias_ref) = refs[:20], refs[20:]
    for base in (0, 1):
        kernel, cbias, gain, shift, inb, outb, gain_two, shift_two, upb, downb = inputs[base * 10 : base * 10 + 10]
        table_ref[pl.ds(base * 16, 9), :] = kernel[...]
        for index, item in enumerate((cbias, gain, shift, outb, gain_two, shift_two, downb)):
            table_ref[pl.ds(base * 16 + 9 + index, 1), :] = item[...].reshape(1, -1)
        first = 0 if base == 0 else 6
        count = inb.shape[0]
        bias_ref[pl.ds(first, count), :] = inb[...]
        wide = upb[...].reshape(1, -1)
        step = wide.shape[1] // 4
        for index in range(4):
            bias_ref[pl.ds(first + count + index, 1), :] = wide[:, index * step : (index + 1) * step]
    bias_ref[pl.ds(13, 3), :] = jnp.zeros((3, bias_ref.shape[1]), F32)


def tables(*small):
    width = small[0].shape[1]
    return call(table_kernel, [struct((32, width), F32), struct((16, small[4].shape[1]), F32)], list(small))


def order_kernel(place_ref, g0, g1, g2, head_ref, hidden_ref):
    core, wid = place_ref[0], place_ref[1]
    hids = [g0, g1, g2.at[0], g2.at[1]]
    step = g0.shape[1]
    half = step // 2
    head_ref[...] = jnp.zeros_like(head_ref)
    hidden_ref[...] = jnp.zeros_like(hidden_ref)
    for row, source in ((0, 0), (2, 1), (3, 6), (4, 7), (5, 8)):
        for i in range(4):
            head_ref[row : row + 1, i * step : (i + 1) * step] = hids[i][source : source + 1, :]
    for index, first in ((0, 2), (1, 9)):
        for side in range(2):
            for i in range(4):
                hid = hids[i if side == 0 else SWAP[i]]
                for j in range(4):
                    line = hid[pl.ds(first + jnp.bitwise_xor(wid, SWAP[j]), 1), :]
                    value = jnp.where(core == side, line[:, :half], line[:, half:])
                    lane = side * 16 * half + (i * 4 + j) * half
                    hidden_ref[index : index + 1, lane : lane + half] = value


def order_biases(place, g0, g1, g2):
    step = g0.shape[1]
    outs = [struct((8, 4 * step), F32), struct((8, 16 * step), F32)]
    return call(order_kernel, outs, [place, g0, g1, g2], SMALL)


BIASES = 16


def small_kernel(counts, place_ref, *refs):
    out_ref = refs[-1]
    core, wid, hid = place_ref[0], place_ref[1], place_ref[2]
    out_ref[...] = jnp.zeros_like(out_ref)
    row = 0
    for count, ref in zip(counts, refs):
        out_ref[pl.ds(row, count), :] = ref[...]
        row += count
    base = out_ref.shape[0] - 2 * BIASES
    window_heads, channel_heads, *hiddens = refs[len(counts) : -1]
    step = window_heads.shape[1] // 4
    half = step // 2
    gap = jnp.zeros((1, 256 - step), F32)
    for i in range(4):
        owned = jnp.bitwise_xor(hid, jnp.where(core == 0, i, SWAP[i]))
        for j in range(4):
            parts = []
            for ref in hiddens:
                lane = (i * 4 + j) * half
                mine = ref[0:1, lane : lane + half]
                lane = 16 * half + (SWAP[i] * 4 + j) * half
                other = ref[0:1, lane : lane + half]
                parts += [jnp.where(core == 0, mine, other), jnp.where(core == 0, other, mine), gap]
            line = pl.ds(base + owned * 4 + jnp.bitwise_xor(wid, SWAP[j]), 1)
            out_ref[line, 0:512] = jnp.concatenate(parts, axis=1)
        for first, heads, kinds in ((base, channel_heads, (0, 1, 2)), (base + BIASES, window_heads, (0, 2))):
            for position, kind in enumerate(kinds):
                value = heads[kind : kind + 1, i * step : (i + 1) * step]
                line = pl.ds(first + owned * 4 + position, 1)
                out_ref[line, 512:768] = jnp.concatenate([value, gap], axis=1)


def small_table(place, rows, window_heads, channel_heads, hiddens):
    counts = [item.shape[0] for item in rows]
    total = (sum(counts) + 7) // 8 * 8 + 2 * BIASES
    return call(
        partial(small_kernel, counts), [struct((total, rows[0].shape[1]), F32)],
        [place, *rows, window_heads, channel_heads, *hiddens], SMALL,
    )[0]


def outputs_kernel(place_ref, table_ref, *outs):
    hid = place_ref[2]
    base = table_ref.shape[0] - 2 * BIASES
    plan = ((outs[:10], 0, 10, 13, base + BIASES, 0), (outs[10:], 16, 26, 29, base, 256))
    for refs, sums, one, two, heads, lane in plan:
        kernel, cbias, gain, shift, inb, outb, gain_two, shift_two, upb, downb = refs
        kernel[...] = table_ref[pl.ds(sums, 9), :]
        rows = (sums + 9, one, one + 1, one + 2, two, two + 1, two + 2)
        for ref, row in zip((cbias, gain, shift, outb, gain_two, shift_two, downb), rows):
            ref[...] = table_ref[pl.ds(row, 1), :].reshape(-1)
        step = inb.shape[1]
        for index in range(inb.shape[0]):
            inb[pl.ds(index, 1), :] = table_ref[pl.ds(heads + hid * 4 + index, 1), :][:, 512 : 512 + step]
        for index in range(4):
            line = table_ref[pl.ds(base + hid * 4 + index, 1), :]
            upb[pl.ds(index * step, step)] = line[:, lane : lane + step].reshape(-1)


def small_outputs(place, table):
    width = table.shape[1]
    step = width // 4
    outs = []
    for count in (2, 3):
        flat = struct((width,), F32)
        outs += [struct((9, width), F32), flat, flat, flat, struct((count, step), F32), flat, flat, flat, flat, flat]
    return call(outputs_kernel, outs, [place, table], SMALL)


def join_kernel(first_ref, second_ref, out_ref):
    count = first_ref.shape[0]
    out_ref[:count] = first_ref[...]
    out_ref[count:] = second_ref[...]


def join(first, second, wait=5):
    shape = (2 * first.shape[0], *first.shape[1:])
    return call(join_kernel, [struct(shape, first.dtype)], [first, second], flops=max(wait * WAIT, 1))[0]


def fold_kernel(kept_ref, arrived_ref, still_ref, sent_ref):
    half = still_ref.shape[0]
    still_ref[...] = kept_ref[:half].astype(F32) + arrived_ref[:half].astype(F32)
    sent_ref[...] = (kept_ref[half:].astype(F32) + arrived_ref[half:].astype(F32)).astype(BF16)


def fold(kept, arrived):
    shape = (kept.shape[0] // 2, *kept.shape[1:])
    return call(fold_kernel, [struct(shape, F32), struct(shape, BF16)], [kept, arrived], flops=FOLD * WAIT)


def total_kernel(kept_ref, arrived_ref, out_ref):
    out_ref[...] = kept_ref[0] + arrived_ref[0].astype(F32)


def fold_last(kept, arrived):
    return call(total_kernel, [struct(kept.shape[1:], F32)], [kept, arrived], flops=FOLD * WAIT)[0]


def rows_kernel(place_ref, own_ref, other_ref, *outs):
    rows = own_ref.shape[1]
    core = place_ref[0]
    for index, out_ref in enumerate(outs):
        out_ref[pl.ds(pl.multiple_of(core * rows, 8), rows), :] = own_ref[index]
        out_ref[pl.ds(pl.multiple_of((1 - core) * rows, 8), rows), :] = other_ref[index]


def both_rows(place, own, other):
    out = struct((2 * own.shape[1], own.shape[2]), F32)
    return call(rows_kernel, [out, out], [place, own, other], SMALL)


def columns_kernel(place_ref, own_ref, other_ref, in_ref, out_ref):
    half = own_ref.shape[2]
    core = place_ref[0]
    for turn, ref in ((core, own_ref), (1 - core, other_ref)):
        cut = pl.ds(pl.multiple_of(turn * half, 128), half)
        for m in range(3):
            in_ref[m, :, cut] = ref[m]
        out_ref[:, cut] = ref[3]


def both_columns(place, own, other):
    rows, width = own.shape[1], own.shape[2] * 2
    return call(
        columns_kernel, [struct((3, rows, width), F32), struct((rows, width), F32)], [place, own, other], SMALL
    )


def add_kernel(first_ref, second_ref, out_ref):
    out_ref[...] = first_ref[...] + second_ref[...]


def add(first, second):
    return call(add_kernel, [struct(first.shape, F32)], [first, second])[0]


class Line:
    def __init__(self, mark):
        self.mark = mark

    def gate(self, tree):
        tree, self.mark = lax.optimization_barrier((tree, self.mark))
        return tree

    def run(self, function, *operands):
        return self.gate(function(*self.gate(operands)))


class Scatter:
    def __init__(self, line, place, near, far, heads):
        self.line, self.place, self.kept, self.sent = line, place, near, far
        self.heads, self.step = heads, 0

    def advance(self):
        gate = self.line.gate
        if self.step in (1, 2, 3):
            self.kept, self.sent = self.line.run(fold, self.kept, self.flight)
        elif self.step == 4:
            self.kept = self.line.run(fold_last, self.kept, self.flight)
            bit = 2
            while bit < lax.axis_size("dp"):
                self.kept = self.line.run(add, self.kept, exchange(self.kept, "dp", bit))
                bit *= 2
        elif self.step == 5:
            join_cores = both_columns if self.heads else both_rows
            self.total = self.line.run(join_cores, self.place, self.kept, self.flight)
        if self.step < 4:
            self.sent = gate(self.sent)
        if self.step == 0:
            self.flight = cross(self.sent, False)
        elif self.step == 1:
            self.flight = cross(self.sent, True)
        elif self.step == 2:
            self.flight = exchange(self.sent, "wid", 1)
        elif self.step == 3:
            self.flight = exchange(self.sent, "wid", 2)
        elif self.step == 4:
            self.flight = sibling(gate(self.kept))
        self.step += 1


class Small:
    def __init__(self, line, table):
        self.line, self.table, self.flight = line, table, None
        self.steps = []
        for axis in ("dp", "hid", "wid"):
            bit = 1
            while bit < lax.axis_size(axis):
                self.steps.append((axis, bit))
                bit *= 2

    def advance(self):
        if self.flight is not None:
            self.table = self.line.run(add, self.table, self.flight)
            self.flight = None
        if self.steps:
            axis, bit = self.steps.pop(0)
            self.table = self.line.gate(self.table)
            self.flight = exchange(self.table, axis, bit)
            return True
        return False


def body(
    inputs, grid_sizes, cotangent,
    wkernel, wcbias, wgain, wshift, winw, winb, woutw, woutb,
    wgain_two, wshift_two, wupw, wupb, wdownw, wdownb,
    ckernel, ccbias, cgain, cshift, cinw, cinb, coutw, coutb,
    cgain_two, cshift_two, cupw, cupb, cdownw, cdownb,
):
    image_count = inputs.shape[0] // (PADDED * PADDED)
    hid, wid = lax.axis_index("hid"), lax.axis_index("wid")
    own_sizes = lax.dynamic_slice_in_dim(
        grid_sizes, (hid * lax.axis_size("wid") + wid) * image_count, image_count, 0
    )
    at = jnp.stack([lax.rem(lax.axis_index("dp"), 2), wid, hid]).astype(jnp.int32)
    place = jnp.concatenate([at, own_sizes])
    line = Line(winb[0, 0])

    def send(move, values):
        return move(line.gate(values))

    def w1(values):
        return exchange(values, "wid", 2)

    def w2(values):
        return exchange(values, "wid", 1)

    def h1(values):
        return cross(values, True)

    def h2(values):
        return cross(values, False)

    gate = line.gate

    def both(near, arrived, wait=5):
        return line.run(partial(join, wait=wait), near, arrived)

    own0, own1, own2, own3 = pieces(place, winw, woutw, wupw, wdownw, cinw, coutw, cupw, cdownw)

    w1_0 = send(w1, own0)
    table, bias = line.run(
        tables, wkernel, wcbias, wgain, wshift, winb, woutb, wgain_two, wshift_two, wupb, wdownb,
        ckernel, ccbias, cgain, cshift, cinb, coutb, cgain_two, cshift_two, cupb, cdownb,
    )
    near0 = both(own0, w1_0)
    w2_0 = send(w2, near0)
    w1_1 = send(w1, own1)
    bias_one = send(h1, bias)
    start, after_conv = line.run(partial(first_conv, 0), place, inputs, table)
    cotangent = line.run(cells, cotangent)
    bias_one = gate(bias_one)
    bias_two = send(h2, jnp.stack([bias, bias_one]))
    near1 = both(own1, w1_1)
    bias_two = gate(bias_two)
    head_bias, hidden_bias = line.run(order_biases, place, bias, bias_one, bias_two)
    near0 = both(near0, w2_0)
    h1_0 = send(h1, near0)
    w2_1 = send(w2, near1)
    near0 = both(near0, h1_0, 0)
    h2_0 = send(h2, near0)
    near1 = both(near1, w2_1, 9)
    h1_1 = send(h1, near1)
    w1_2 = send(w1, own2)
    far0 = gate(h2_0)
    s_0 = send(sibling, near0), send(sibling, far0)
    near2 = both(own2, w1_2)
    w2_2 = send(w2, near2)
    s_0 = gate(s_0)
    att_one = [near0, far0, *s_0]
    near1 = both(near1, h1_1)
    h2_1 = send(h2, near1)
    near2 = both(near2, w2_2)
    h1_2 = send(h1, near2)
    w1_3 = send(w1, own3)
    after_attn, normed_one, qkv_one, mixed_one = line.run(
        partial(attention, True), place, after_conv, table, head_bias, att_one
    )
    near3 = both(own3, w1_3)
    w2_3 = send(w2, near3)
    near2 = both(near2, h1_2)
    h2_2 = send(h2, near2)
    near3 = both(near3, w2_3)
    h1_3 = send(h1, near3)
    far1 = gate(h2_1)
    s_1 = send(sibling, near1), send(sibling, far1)
    far2 = gate(h2_2)
    s_2 = send(sibling, near2), send(sibling, far2)
    s_1 = gate(s_1)
    s_2 = gate(s_2)
    near3 = both(near3, h1_3)
    h2_3 = send(h2, near3)
    s_3 = send(sibling, near3)
    mlp_two = [near1, far1, *s_1]
    after_mlp, acted_two, fpack_two, deriv_two = line.run(
        partial(mlp, 0), place, after_attn, table, hidden_bias, mlp_two
    )
    after_conv_c = line.run(partial(conv, 16), place, after_mlp, table)
    att_three = [near2, far2, *s_2]
    after_attn_c, normed_three, qkv_three, mixed_three = line.run(
        partial(attention, False), place, after_conv_c, table, head_bias, att_three
    )
    s_3 = gate(s_3)
    far3 = gate(h2_3)
    s_far3 = gate(send(sibling, far3))
    mlp_four = [near3, far3, s_3, s_far3]
    outputs, acted_four, fpack_four, deriv_four = line.run(
        partial(mlp, 16), place, after_attn_c, table, hidden_bias, mlp_four
    )

    def scatter(near, far, heads):
        group = Scatter(line, place, near, far, heads)
        group.advance()
        return group

    fpack_four_other = send(sibling, fpack_four)
    flowing, gh_four, ghs_four, low_four, little_four, upb_four = line.run(
        partial(mlp_back, 16), place, cotangent, after_attn_c, table, deriv_four, mlp_four
    )
    fpack_four_other = gate(fpack_four_other)
    ghs_four_other, low_four_other = gate((send(sibling, ghs_four), send(sibling, low_four)))
    m_four = scatter(
        *line.run(pair_grads, acted_four, fpack_four, fpack_four_other, gh_four, low_four, ghs_four_other, low_four_other), False
    )
    flowing, left_three, rest_three, mine_three, little_three, inb_three = line.run(
        partial(attention_back, False),
        place, flowing, after_conv_c, table, normed_three, qkv_three, mixed_three, att_three,
    )
    sent_three = gate((send(sibling, left_three), send(sibling, rest_three)))
    near_far = line.run(head_grads, place, left_three, rest_three, *sent_three, mine_three)
    a_three = scatter(*near_far, True)
    m_four.advance()
    fpack_two_other = send(sibling, fpack_two)
    flowing, sums_three = line.run(partial(conv_back, 16, False), place, flowing, after_mlp, table)
    flowing, gh_two, ghs_two, low_two, little_two, upb_two = line.run(
        partial(mlp_back, 0), place, flowing, after_attn, table, deriv_two, mlp_two
    )
    ghs_two_other, low_two_other = gate((send(sibling, ghs_two), send(sibling, low_two)))
    fpack_two_other = gate(fpack_two_other)
    near_far = line.run(pair_grads, acted_two, fpack_two, fpack_two_other, gh_two, low_two, ghs_two_other, low_two_other)
    m_two = scatter(*near_far, False)
    m_four.advance()
    a_three.advance()
    flowing, left_one, rest_one, mine_one, little_one, inb_one = line.run(
        partial(attention_back, True),
        place, flowing, after_conv, table, normed_one, qkv_one, mixed_one, att_one,
    )
    a_three.advance()
    m_four.advance()
    sent_one = gate((send(sibling, left_one), send(sibling, rest_one)))
    near_far = line.run(head_grads, place, left_one, rest_one, *sent_one, mine_one)
    a_one = scatter(*near_far, True)
    m_two.advance()
    input_grad, sums_one = line.run(partial(conv_back, 0, True), place, flowing, start, table)
    small = line.run(
        small_table, place, [sums_one, little_one, little_two, sums_three, little_three, little_four],
        inb_one, inb_three, [upb_two, upb_four],
    )
    small = Small(line, small)
    small.advance()
    a_three.advance()
    m_four.advance()
    small.advance()
    a_three.advance()
    small.advance()
    a_one.advance()
    m_two.advance()
    small.advance()
    m_four.advance()
    a_one.advance()
    small.advance()
    m_two.advance()
    a_three.advance()
    a_one.advance()
    small.advance()
    m_two.advance()
    a_one.advance()
    m_two.advance()
    a_one.advance()
    small = line.run(small_outputs, place, small.table)

    def ordered(small, attention, units):
        return (
            *small[:4], attention[0], small[4], attention[1], *small[5:8], units[0], small[8], units[1], small[9]
        )

    return (
        outputs, input_grad,
        *ordered(small[:10], a_one.total, m_two.total),
        *ordered(small[10:], a_three.total, m_four.total),
    )


def solution(mesh):
    tokens, everywhere = P(("dp", "hid", "wid"), None), P()
    stacked, rows = P(None, ("hid", "wid"), None), P(("hid", "wid"), None)
    block = (
        everywhere, everywhere, everywhere, everywhere, stacked, P(None, "hid"), rows, everywhere,
        everywhere, everywhere, rows, P("hid"), rows, everywhere,
    )
    return jax.shard_map(
        body,
        mesh=mesh,
        in_specs=(tokens, P("dp"), tokens) + block + block,
        out_specs=(tokens, tokens) + block + block,
        check_vma=False,
    )
```
